32 devices in a mesh: dp: 2 (over core), graph: 4 (over z), mp: 4 (over y, x).
Axes of the slice: x: 2, y: 2, z: 4, core: 2. Of those that a mesh axis runs over, the one named last changes fastest.
Arguments:
- nodes: bfloat16 [2, 512, 512], P('dp', 'graph'), may hold values from -6 to 6
- edges: bfloat16 [2, 512, 60, 192], P('dp', 'graph', 'mp'), may hold values from -6 to 6
- neighbours: int32 [2, 512, 60], P('dp', 'graph'), may hold values from 0 to 511, as said below
- resmask: int32 [2, 512], P('dp'), may hold values 0 or 1
- node_gain_a: float32 [512], replicated, may hold values from 0.25 to 1.75
- edge_gain_a: float32 [192], replicated, may hold values from 0.25 to 1.75
- message_self: bfloat16 [512, 512], P(None, 'mp'), may hold values from -0.15625 to 0.15625
- message_other: bfloat16 [512, 512], P(None, 'mp'), may hold values from -0.15625 to 0.15625
- message_edge: bfloat16 [192, 512], P(None, 'mp'), may hold values from -0.15625 to 0.15625
- message_out: bfloat16 [512, 512], P('mp'), may hold values from -0.5 to 0.5
- node_gain_b: float32 [512], replicated, may hold values from 0.25 to 1.75
- ffn_in: bfloat16 [512, 2048], P(None, 'mp'), may hold values from -0.25 to 0.25
- ffn_out: bfloat16 [2048, 512], P('mp'), may hold values from -0.25 to 0.25
- node_gain_c: float32 [512], replicated, may hold values from 0.25 to 1.75
- edge_gain_b: float32 [192], replicated, may hold values from 0.25 to 1.75
- update_self: bfloat16 [512, 512], P(None, 'mp'), may hold values from -0.15625 to 0.15625
- update_other: bfloat16 [512, 512], P(None, 'mp'), may hold values from -0.15625 to 0.15625
- update_edge: bfloat16 [192, 512], P(None, 'mp'), may hold values from -0.15625 to 0.15625
- update_out: bfloat16 [512, 192], P('mp'), may hold values from -0.375 to 0.375
- node_cot: bfloat16 [2, 512, 512], P('dp', 'graph'), may hold values from -6 to 6
- edge_cot: bfloat16 [2, 512, 60, 192], P('dp', 'graph', 'mp'), may hold values from -6 to 6
Outputs:
- nodes_out: bfloat16 [2, 512, 512], P('dp', 'graph')
- edges_out: bfloat16 [2, 512, 60, 192], P('dp', 'graph', 'mp')
- grad_nodes: float32 [2, 512, 512], P('dp', 'graph')
- grad_edges: float32 [2, 512, 60, 192], P('dp', 'graph', 'mp')
- grad_node_gain_a: float32 [512], replicated
- grad_edge_gain_a: float32 [192], replicated
- grad_message_self: float32 [512, 512], P(None, 'mp')
- grad_message_other: float32 [512, 512], P(None, 'mp')
- grad_message_edge: float32 [192, 512], P(None, 'mp')
- grad_message_out: float32 [512, 512], P('mp')
- grad_node_gain_b: float32 [512], replicated
- grad_ffn_in: float32 [512, 2048], P(None, 'mp')
- grad_ffn_out: float32 [2048, 512], P('mp')
- grad_node_gain_c: float32 [512], replicated
- grad_edge_gain_b: float32 [192], replicated
- grad_update_self: float32 [512, 512], P(None, 'mp')
- grad_update_other: float32 [512, 512], P(None, 'mp')
- grad_update_edge: float32 [192, 512], P(None, 'mp')
- grad_update_out: float32 [512, 192], P('mp')
The draws below stay inside these ranges and needn't reach their ends.
Inputs may be any that keep to these rules, and one draw needn't show every extreme that they name: `neighbours`: each row holds 60 different residue numbers of the same complex, none equal to the row's own residue.
All inputs are finite; a program needn't handle non-finite values. No bound on the sum of `resmask` on one device may be relied on, other than what follows from the above.
Results may differ from the reference program's by a relative error of at most 0.02.
Values may be sent and summed in bfloat16 or wider, within the bound.
No kernel may reach another device: no remote copies, remote signals or barrier semaphores. Data moves between devices by JAX's collectives and lax.ppermute only.
A program may use at most 128 MiB of HBM per device.

```python
import jax
import jax.numpy as jnp
from jax import lax

D = 512
DE = 192
MH = 512
FF = 2048
EH = 512
K = 60
COMPLEXES = 2
NRES = 512


def draw_neighbours(key, part):
    key = jax.random.fold_in(key, 7)
    near_key = jax.random.fold_in(key, 1)
    far_key = jax.random.fold_in(key, 2)
    order_key = jax.random.fold_in(key, 3)
    far_count = K // 4
    near_count = K - far_count
    shape = (COMPLEXES, NRES, NRES)
    near_noise = jax.random.randint(near_key, shape, 0, 4096, dtype=jnp.int32)
    far_noise = jax.random.randint(far_key, shape, 0, 4096, dtype=jnp.int32)
    row_ids = jnp.arange(NRES, dtype=jnp.int32)[:, None]
    col_ids = jnp.arange(NRES, dtype=jnp.int32)[None, :]
    distance = jnp.abs(row_ids - col_ids)
    lowest = jnp.int32(-2 ** 30)
    near_ok = (distance >= 1) & (distance <= near_count)
    near_score = jnp.where(near_ok, (near_noise - 16 * distance) * NRES + col_ids, lowest)
    far_score = jnp.where(distance > near_count, far_noise * NRES + col_ids, lowest)
    near_pick = lax.top_k(near_score, near_count)[1].astype(jnp.int32)
    far_pick = lax.top_k(far_score, far_count)[1].astype(jnp.int32)
    picked = jnp.concatenate([near_pick, far_pick], axis=-1)
    order_noise = jax.random.randint(order_key, (COMPLEXES, NRES, K), 0, 4096, dtype=jnp.int32)
    order_score = order_noise * K + jnp.arange(K, dtype=jnp.int32)[None, None, :]
    order = jnp.argsort(order_score, axis=-1, stable=True).astype(jnp.int32)
    return jnp.take_along_axis(picked, order, axis=-1).astype(jnp.int32)


def place_ends(values, rng, smallest, largest):
    dims = values.shape
    spot = [jax.random.randint(jax.random.fold_in(rng, axis), (), 0, dims[axis]) for axis in range(len(dims))]
    values = values.at[tuple(spot)].set(smallest)
    longest = dims.index(max(dims))
    spot[longest] = (spot[longest] + 1) % dims[longest]
    return values.at[tuple(spot)].set(largest)


def block_levels(own_key, extent, pieces, smallest, high):
    def one(axis_at, blocks):
        draws = jax.random.uniform(jax.random.fold_in(jax.random.fold_in(own_key, 6), axis_at), (blocks,), jnp.float32, smallest / len(pieces), high / len(pieces))
        return jnp.repeat(jnp.exp(draws), extent[axis_at] // blocks).reshape((-1,) + (1,) * (len(extent) - axis_at - 1))

    loudness = one(*pieces[0])
    for cut in pieces[1:]:
        loudness = loudness * one(*cut)
    return loudness


def normal_values(stream_key, dims, spread, limit, pieces=(), held_as=jnp.bfloat16):
    factor_of = block_levels(stream_key, dims, pieces, -0.22, 0.18) if pieces else 1.0
    drawn = jax.random.normal(stream_key, dims, jnp.float32) * spread * factor_of
    return jnp.minimum(jnp.maximum(drawn, -limit), limit).astype(held_as)


def setup_inputs(seed: int = 0) -> dict:
    splits = jax.random.split(jax.random.key(seed), 22)
    return {
        "nodes": normal_values(splits[0], (COMPLEXES, NRES, D), 1.0, 6.0, ((0, 2), (1, 4))),
        "edges": normal_values(splits[1], (COMPLEXES, NRES, K, DE), 1.0, 6.0, ((0, 2), (1, 4), (2, 4))),
        "neighbours": draw_neighbours(jax.random.fold_in(splits[21], 71), 0),
        "resmask": place_ends((jax.random.randint(splits[3], (COMPLEXES, NRES), 0, 8) < 7).astype(jnp.int32), jax.random.fold_in(splits[3], 1), 0, 1),
        "node_gain_a": jnp.clip(1.0 + 0.15 * jax.random.normal(splits[4], (D,), jnp.float32), 0.25, 1.75),
        "edge_gain_a": jnp.clip(1.0 + 0.15 * jax.random.normal(splits[5], (DE,), jnp.float32), 0.25, 1.75),
        "message_self": normal_values(splits[6], (D, MH), (2 * D + DE) ** -0.5, 0.15625, ((1, 4),)),
        "message_other": normal_values(splits[7], (D, MH), (2 * D + DE) ** -0.5, 0.15625, ((1, 4),)),
        "message_edge": normal_values(splits[8], (DE, MH), (2 * D + DE) ** -0.5, 0.15625, ((1, 4),)),
        "message_out": normal_values(splits[9], (MH, D), (MH // 4) ** -0.5, 0.5, ((0, 4),)),
        "node_gain_b": jnp.clip(1.0 + 0.15 * jax.random.normal(splits[10], (D,), jnp.float32), 0.25, 1.75),
        "ffn_in": normal_values(splits[11], (D, FF), D ** -0.5, 0.25, ((1, 4),)),
        "ffn_out": normal_values(splits[12], (FF, D), (FF // 4) ** -0.5, 0.25, ((0, 4),)),
        "node_gain_c": jnp.clip(1.0 + 0.15 * jax.random.normal(splits[13], (D,), jnp.float32), 0.25, 1.75),
        "edge_gain_b": jnp.clip(1.0 + 0.15 * jax.random.normal(splits[14], (DE,), jnp.float32), 0.25, 1.75),
        "update_self": normal_values(splits[15], (D, EH), (2 * D + DE) ** -0.5, 0.15625, ((1, 4),)),
        "update_other": normal_values(splits[16], (D, EH), (2 * D + DE) ** -0.5, 0.15625, ((1, 4),)),
        "update_edge": normal_values(splits[17], (DE, EH), (2 * D + DE) ** -0.5, 0.15625, ((1, 4),)),
        "update_out": normal_values(splits[18], (EH, DE), (EH // 2) ** -0.5, 0.375, ((0, 4),)),
        "node_cot": normal_values(splits[19], (COMPLEXES, NRES, D), 1.0, 6.0, ((0, 2), (1, 4))),
        "edge_cot": normal_values(splits[20], (COMPLEXES, NRES, K, DE), 1.0, 6.0, ((0, 2), (1, 4), (2, 4))),
    }


@jax.custom_vjp
def low(v):
    return lax.optimization_barrier(v.astype(jnp.bfloat16)).astype(jnp.float32)

@jax.custom_vjp
def low_back(v):
    return v

def low_keep(v):
    return (low(v), None)

def low_pass(kept, grad):
    return (grad,)

def back_keep(v):
    return (v, None)

def back_low(kept, grad):
    return (low(grad),)
low.defvjp(low_keep, low_pass)
low_back.defvjp(back_keep, back_low)
EPSILON = 1e-05
HIGH = lax.Precision.HIGHEST

def normalize(values):
    centre = values - lax.optimization_barrier(jnp.mean(values, axis=-1, keepdims=True))
    variance = lax.optimization_barrier(jnp.mean(centre * centre, axis=-1, keepdims=True))
    return centre * lax.rsqrt(variance + EPSILON)

def product(form, left, right):
    return jnp.einsum(form, left, right, precision=HIGH)

def layer_pair(node_in, edge_in, nbr_rows, weight_mask, params):
    gain_na, gain_ea, msg_self, msg_other, msg_edge, msg_out, gain_nb, lin_in, lin_out, gain_nc, gain_eb, upd_self, upd_other, upd_edge, upd_out = params
    edge_hat = normalize(edge_in)
    node_low = low(normalize(node_in) * gain_na)
    edge_low = low(edge_hat * gain_ea)
    edge_lowb = low(edge_hat * gain_eb)
    pre_msg = low_back(product('rd,dh->rh', node_low, msg_self)[:, None, :] + product('rkd,dh->rkh', node_low[nbr_rows], msg_other) + product('rke,eh->rkh', edge_low, msg_edge))
    act_msg = low(jax.nn.gelu(pre_msg))
    pooled = low(lax.optimization_barrier(jnp.sum(act_msg * weight_mask[:, :, None], axis=1)))
    node_one = node_in + low_back(product('rh,hd->rd', pooled, msg_out))
    ffn_low = low(normalize(node_one) * gain_nb)
    pre_ffn = low_back(product('rd,df->rf', ffn_low, lin_in))
    act_ffn = low(jax.nn.gelu(pre_ffn))
    node_two = node_one + low_back(product('rf,fd->rd', act_ffn, lin_out))
    third_low = low(normalize(node_two) * gain_nc)
    pre_upd = low_back(product('rd,dh->rh', third_low, upd_self)[:, None, :] + product('rkd,dh->rkh', third_low[nbr_rows], upd_other) + product('rke,eh->rkh', edge_lowb, upd_edge))
    act_upd = low(jax.nn.gelu(pre_upd))
    edge_out = edge_in + low_back(product('rkh,he->rke', act_upd, upd_out))
    return (node_two, edge_out)

def reference(nodes, edges, neighbours, resmask, node_gain_a, edge_gain_a, message_self, message_other, message_edge, message_out, node_gain_b, ffn_in, ffn_out, node_gain_c, edge_gain_b, update_self, update_other, update_edge, update_out, node_cot, edge_cot):
    params = tuple((w.astype(jnp.float32) for w in (node_gain_a, edge_gain_a, message_self, message_other, message_edge, message_out, node_gain_b, ffn_in, ffn_out, node_gain_c, edge_gain_b, update_self, update_other, update_edge, update_out)))

    def one_complex(totals, item):
        node_in, edge_in, nbr_rows, mask_row, cot_node, cot_edge = item
        weight_mask = mask_row.astype(jnp.float32)[nbr_rows] / K

        def forward(node_x, edge_x, param_x):
            return layer_pair(node_x, edge_x, nbr_rows, weight_mask, param_x)
        outputs, pull = jax.vjp(forward, node_in.astype(jnp.float32), edge_in.astype(jnp.float32), params)
        grad_node, grad_edge, grad_params = pull((cot_node.astype(jnp.float32), cot_edge.astype(jnp.float32)))
        totals = jax.tree.map(lambda left, right: left + right, totals, grad_params)
        return (totals, (outputs[0].astype(jnp.bfloat16), outputs[1].astype(jnp.bfloat16), grad_node, grad_edge))
    zeros = jax.tree.map(jnp.zeros_like, params)
    totals, stacked = lax.scan(one_complex, zeros, (nodes, edges, neighbours, resmask, node_cot, edge_cot))
    return (stacked[0], stacked[1], stacked[2], stacked[3], totals[0], totals[1], totals[2], totals[3], totals[4], totals[5], totals[6], totals[7], totals[8], totals[9], totals[10], totals[11], totals[12], totals[13], totals[14])
```

```python
import functools

import jax
import jax.numpy as jnp
from jax import lax
from jax.experimental import pallas as pl
from jax.experimental.pallas import tpu as pltpu
from jax.sharding import PartitionSpec as P

EPSILON = 1e-05
F32 = jnp.float32
BF16 = jnp.bfloat16
GELU_A = 0.7978845608028654
GELU_B = 0.044715


def dot(left, right):
    return lax.dot_general(left, right, (((1,), (0,)), ((), ())), preferred_element_type=F32)


def dot_nt(left, right):
    return lax.dot_general(left, right, (((1,), (1,)), ((), ())), preferred_element_type=F32)


def dot_tn(left, right):
    return lax.dot_general(left, right, (((0,), (0,)), ((), ())), preferred_element_type=F32)


def normalize(values):
    centre = values - jnp.mean(values, axis=-1, keepdims=True)
    variance = jnp.mean(centre * centre, axis=-1, keepdims=True)
    scale_inv = lax.rsqrt(variance + EPSILON)
    return centre * scale_inv, scale_inv


def norm_back(grad_hat, normed, scale_inv):
    return scale_inv * (
        grad_hat
        - jnp.mean(grad_hat, axis=-1, keepdims=True)
        - normed * jnp.mean(grad_hat * normed, axis=-1, keepdims=True)
    )


def gelu_both(u):
    square = u * u
    th = jnp.tanh(u * (GELU_A + (GELU_A * GELU_B) * square))
    half = 0.5 + 0.5 * th
    slope = half + (0.5 * u) * (1.0 - th * th) * (GELU_A + (3.0 * GELU_A * GELU_B) * square)
    return u * half, slope


def cat(refs, lo, hi):
    return jnp.concatenate([r[lo:hi, :] for r in refs], axis=1)


def edge_prep(et_ref, idx_ref, mask_ref, ga_ref, gb_ref, f_ref, q_ref, oh_ref, oht_ref, mk_ref):
    slots, rows, width = et_ref.shape
    total = mask_ref.shape[0]
    for s in range(slots):
        hat, _ = normalize(et_ref[s].astype(F32))
        f_ref[s] = (hat * ga_ref[...]).astype(BF16)
        q_ref[s] = (hat * gb_ref[...]).astype(BF16)
        idx = idx_ref[s]
        here = lax.broadcasted_iota(jnp.int32, (total, rows), 0)
        oht_ref[:, s * rows : (s + 1) * rows] = (here == idx).astype(F32).astype(BF16)
        eye = lax.broadcasted_iota(jnp.int32, (rows, rows), 0) == lax.broadcasted_iota(
            jnp.int32, (rows, rows), 1
        )
        high = jnp.where(eye, (idx // 64).astype(F32), 0.0).astype(BF16)
        low = jnp.where(eye, (idx % 64).astype(F32), 0.0).astype(BF16)
        ones = jnp.ones((rows, 128), BF16)
        column = (dot(high, ones) * 64.0 + dot(low, ones)).astype(jnp.int32)
        lane = lax.broadcasted_iota(jnp.int32, (rows, 128), 1)
        parts = [
            ((lane + base) == column).astype(F32).astype(BF16) for base in range(0, total, 128)
        ]
        onehot = jnp.concatenate(parts, axis=1)
        oh_ref[s] = onehot
        mk_ref[s] = dot(onehot, mask_ref[...]).astype(BF16)


def message_forward(
    nbr_scale, total_steps, f_ref, oh_ref, mk_ref, nodes_ref, gain_ref, w0, w1, w2, w3, slope_ref, pooled_ref, a_ref, p_ref, ps_ref, acc_ref
):
    step = pl.program_id(0)
    slots, rows, _ = f_ref.shape
    width = nodes_ref.shape[1]
    ws = (w0, w1, w2, w3)

    @pl.when(step == 0)
    def _():
        hat, _ = normalize(nodes_ref[...].astype(F32))
        a = (hat * gain_ref[...]).astype(BF16)
        p_ref[...] = dot(a, cat(ws, width, 2 * width)).astype(BF16)
        own = a[:rows]
        a_ref[...] = own
        ps_ref[...] = dot(own, cat(ws, 0, width))
        acc_ref[...] = jnp.zeros_like(acc_ref)

    we = cat(ws, 2 * width, w0.shape[0])
    for s in range(slots):
        u = dot(oh_ref[s], p_ref[...]) + dot(f_ref[s], we) + ps_ref[...]
        z, slope = gelu_both(u)
        mask = jnp.concatenate([mk_ref[s].astype(F32)] * (u.shape[1] // 128), axis=1)
        acc_ref[...] += z.astype(BF16).astype(F32) * mask
        slope_ref[s] = (slope * mask).astype(BF16)

    @pl.when(step == total_steps - 1)
    def _():
        pooled_ref[...] = (acc_ref[...] * nbr_scale).astype(BF16)


def node_forward(
    s0, s1, s2, s3, nodes_ref, o0, o1, o2, o3, gain_ref, win_ref, wout_ref, s_ref, h1_ref, b_ref, y_ref, slope_ref, part_ref
):
    sums = []
    for p in range(4):
        acc = None
        for k, ref in enumerate((s0, s1, s2, s3)):
            at = (p ^ k) * 128
            term = ref[:, at : at + 128].astype(F32)
            acc = term if acc is None else acc + term
        sums.append(acc.astype(BF16))
    pooled = jnp.concatenate(sums, axis=1)
    s_ref[...] = pooled
    wo = jnp.concatenate([o0[...], o1[...], o2[...], o3[...]], axis=0)
    h1 = nodes_ref[...].astype(F32) + dot(pooled, wo)
    h1_ref[...] = h1
    hat, _ = normalize(h1)
    b = (hat * gain_ref[...]).astype(BF16)
    b_ref[...] = b
    y, slope = gelu_both(dot(b, win_ref[...]))
    y = y.astype(BF16)
    y_ref[...] = y
    slope_ref[...] = slope.astype(BF16)
    part_ref[...] = dot(y, wout_ref[...]).astype(BF16)


def node_close(h1_ref, p0, p1, p2, p3, gain_ref, h2_ref, c_ref, out_ref):
    h2 = h1_ref[...] + (
        (p0[...].astype(F32) + p1[...].astype(F32)) + (p2[...].astype(F32) + p3[...].astype(F32))
    )
    h2_ref[...] = h2
    hat, _ = normalize(h2)
    c_ref[...] = (hat * gain_ref[...]).astype(BF16)
    out_ref[...] = h2.astype(BF16)


def update_kernel(
    total_steps, q_ref, oh_ref, oht_ref, cot_ref, c_ref, w0, w1, w2, w3, o0, o1, o2, o3, w_ref, dv_ref, r_ref, *rest
):
    s_refs, (p_ref, ps_ref, racc_ref, sacc_ref) = rest[:-4], rest[-4:]
    step = pl.program_id(0)
    slots, rows, _ = q_ref.shape
    width = c_ref.shape[1]
    ws = (w0, w1, w2, w3)

    @pl.when(step == 0)
    def _():
        p_ref[...] = dot(c_ref[...], cat(ws, width, 2 * width)).astype(BF16)
        ps_ref[...] = dot(c_ref[:rows, :], cat(ws, 0, width))
        racc_ref[...] = jnp.zeros_like(racc_ref)
        sacc_ref[...] = jnp.zeros_like(sacc_ref)

    we = cat(ws, 2 * width, w0.shape[0])
    wo = jnp.concatenate([o0[...], o1[...], o2[...], o3[...]], axis=0)
    for s in range(slots):
        v = dot(oh_ref[s], p_ref[...]) + dot(q_ref[s], we) + ps_ref[...]
        w, slope = gelu_both(v)
        w_ref[s] = w.astype(BF16)
        dv = (slope * dot_nt(cot_ref[s], wo)).astype(BF16)
        dv_ref[s] = dv
        racc_ref[...] += dv.astype(F32)
    dvs = dv_ref[...].reshape(slots * rows, dv_ref.shape[2])
    sacc_ref[...] += dot(oht_ref[...], dvs)

    @pl.when(step == total_steps - 1)
    def _():
        r_ref[...] = racc_ref[...].astype(BF16)
        for b, ref in enumerate(s_refs):
            n = ref.shape[0]
            ref[...] = sacc_ref[b * n : (b + 1) * n, :].astype(BF16)


def update_edges(
    et_ref, w_ref, dv_ref, q_ref, cot_ref, w0, w1, w2, w3, o0, o1, o2, o3, out_ref, dq_ref, gout_ref, gedge_ref, gacc_ref, eacc_ref
):
    step = pl.program_id(0)
    slots, rows, width_e = et_ref.shape
    we = cat((w0, w1, w2, w3), w0.shape[0] - width_e, w0.shape[0])
    wo = jnp.concatenate([o0[...], o1[...], o2[...], o3[...]], axis=0)

    @pl.when(step == 0)
    def _():
        gacc_ref[...] = jnp.zeros_like(gacc_ref)
        eacc_ref[...] = jnp.zeros_like(eacc_ref)

    for s in range(slots):
        w = w_ref[s]
        dv = dv_ref[s]
        out_ref[s] = (et_ref[s].astype(F32) + dot(w, wo)).astype(BF16)
        dq_ref[s] = dot_nt(dv, we).astype(BF16)
        gacc_ref[...] += dot_tn(cot_ref[s], w)
        eacc_ref[...] += dot_tn(q_ref[s], dv)
    gout_ref[...] = gacc_ref[...].astype(BF16)
    gedge_ref[...] = eacc_ref[...].astype(BF16)


def node_terms(r_ref, s0, s1, s2, s3, w0, w1, w2, w3, sum_ref, part_ref):
    width = w0.shape[0] if False else part_ref.shape[1]
    ws = (w0, w1, w2, w3)
    total = (
        (s0[...].astype(F32) + s1[...].astype(F32)) + (s2[...].astype(F32) + s3[...].astype(F32))
    ).astype(BF16)
    sum_ref[...] = total
    part_ref[...] = (
        dot_nt(r_ref[...], cat(ws, 0, width)) + dot_nt(total, cat(ws, width, 2 * width))
    ).astype(BF16)


def node_terms_one(r_ref, s_ref, w0, w1, w2, w3, part_ref):
    width = part_ref.shape[1]
    ws = (w0, w1, w2, w3)
    part_ref[...] = (
        dot_nt(r_ref[...], cat(ws, 0, width)) + dot_nt(s_ref[...], cat(ws, width, 2 * width))
    ).astype(BF16)


def sum4(refs):
    a, b, c, d = [r[...].astype(F32) for r in refs]
    return (a + b) + (c + d)


def node_backward(
    t0, t1, t2, t3, h2_ref, cot_ref, gain_ref, slope_ref, win_ref, wout_ref, dh2_ref, dr_ref, dp_ref, gain_out, part_ref
):
    dc = sum4((t0, t1, t2, t3))
    hat, inv = normalize(h2_ref[...])
    gain_out[...] = jnp.sum(dc * hat, axis=0, keepdims=True)
    dh2 = cot_ref[...].astype(F32) + norm_back(dc * gain_ref[...], hat, inv)
    dh2_ref[...] = dh2
    dr = dh2.astype(BF16)
    dr_ref[...] = dr
    dp = (slope_ref[...].astype(F32) * dot_nt(dr, wout_ref[...])).astype(BF16)
    dp_ref[...] = dp
    part_ref[...] = dot_nt(dp, win_ref[...]).astype(BF16)


def message_backward(
    nbr_scale, total_steps, t0, t1, t2, t3, h1_ref, dh2_ref, gain_ref, o0, o1, o2, o3, slope_ref, oht_ref,
    dh1_ref, dt_ref, gain_out, du_ref, r_ref, *rest
):
    s_refs, (g_ref, racc_ref, sacc_ref) = rest[:-3], rest[-3:]
    step = pl.program_id(0)
    slots, rows, _ = slope_ref.shape

    @pl.when(step == 0)
    def _():
        db = sum4((t0, t1, t2, t3))
        hat, inv = normalize(h1_ref[...])
        gain_out[...] = jnp.sum(db * hat, axis=0, keepdims=True)
        dh1 = dh2_ref[...] + norm_back(db * gain_ref[...], hat, inv)
        dh1_ref[...] = dh1
        dt = dh1.astype(BF16)
        dt_ref[...] = dt
        wo = jnp.concatenate([o0[...], o1[...], o2[...], o3[...]], axis=0)
        g_ref[...] = dot_nt(dt, wo) * nbr_scale
        racc_ref[...] = jnp.zeros_like(racc_ref)
        sacc_ref[...] = jnp.zeros_like(sacc_ref)

    for s in range(slots):
        du = (slope_ref[s].astype(F32) * g_ref[...]).astype(BF16)
        du_ref[s] = du
        racc_ref[...] += du.astype(F32)
    dus = du_ref[...].reshape(slots * rows, du_ref.shape[2])
    sacc_ref[...] += dot(oht_ref[...], dus)

    @pl.when(step == total_steps - 1)
    def _():
        r_ref[...] = racc_ref[...].astype(BF16)
        for b, ref in enumerate(s_refs):
            n = ref.shape[0]
            ref[...] = sacc_ref[b * n : (b + 1) * n, :].astype(BF16)


def message_edges(
    et_ref, du_ref, dq_ref, f_ref, cot_ref, ga_ref, gb_ref, w0, w1, w2, w3, out_ref, gedge_ref, gains_ref, eacc_ref
):
    step = pl.program_id(0)
    slots, rows, width_e = et_ref.shape
    we = cat((w0, w1, w2, w3), w0.shape[0] - width_e, w0.shape[0])

    @pl.when(step == 0)
    def _():
        eacc_ref[...] = jnp.zeros_like(eacc_ref)
        gains_ref[...] = jnp.zeros_like(gains_ref)

    for s in range(slots):
        du = du_ref[s]
        df = dot_nt(du, we)
        dq = dq_ref[s].astype(F32)
        hat, inv = normalize(et_ref[s].astype(F32))
        gains_ref[0:1, :] += jnp.sum(df * hat, axis=0, keepdims=True)
        gains_ref[1:2, :] += jnp.sum(dq * hat, axis=0, keepdims=True)
        out_ref[s] = cot_ref[s].astype(F32) + norm_back(
            ga_ref[...] * df + gb_ref[...] * dq, hat, inv
        )
        eacc_ref[...] += dot_tn(f_ref[s], du)
    gedge_ref[...] = eacc_ref[...].astype(BF16)


def node_finish(t0, t1, t2, t3, nodes_ref, dh1_ref, gain_ref, gain_out, out_ref):
    da = sum4((t0, t1, t2, t3))
    hat, inv = normalize(nodes_ref[...].astype(F32))
    gain_out[...] = jnp.sum(da * hat, axis=0, keepdims=True)
    out_ref[...] = dh1_ref[...] + norm_back(da * gain_ref[...], hat, inv)


def whole(shape):
    zeros = (0,) * len(shape)
    return pl.BlockSpec(tuple(shape), lambda i: zeros)


def call(body, grid, ins, outs, scratch=(), vmem=48, flops=0, name=None):
    in_specs = [whole(a.shape) if s is None else s for a, s in ins]
    out_specs = [whole(sh) if s is None else s for sh, _, s in outs]
    moved = sum(a.size * a.dtype.itemsize for a, _ in ins)
    moved += sum(jnp.dtype(t).itemsize * int(jnp.prod(jnp.array(sh))) if False else _bytes(sh, t) for sh, t, _ in outs)
    return pl.pallas_call(
        body,
        grid=(grid,),
        in_specs=in_specs,
        out_specs=out_specs,
        out_shape=[jax.ShapeDtypeStruct(sh, t) for sh, t, _ in outs],
        scratch_shapes=list(scratch),
        compiler_params=pltpu.CompilerParams(
            vmem_limit_bytes=vmem << 20, dimension_semantics=("arbitrary",)
        ),
        cost_estimate=pl.CostEstimate(flops=int(flops), bytes_accessed=int(moved), transcendentals=0),
        name=name,
    )(*[a for a, _ in ins])


def _bytes(shape, dtype):
    n = jnp.dtype(dtype).itemsize
    for d in shape:
        n *= d
    return n


def swap(values, axis, bits, size):
    return lax.ppermute(values, axis, [(i, i ^ bits) for i in range(size)])


def partners(values, axis, size):
    return [values] + [swap(values, axis, k, size) for k in range(1, size)]


def local(sizes, *args):
    (
        nodes, edges, neighbours, resmask, node_gain_a, edge_gain_a, message_self, message_other, message_edge,
        message_out, node_gain_b, ffn_in, ffn_out, node_gain_c, edge_gain_b, update_self, update_other, update_edge,
        update_out, node_cot, edge_cot,
    ) = args
    dp, graph, mp = sizes
    at_core, at_graph, at_mp = (lax.axis_index(a) for a in ("dp", "graph", "mp"))
    _, rows, width = nodes.shape
    slots, width_e = edges.shape[2:]
    nbrs = neighbours.shape[2]
    total = resmask.shape[1]
    hidden = message_self.shape[1] * mp
    near = graph <= 4
    vmem = 40 if total <= 1024 else 60
    tile = 3 if slots % 3 == 0 else 1
    steps = slots // tile

    def tiles(*dims):
        return pl.BlockSpec((tile,) + dims, lambda i: (i,) + (0,) * len(dims))

    def gather_rows(values):
        if near:
            return jnp.concatenate(partners(values, "graph", graph), axis=0)
        return lax.all_gather(values, "graph", axis=0, tiled=True)

    def return_rows(blocks):
        if near:
            return [blocks[0]] + [swap(blocks[k], "graph", k, graph) for k in range(1, graph)]
        one = lax.psum_scatter(
            jnp.concatenate(blocks, axis=0), "graph", scatter_dimension=0, tiled=True
        )
        return [one]

    nbr_own = lax.dynamic_slice_in_dim(neighbours[0], at_mp * slots, slots, axis=1).T
    if near:
        nbr_own = ((nbr_own // rows) ^ at_graph) * rows + nbr_own % rows
        mask_row = jnp.concatenate(
            [lax.dynamic_slice_in_dim(resmask[0], (at_graph ^ k) * rows, rows) for k in range(graph)]
        )
    else:
        mask_row = resmask[0]
    mask_lanes = jnp.broadcast_to(mask_row.astype(BF16)[:, None], (total, 128))

    nodes_all = gather_rows(nodes[0])
    wm = partners(jnp.concatenate([message_self, message_other, message_edge], axis=0), "mp", mp)
    wmo = partners(message_out, "mp", mp)
    wu = partners(jnp.concatenate([update_self, update_other, update_edge], axis=0), "mp", mp)
    wuo = partners(update_out, "mp", mp)

    ga_e, gb_e = edge_gain_a[None, :], edge_gain_b[None, :]
    ga_n, gb_n, gc_n = node_gain_a[None, :], node_gain_b[None, :], node_gain_c[None, :]

    et = jnp.swapaxes(edges[0], 0, 1)
    cot = jnp.swapaxes(edge_cot[0], 0, 1)
    slab = (slots, rows)
    edge_spec = tiles(rows, width_e)
    hid_spec = tiles(rows, hidden)
    oht_spec = pl.BlockSpec((total, tile * rows), lambda i: (0, i))

    f, q, oh, oht, mk = call(
        edge_prep, steps,
        [(et, edge_spec), (nbr_own[:, None, :], tiles(1, rows)), (mask_lanes, None), (ga_e, None), (gb_e, None)],
        [
            (slab + (width_e,), BF16, edge_spec), (slab + (width_e,), BF16, edge_spec),
            (slab + (total,), BF16, tiles(rows, total)), ((total, slots * rows), BF16, oht_spec),
            (slab + (128,), BF16, tiles(rows, 128)),
        ],
        vmem=vmem, name="edge_prep",
    )

    slope_m, pooled_part, a_own = call(
        functools.partial(message_forward, 1.0 / nbrs, steps), steps,
        [(f, edge_spec), (oh, tiles(rows, total)), (mk, tiles(rows, 128)), (nodes_all, None), (ga_n, None)]
        + [(w, None) for w in wm],
        [(slab + (hidden,), BF16, hid_spec), ((rows, hidden), BF16, None), ((rows, width), BF16, None)],
        [pltpu.VMEM((total, hidden), BF16), pltpu.VMEM((rows, hidden), F32), pltpu.VMEM((rows, hidden), F32)],
        vmem=vmem, name="message_forward",
    )

    s_parts = partners(pooled_part, "mp", mp)
    ff = ffn_in.shape[1]
    pooled, h1, b, y, slope_f, h2_part = call(
        node_forward, 1,
        [(v, None) for v in s_parts] + [(nodes[0], None)] + [(v, None) for v in wmo]
        + [(gb_n, None), (ffn_in, None), (ffn_out, None)],
        [((rows, hidden), BF16, None), ((rows, width), F32, None), ((rows, width), BF16, None),
         ((rows, ff), BF16, None), ((rows, ff), BF16, None), ((rows, width), BF16, None)],
        vmem=vmem, name="node_forward",
    )
    h2, c_own, nodes_out = call(
        node_close, 1,
        [(h1, None)] + [(v, None) for v in partners(h2_part, "mp", mp)] + [(gc_n, None)],
        [((rows, width), F32, None), ((rows, width), BF16, None), ((rows, width), BF16, None)],
        vmem=vmem, name="node_close",
    )
    c_all = gather_rows(c_own)

    blocks = [((rows, hidden), BF16, None)] * graph
    wu_ins = [(v, None) for v in wu]
    wuo_ins = [(v, None) for v in wuo]
    w_act, dv, r_upd, *s_upd = call(
        functools.partial(update_kernel, steps), steps,
        [(q, edge_spec), (oh, tiles(rows, total)), (oht, oht_spec), (cot, edge_spec), (c_all, None)] + wu_ins + wuo_ins,
        [(slab + (hidden,), BF16, hid_spec), (slab + (hidden,), BF16, hid_spec), ((rows, hidden), BF16, None)] + blocks,
        [pltpu.VMEM((total, hidden), BF16), pltpu.VMEM((rows, hidden), F32), pltpu.VMEM((rows, hidden), F32),
         pltpu.VMEM((total, hidden), F32)],
        vmem=vmem, name="update_forward_backward",
    )
    s_upd_parts = return_rows(s_upd)

    eo, dq, g_out_t, g_edge_u = call(
        update_edges, steps,
        [(et, edge_spec), (w_act, hid_spec), (dv, hid_spec), (q, edge_spec), (cot, edge_spec)] + wu_ins + wuo_ins,
        [(slab + (width_e,), BF16, edge_spec), (slab + (width_e,), BF16, edge_spec),
         ((width_e, hidden), BF16, None), ((width_e, hidden), BF16, None)],
        [pltpu.VMEM((width_e, hidden), F32), pltpu.VMEM((width_e, hidden), F32)],
        vmem=vmem, name="update_edges",
    )
    edges_out = jnp.swapaxes(eo, 0, 1)[None]

    def terms(r, parts, weights, name):
        outs = [((rows, hidden), BF16, None), ((rows, width), BF16, None)]
        if len(parts) == 4:
            return call(
                node_terms, 1, [(r, None)] + [(v, None) for v in parts] + weights, outs, vmem=vmem, name=name
            )
        (part,) = call(
            node_terms_one, 1, [(r, None), (parts[0], None)] + weights, outs[1:], vmem=vmem, name=name
        )
        return parts[0], part

    s_upd_own, dc_part = terms(r_upd, s_upd_parts, wu_ins, "update_node_terms")
    dc_parts = partners(dc_part, "mp", mp)
    dh2, dr, dp_ffn, gain_c, db_part = call(
        node_backward, 1,
        [(v, None) for v in dc_parts]
        + [(h2, None), (node_cot[0], None), (gc_n, None), (slope_f, None), (ffn_in, None), (ffn_out, None)],
        [((rows, width), F32, None), ((rows, width), BF16, None), ((rows, ff), BF16, None), ((1, width), F32, None),
         ((rows, width), BF16, None)],
        vmem=vmem, name="node_backward",
    )
    db_parts = partners(db_part, "mp", mp)
    dh1, dt, gain_b, du, r_msg, *s_msg = call(
        functools.partial(message_backward, 1.0 / nbrs, steps), steps,
        [(v, None) for v in db_parts] + [(h1, None), (dh2, None), (gb_n, None)] + [(v, None) for v in wmo]
        + [(slope_m, hid_spec), (oht, oht_spec)],
        [((rows, width), F32, None), ((rows, width), BF16, None), ((1, width), F32, None),
         (slab + (hidden,), BF16, hid_spec), ((rows, hidden), BF16, None)] + blocks,
        [pltpu.VMEM((rows, hidden), F32), pltpu.VMEM((rows, hidden), F32), pltpu.VMEM((total, hidden), F32)],
        vmem=vmem, name="message_backward",
    )
    s_msg_parts = return_rows(s_msg)
    wm_ins = [(v, None) for v in wm]
    ge, g_edge_m, gains_e = call(
        message_edges, steps,
        [(et, edge_spec), (du, hid_spec), (dq, edge_spec), (f, edge_spec), (cot, edge_spec), (ga_e, None), (gb_e, None)]
        + wm_ins,
        [(slab + (width_e,), F32, edge_spec), ((width_e, hidden), BF16, None), ((2, width_e), F32, None)],
        [pltpu.VMEM((width_e, hidden), F32)],
        vmem=vmem, name="message_edges",
    )
    grad_edges = jnp.swapaxes(ge, 0, 1)[None]
    s_msg_own, da_part = terms(r_msg, s_msg_parts, wm_ins, "message_node_terms")
    da_parts = partners(da_part, "mp", mp)
    gain_a, grad_nodes = call(
        node_finish, 1,
        [(v, None) for v in da_parts] + [(nodes[0], None), (dh1, None), (ga_n, None)],
        [((1, width), F32, None), ((rows, width), F32, None)],
        vmem=vmem, name="node_finish",
    )

    shard = hidden // mp

    def own_units(partial):
        pieces = [partial[:, k * shard : (k + 1) * shard] for k in range(mp)]
        got = [swap(pieces[k], "mp", k, mp) for k in range(1, mp)]
        return sum((v.astype(F32) for v in got), pieces[0].astype(F32)).astype(BF16)

    def product(left, right):
        return lax.dot_general(left, right, (((0,), (0,)), ((), ())), preferred_element_type=F32).astype(BF16)

    def reduce_all(values):
        half = values.shape[0] // dp
        keep = lax.dynamic_slice_in_dim(values, at_core * half, half)
        send = lax.dynamic_slice_in_dim(values, (1 - at_core) * half, half)
        part = keep.astype(F32) + swap(send, "dp", 1, dp).astype(F32)
        if near:
            part = part.astype(BF16)
            got = lax.ppermute(part, "graph", [(0, 1), (3, 2)])
            part = (part.astype(F32) + got.astype(F32)).astype(BF16)
            got = lax.ppermute(part, "graph", [(1, 2), (2, 1)])
            part = (part.astype(F32) + got.astype(F32)).astype(BF16)
            got = lax.ppermute(part, "graph", [(1, 0), (2, 3)])
            done = jnp.where((at_graph == 1) | (at_graph == 2), part, got)
        else:
            done = lax.psum(part, "graph").astype(BF16)
        other = swap(done, "dp", 1, dp)
        first = jnp.where(at_core == 0, done, other)
        second = jnp.where(at_core == 0, other, done)
        return jnp.concatenate([first, second], axis=0).astype(F32)

    upd = reduce_all(
        jnp.concatenate(
            [product(c_own, own_units(r_upd)), product(c_own, own_units(s_upd_own)), own_units(g_edge_u), own_units(g_out_t)],
            axis=0,
        )
    )
    ffn = reduce_all(jnp.concatenate([product(b, dp_ffn), product(y, dr)], axis=0))
    msg = reduce_all(
        jnp.concatenate(
            [product(a_own, own_units(r_msg)), product(a_own, own_units(s_msg_own)), own_units(g_edge_m),
             product(dt, pooled[:, :shard])],
            axis=0,
        )
    )

    gains_e = sum(partners(gains_e, "mp", mp))
    gains = jnp.concatenate([gain_a, gain_b, gain_c, jnp.pad(gains_e, ((0, 0), (0, width - width_e)))], axis=0)
    gains = gains + swap(gains, "dp", 1, dp)
    if near:
        gains = sum(partners(gains, "graph", graph))
    else:
        gains = lax.psum(gains, "graph")

    e0, e1 = 2 * width, 2 * width + width_e
    return (
        nodes_out[None],
        edges_out,
        grad_nodes[None],
        grad_edges,
        gains[0],
        gains[3, :width_e],
        msg[:width],
        msg[width:e0],
        msg[e0:e1],
        msg[e1:].T,
        gains[1],
        ffn[:width],
        ffn[width:],
        gains[2],
        gains[4, :width_e],
        upd[:width],
        upd[width:e0],
        upd[e0:e1],
        upd[e1:].T,
    )


def solution(mesh):
    sizes = (mesh.shape["dp"], mesh.shape["graph"], mesh.shape["mp"])
    rows = P("dp", "graph", None)
    slots = P("dp", "graph", "mp", None)
    cols, tops = P(None, "mp"), P("mp", None)
    return jax.shard_map(
        functools.partial(local, sizes),
        mesh=mesh,
        in_specs=(
            rows, slots, rows, P("dp", None), P(), P(), cols, cols, cols, tops, P(), cols, tops, P(), P(), cols, cols,
            cols, tops, rows, slots,
        ),
        out_specs=(
            rows, slots, rows, slots, P(), P(), cols, cols, cols, tops, P(), cols, tops, P(), P(), cols, cols, cols,
            tops,
        ),
        check_vma=False,
    )
```

```python
import functools

import jax
import jax.numpy as jnp
from jax import lax
from jax.experimental import pallas as pl
from jax.experimental.pallas import tpu as pltpu
from jax.sharding import PartitionSpec as P

EPSILON = 1e-05
F32 = jnp.float32
BF16 = jnp.bfloat16
GELU_A = 0.7978845608028654
GELU_B = 0.044715


def dot(left, right):
    return lax.dot_general(left, right, (((1,), (0,)), ((), ())), preferred_element_type=F32)


def dot_nt(left, right):
    return lax.dot_general(left, right, (((1,), (1,)), ((), ())), preferred_element_type=F32)


def dot_tn(left, right):
    return lax.dot_general(left, right, (((0,), (0,)), ((), ())), preferred_element_type=F32)


def normalize(values, axis=-1):
    centre = values - jnp.mean(values, axis=axis, keepdims=True)
    variance = jnp.mean(centre * centre, axis=axis, keepdims=True)
    scale_inv = lax.rsqrt(variance + EPSILON)
    return centre * scale_inv, scale_inv


def norm_back(grad_hat, normed, scale_inv, axis=-1):
    return scale_inv * (
        grad_hat
        - jnp.mean(grad_hat, axis=axis, keepdims=True)
        - normed * jnp.mean(grad_hat * normed, axis=axis, keepdims=True)
    )


def gelu_both(u):
    poly = GELU_A + (GELU_A * GELU_B) * (u * u)
    half = 0.5 + 0.5 * jnp.tanh(u * poly)
    value = u * half
    return value, half + (value * (1.0 - half)) * (6.0 * poly - 4.0 * GELU_A)


def stack(refs, lo, hi):
    return jnp.concatenate([r[:, lo:hi] for r in refs], axis=0)


def rows_of(refs):
    return refs[0][...] if len(refs) == 1 else jnp.concatenate([r[...] for r in refs], axis=0)


def sum_of(refs, lo=None, hi=None):
    parts = [r[...].astype(F32) if lo is None else r[:, lo:hi].astype(F32) for r in refs]
    while len(parts) > 1:
        parts = [sum(parts[i : i + 2]) if i + 1 < len(parts) else parts[i] for i in range(0, len(parts), 2)]
    return parts[0]


def spread(row, count):
    return jnp.concatenate([row[:, i * 128 : i * 128 + 128] for i in range(count)], axis=0)


def by_core(first, second):
    core = lax.axis_index("dp")
    pl.when(core == 0)(first)
    pl.when(core != 0)(second)


def onehot(idx, total):
    here = lax.broadcasted_iota(jnp.int32, (total, idx.shape[1]), 0)
    return (here == idx).astype(F32).astype(BF16)


def lanes(refs):
    return jnp.concatenate([refs[s] for s in range(refs.shape[0])], axis=1)


def edge_prep(graph, near, et_ref, nbr_ref, res_ref, ga_ref, gb_ref, f_ref, q_ref, idx_ref, mask_ref, gains_ref):
    rows = et_ref.shape[2]
    slots, total = idx_ref.shape[0], mask_ref.shape[1]

    @pl.when(pl.program_id(0) == 0)
    def _():
        at_graph, at_mp = lax.axis_index("graph"), lax.axis_index("mp")
        for s in range(slots):
            nbr = nbr_ref[at_mp * slots + s]
            if near:
                idx_ref[s] = ((nbr // rows) ^ at_graph) * rows + lax.rem(nbr, rows)
            else:
                moved = nbr + (total - at_graph * rows)
                idx_ref[s] = jnp.where(moved >= total, moved - total, moved)
        for k in range(graph):
            block = (at_graph ^ k) if near else lax.rem(at_graph + k, graph)
            mask_ref[:, k * rows : (k + 1) * rows] = res_ref[:, pl.ds(pl.multiple_of(block * rows, rows), rows)]
        for i, ref in enumerate((ga_ref, gb_ref)):
            gains_ref[i] = jnp.broadcast_to(ref[...], (rows, ref.shape[1])).T

    for s in range(et_ref.shape[0]):
        hat, _ = normalize(et_ref[s].astype(F32), 0)
        f_ref[s] = (hat * gains_ref[0]).astype(BF16)
        q_ref[s] = (hat * gains_ref[1]).astype(BF16)


def node_close(h1_ref, p0, p1, p2, p3, gain_ref, h2_ref, c_ref, out_ref):
    h2 = h1_ref[...] + sum_of((p0, p1, p2, p3))
    h2_ref[...] = h2
    hat, _ = normalize(h2)
    c_ref[...] = (hat * gain_ref[...]).astype(BF16)
    out_ref[...] = h2.astype(BF16)


def node_backward(
    t0, t1, t2, t3, h2_ref, cot_ref, gain_ref, slope_ref, win_ref, wout_ref,
    dh2_ref, dr_ref, dp_ref, gain_out, share_ref, part_ref,
):
    width = h2_ref.shape[1]
    dc = sum_of((t0, t1, t2, t3), 0, width)
    share_ref[...] = sum_of((t0, t1, t2, t3), width, width + 128).astype(BF16)
    hat, inv = normalize(h2_ref[...])
    gain_out[...] = jnp.sum(dc * hat, axis=0, keepdims=True)
    dh2 = cot_ref[...].astype(F32) + norm_back(dc * gain_ref[...], hat, inv)
    dh2_ref[...] = dh2
    dr = dh2.astype(BF16)
    dr_ref[...] = dr
    dp = (slope_ref[...].astype(F32) * dot_nt(dr, wout_ref[...])).astype(BF16)
    dp_ref[...] = dp
    part_ref[...] = dot_nt(dp, win_ref[...]).astype(BF16)


def pack_weights(ms, mo, me, mout, us, uo, ue, uout_t, front_ref, back_ref, mine_ref, first_ref, second_ref, half_ref):
    side = me.shape[0]
    gap = jnp.zeros((ms.shape[1], 256 - side), BF16)

    def turned(ref):
        return ref[...].astype(F32).T.astype(BF16)

    front = jnp.concatenate([turned(mo), turned(me), gap, turned(ue), gap], axis=1)
    back = jnp.concatenate([turned(ms), mout[...]], axis=1)
    out = jnp.concatenate([turned(uout_t), gap], axis=1)
    first = jnp.concatenate([turned(uo), out[:, :128]], axis=1)
    second = jnp.concatenate([turned(us), out[:, 128:]], axis=1)
    front_ref[...] = front
    back_ref[...] = back
    first_ref[...] = first
    second_ref[...] = second

    def keep_front():
        mine_ref[...] = front
        half_ref[...] = first

    def keep_back():
        mine_ref[...] = back
        half_ref[...] = second

    by_core(keep_front, keep_back)


def message_forward(nbr_scale, steps, parts, f_ref, idx_ref, mask_ref, gain_ref, front_ref, back_ref, *rest):
    node_refs, got, swapped = rest[:parts], rest[parts : parts + 3], rest[parts + 3 : parts + 6]
    slope_ref, pooled_ref, a_ref, fronts_ref, backs_ref, lhs_ref, rhs_ref, ps_ref, acc_ref = rest[parts + 6 :]
    step = pl.program_id(0)
    slots, side, rows = f_ref.shape
    total, width = a_ref.shape
    hidden = ps_ref.shape[0]

    @pl.when(step == 0)
    def _():
        fronts_ref[:rows, :] = front_ref[...]
        backs_ref[:rows, :] = back_ref[...]

        def place(front_of, back_of):
            for k in range(3):
                fronts_ref[(k + 1) * rows : (k + 2) * rows, :] = front_of[k][...]
                backs_ref[(k + 1) * rows : (k + 2) * rows, :] = back_of[k][...]

        by_core(lambda: place(got, swapped), lambda: place(swapped, got))
        block = node_refs[0].shape[0] if parts > 1 else 512
        for at in range(0, total, block):
            ref = node_refs[at // block] if parts > 1 else node_refs[0].at[at : at + block]
            hat, _ = normalize(ref[...].astype(F32))
            a = (hat * gain_ref[...]).astype(BF16)
            a_ref[at : at + block, :] = a
            lhs_ref[:hidden, at : at + block] = dot_nt(fronts_ref[:, :width], a).astype(BF16)
        lhs_ref[:hidden, total:] = fronts_ref[:, width : width + side]
        top = lax.broadcasted_iota(jnp.int32, (16, total), 0) == 0
        lhs_ref[hidden:, :total] = jnp.where(top, mask_ref[...].astype(F32), 0.0).astype(BF16)
        lhs_ref[hidden:, total:] = jnp.zeros((16, side), BF16)
        ps_ref[...] = dot_nt(backs_ref[:, :width], a_ref[:rows, :])
        acc_ref[...] = jnp.zeros_like(acc_ref)

    for s in range(slots):
        rhs_ref[:total, s * rows : (s + 1) * rows] = onehot(idx_ref[s], total)
        rhs_ref[total:, s * rows : (s + 1) * rows] = f_ref[s]
    u_all = dot(lhs_ref[...], rhs_ref[...])
    for s in range(slots):
        u = u_all[:hidden, s * rows : (s + 1) * rows] + ps_ref[...]
        mask = u_all[hidden : hidden + 1, s * rows : (s + 1) * rows]
        z, slope = gelu_both(u)
        acc_ref[...] += z * mask
        slope_ref[s] = (slope * mask).astype(BF16)

    @pl.when(step == steps - 1)
    def _():
        pooled_ref[...] = (acc_ref[...] * nbr_scale).T.astype(BF16)


def node_forward(
    s0, s1, s2, s3, nodes_ref, backs_ref, gain_ref, win_ref, wout_ref, s_ref, h1_ref, b_ref, y_ref, slope_ref, part_ref
):
    width = nodes_ref.shape[1]
    sums = []
    for p in range(4):
        sums.append(sum(
            ref[:, (p ^ k) * 128 : (p ^ k) * 128 + 128].astype(F32) for k, ref in enumerate((s0, s1, s2, s3))
        ).astype(BF16))
    pooled = jnp.concatenate(sums, axis=1)
    s_ref[...] = pooled
    h1 = nodes_ref[...].astype(F32) + dot(pooled, backs_ref[:, width : 2 * width])
    h1_ref[...] = h1
    hat, _ = normalize(h1)
    b = (hat * gain_ref[...]).astype(BF16)
    b_ref[...] = b
    y, slope = gelu_both(dot(b, win_ref[...]))
    y = y.astype(BF16)
    y_ref[...] = y
    slope_ref[...] = slope.astype(BF16)
    part_ref[...] = dot(y, wout_ref[...]).astype(BF16)


def update_nodes(steps, parts, outs, q_ref, cot_ref, idx_ref, fronts_ref, *rest):
    node_refs, (first_ref, second_ref) = rest[:parts], rest[parts : parts + 2]
    got, swapped = rest[parts + 2 : parts + 5], rest[parts + 5 : parts + 8]
    w_ref, dv_ref, r_ref, firsts_ref, seconds_ref = rest[parts + 8 : parts + 13]
    s_refs = rest[parts + 13 : parts + 13 + outs]
    lhs_ref, rhs_ref, ps_ref, wo_ref, racc_ref, sacc_ref = rest[parts + 13 + outs :]
    step = pl.program_id(0)
    slots, side, rows = q_ref.shape
    total = rhs_ref.shape[0] - side
    width = node_refs[0].shape[1]

    @pl.when(step == 0)
    def _():
        firsts_ref[:rows, :] = first_ref[...]
        seconds_ref[:rows, :] = second_ref[...]

        def place(first_of, second_of):
            for k in range(3):
                firsts_ref[(k + 1) * rows : (k + 2) * rows, :] = first_of[k][...]
                seconds_ref[(k + 1) * rows : (k + 2) * rows, :] = second_of[k][...]

        by_core(lambda: place(got, swapped), lambda: place(swapped, got))
        block = node_refs[0].shape[0] if parts > 1 else 512
        for at in range(0, total, block):
            ref = node_refs[at // block] if parts > 1 else node_refs[0].at[at : at + block]
            lhs_ref[:, at : at + block] = dot_nt(firsts_ref[:, :width], ref[...]).astype(BF16)
        lhs_ref[:, total:] = fronts_ref[:, width + 256 : width + 256 + side]
        wo_ref[...] = jnp.concatenate([firsts_ref[:, width:], seconds_ref[:, width : width + side - 128]], axis=1)
        ps_ref[...] = dot_nt(seconds_ref[:, :width], node_refs[0][:rows, :])
        racc_ref[...] = jnp.zeros_like(racc_ref)
        sacc_ref[...] = jnp.zeros_like(sacc_ref)

    for s in range(slots):
        rhs_ref[:total, s * rows : (s + 1) * rows] = onehot(idx_ref[s], total)
        rhs_ref[total:, s * rows : (s + 1) * rows] = q_ref[s]
    v_all = dot(lhs_ref[...], rhs_ref[...])
    g_all = dot(wo_ref[...], lanes(cot_ref))
    dvs = []
    for s in range(slots):
        w, slope = gelu_both(v_all[:, s * rows : (s + 1) * rows] + ps_ref[...])
        w_ref[s] = w.astype(BF16)
        dv = slope * g_all[:, s * rows : (s + 1) * rows]
        racc_ref[...] += dv
        dv = dv.astype(BF16)
        dv_ref[s] = dv
        dvs.append(dv)
    sacc_ref[...] += dot_nt(rhs_ref[:total, :], jnp.concatenate(dvs, axis=1))

    @pl.when(step == steps - 1)
    def _():
        r_ref[...] = racc_ref[...].T.astype(BF16)
        for b, ref in enumerate(s_refs):
            n = ref.shape[0]
            ref[...] = sacc_ref[b * n : (b + 1) * n, :].astype(BF16)


def update_edges(
    steps, et_ref, w_ref, dv_ref, q_ref, cot_ref, r_ref, fronts_ref, firsts_ref, seconds_ref,
    out_ref, dq_ref, x0, x1, x2, x3, ue_ref, uo_ref, gout_ref, gedge_ref,
):
    step = pl.program_id(0)
    slots, side, rows = et_ref.shape
    width = r_ref.shape[1]

    @pl.when(step == 0)
    def _():
        ue_ref[...] = fronts_ref[:, width + 256 : width + 256 + side].astype(F32).T.astype(BF16)
        uo = jnp.concatenate([firsts_ref[:, width:], seconds_ref[:, width : width + side - 128]], axis=1)
        uo_ref[...] = uo.astype(F32).T.astype(BF16)
        gout_ref[...] = jnp.zeros_like(gout_ref)
        gedge_ref[...] = jnp.zeros_like(gedge_ref)

    w, dv = lanes(w_ref), lanes(dv_ref)
    o_all = dot(uo_ref[...], w)
    dq_all = dot(ue_ref[...], dv)
    for s in range(slots):
        out_ref[s] = (et_ref[s].astype(F32) + o_all[:, s * rows : (s + 1) * rows]).astype(BF16)
        dq_ref[s] = dq_all[:, s * rows : (s + 1) * rows].astype(BF16)
    gout_ref[...] += dot_nt(lanes(cot_ref), w)
    gedge_ref[...] += dot_nt(lanes(q_ref), dv)

    @pl.when(step == steps - 1)
    def _():
        for k, ref in enumerate((x0, x1, x2, x3)):
            at = slice(k * 128, k * 128 + 128)
            ref[:rows, :] = r_ref[:, at]
            ref[rows : rows + side, :] = gedge_ref[:, at].astype(BF16)
            ref[rows + side :, :] = gout_ref[:, at].astype(BF16)


def update_terms(parts, r_ref, firsts_ref, seconds_ref, *rest):
    s_refs, outs = rest[:parts], rest[parts + 1 :]
    width = r_ref.shape[1]
    total = sum_of(s_refs).astype(BF16)
    term = (dot(r_ref[...], seconds_ref[:, :width]) + dot(total, firsts_ref[:, :width])).astype(BF16)
    for k, ref in enumerate(outs):
        ref[:, :width] = term
        ref[:, width:] = total[:, k * 128 : k * 128 + 128]


def message_terms(parts, r_ref, fronts_ref, backs_ref, nodes_ref, gb_ref, gc_ref, ge_ref, *rest):
    s_refs, outs = rest[:parts], rest[parts:]
    rows, width = r_ref.shape
    total = sum_of(s_refs).astype(BF16)
    term = dot(r_ref[...], backs_ref[:, :width]) + dot(total, fronts_ref[:, :width])
    hat, _ = normalize(nodes_ref[...].astype(F32))
    gain = jnp.sum(term * hat, axis=0, keepdims=True)
    edge = jnp.concatenate([ge_ref[0:2, :], jnp.zeros((2, width - 256), F32)], axis=1)
    gains = jnp.concatenate(
        [gain, gb_ref[...] * 0.25, gc_ref[...] * 0.25, edge, jnp.zeros((11, width), F32)], axis=0
    ).astype(BF16)
    term = term.astype(BF16)
    for k, ref in enumerate(outs):
        ref[:rows, :width] = term
        ref[:rows, width:] = total[:, k * 128 : k * 128 + 128]
        ref[rows:, :width] = gains
        ref[rows:, width:] = jnp.zeros((16, 128), BF16)


def early_grads(b_ref, dp_ref, y_ref, dr_ref, c_ref, share_ref, x0, x1, x2, x3, keep_ref, send_ref):
    rows, width = c_ref.shape
    extra = sum_of((x0, x1, x2, x3)).astype(BF16)
    side = (extra.shape[0] - rows) // 2
    part = (width + side) // 4
    piece = keep_ref.shape[0] // 4

    def put(ref, large, small):
        large = large.astype(BF16)
        small = jnp.concatenate(small, axis=0)
        for i in range(4):
            ref[i * piece : i * piece + 128, :] = large[i * 128 : i * 128 + 128]
            own = jnp.concatenate([small[i * part : (i + 1) * part], jnp.zeros((192 - part, 128), F32)], axis=0)
            ref[i * piece + 128 : (i + 1) * piece, :] = jnp.concatenate(
                [own[j * 48 : j * 48 + 48] for j in range(4)], axis=1
            ).astype(BF16)

    def run(one, two):
        put(one, dot_tn(b_ref[...], dp_ref[...]),
            [dot_tn(c_ref[...], extra[:rows]), extra[rows : rows + side].astype(F32)])
        put(two, dot_tn(y_ref[...], dr_ref[...]),
            [dot_tn(c_ref[...], share_ref[...]), extra[rows + side :].astype(F32)])

    by_core(lambda: run(keep_ref, send_ref), lambda: run(send_ref, keep_ref))


def early_pieces(keep_ref, got_ref, *outs):
    piece = keep_ref.shape[0] // 4
    for k, ref in enumerate(outs):
        at = pl.ds(pl.multiple_of((lax.axis_index("graph") ^ k) * piece, 16), piece)
        ref[...] = (keep_ref[at, :].astype(F32) + got_ref[at, :].astype(F32)).astype(BF16)


def early_total(p0, p1, p2, p3, out_ref):
    out_ref[...] = sum_of((p0, p1, p2, p3)).astype(BF16)


def finish_early(near, *refs):
    mine, theirs = refs[:4], refs[4:8]
    gin_ref, gout_ref, self_ref, edge_ref, other_ref, out_ref, one_ref, two_ref = refs[8:]
    width, side = gin_ref.shape[0], edge_ref.shape[0]
    part = (width + side) // 4

    def run(one, two):
        for pieces, large, small in ((one, gin_ref, one_ref), (two, gout_ref, two_ref)):
            for k, ref in enumerate(pieces):
                i = (lax.axis_index("graph") ^ k) if near else k
                large[pl.ds(pl.multiple_of(i * 128, 128), 128), :] = ref[:128, :].astype(F32)
                own = jnp.concatenate([ref[128:, j * 128 : j * 128 + 128] for j in range(4)], axis=0).astype(F32)
                small[pl.ds(pl.multiple_of(i * part, 16), part), :] = own[:part]

    by_core(lambda: run(mine, theirs), lambda: run(theirs, mine))
    self_ref[...] = one_ref[:width, :]
    edge_ref[...] = one_ref[width:, :]
    other_ref[...] = two_ref[:width, :]
    out_ref[...] = two_ref[width:, :]


def message_backward(nbr_scale, steps, outs, t0, t1, t2, t3, h1_ref, dh2_ref, gain_ref, backs_ref, slope_ref, idx_ref, *rest):
    rest = rest[1:]
    dh1_ref, dt_ref, gain_out, du_ref, r_ref = rest[:5]
    s_refs = rest[5 : 5 + outs]
    g_ref, racc_ref, sacc_ref = rest[5 + outs :]
    step = pl.program_id(0)
    slots, hidden, rows = slope_ref.shape
    total, width = sacc_ref.shape[0], h1_ref.shape[1]

    @pl.when(step == 0)
    def _():
        db = sum_of((t0, t1, t2, t3))
        hat, inv = normalize(h1_ref[...])
        gain_out[...] = jnp.sum(db * hat, axis=0, keepdims=True)
        dh1 = dh2_ref[...] + norm_back(db * gain_ref[...], hat, inv)
        dh1_ref[...] = dh1
        dt = dh1.astype(BF16)
        dt_ref[...] = dt
        g_ref[...] = dot_nt(backs_ref[:, width : 2 * width], dt) * nbr_scale
        racc_ref[...] = jnp.zeros_like(racc_ref)
        sacc_ref[...] = jnp.zeros_like(sacc_ref)

    dus, hots = [], []
    for s in range(slots):
        du = slope_ref[s].astype(F32) * g_ref[...]
        racc_ref[...] += du
        du = du.astype(BF16)
        du_ref[s] = du
        dus.append(du)
        hots.append(onehot(idx_ref[s], total))
    sacc_ref[...] += dot_nt(jnp.concatenate(hots, axis=1), jnp.concatenate(dus, axis=1))

    @pl.when(step == steps - 1)
    def _():
        r_ref[...] = racc_ref[...].T.astype(BF16)
        for b, ref in enumerate(s_refs):
            n = ref.shape[0]
            ref[...] = sacc_ref[b * n : (b + 1) * n, :].astype(BF16)


def message_edges(
    steps, et_ref, du_ref, dq_ref, f_ref, cot_ref, gains_ref, r_ref, fronts_ref, out_ref, ge_ref, m0, m1, m2, m3,
    we_ref, gedge_ref, ga_ref, gb_ref,
):
    step = pl.program_id(0)
    slots, side, rows = et_ref.shape
    width = r_ref.shape[1]

    @pl.when(step == 0)
    def _():
        we_ref[...] = fronts_ref[:, width : width + side].astype(F32).T.astype(BF16)
        gedge_ref[...] = jnp.zeros_like(gedge_ref)
        ga_ref[...] = jnp.zeros_like(ga_ref)
        gb_ref[...] = jnp.zeros_like(gb_ref)

    du = lanes(du_ref)
    df_all = dot(we_ref[...], du)
    gedge_ref[...] += dot_nt(lanes(f_ref), du)
    for s in range(slots):
        df = df_all[:, s * rows : (s + 1) * rows]
        dq = dq_ref[s].astype(F32)
        hat, inv = normalize(et_ref[s].astype(F32), 0)
        ga_ref[...] += df * hat
        gb_ref[...] += dq * hat
        out_ref[s] = cot_ref[s].astype(F32) + norm_back(gains_ref[0] * df + gains_ref[1] * dq, hat, inv, 0)

    @pl.when(step == steps - 1)
    def _():
        lane = lax.broadcasted_iota(jnp.int32, (side, 256), 1)
        row = lax.broadcasted_iota(jnp.int32, (side, 256), 0)

        def laid(ref):
            column = jnp.sum(ref[...], axis=1, keepdims=True)
            return jnp.sum(jnp.where(row == lane, column, 0.0), axis=0, keepdims=True)

        ge_ref[...] = jnp.concatenate([laid(ga_ref), laid(gb_ref), jnp.zeros((6, 256), F32)], axis=0)
        for k, ref in enumerate((m0, m1, m2, m3)):
            at = slice(k * 128, k * 128 + 128)
            ref[:rows, :] = r_ref[:, at]
            ref[rows:, :] = gedge_ref[:, at].astype(BF16)


def late_grads(m0, m1, m2, m3, s_ref, dt_ref, order_ref, share_ref, keep_ref, send_ref):
    rows, width = dt_ref.shape
    total = sum_of((m0, m1, m2, m3))
    share_ref[...] = total[:rows].astype(BF16)
    gout = dot_tn(s_ref[...], dt_ref[...])
    every = jnp.concatenate([total[rows:]] + [gout[:, i * 128 : i * 128 + 128] for i in range(width // 128)], axis=0)
    every = every.astype(BF16)
    half = keep_ref.shape[0]

    def put(one, two):
        one[...] = every[:half]
        two[...] = every[half:]

    by_core(lambda: put(keep_ref, send_ref), lambda: put(send_ref, keep_ref))


def node_finish(t0, t1, t2, t3, nodes_ref, dh1_ref, gain_ref, out_ref, share_ref):
    rows, width = dh1_ref.shape
    every = sum_of((t0, t1, t2, t3))
    hat, inv = normalize(nodes_ref[...].astype(F32))
    out_ref[...] = dh1_ref[...] + norm_back(every[:rows, :width] * gain_ref[...], hat, inv)
    share_ref[:rows, :] = every[:rows, width:].astype(BF16)
    share_ref[rows:, :] = jnp.concatenate(
        [every[rows : rows + 8, i * 128 : i * 128 + 128] for i in range(width // 128)], axis=0
    ).astype(BF16)


def message_grads(parts, a_ref, *rest):
    one, two, out_ref = rest[:parts], rest[parts : 2 * parts], rest[2 * parts]
    rows = a_ref.shape[0] // parts
    width = a_ref.shape[1]
    other = dot_tn(a_ref[...], jnp.concatenate([r[:rows, :] for r in two], axis=0))
    own = dot_tn(a_ref[...], jnp.concatenate([r[:rows, :] for r in one], axis=0))
    out_ref[:width, :] = other.astype(BF16)
    out_ref[width : 2 * width, :] = own.astype(BF16)
    low = 2 * width + one[0].shape[0] - rows
    out_ref[2 * width : low, :] = sum(r[rows:, :].astype(F32) for r in one).astype(BF16)
    out_ref[low:, :] = sum(r[rows:, :].astype(F32) for r in two).astype(BF16)


def finish_late(
    mine_ref, theirs_ref, other_ref, self_ref, edge_ref, out_ref, ga_ref, gb_ref, gc_ref, gea_ref, geb_ref
):
    width, side = other_ref.shape[0], edge_ref.shape[0]
    rows = out_ref.shape[0]
    other_ref[...] = mine_ref[:width, :].astype(F32) + theirs_ref[:width, :].astype(F32)
    self_ref[...] = mine_ref[width : 2 * width, :].astype(F32) + theirs_ref[width : 2 * width, :].astype(F32)
    low = mine_ref.shape[0] - 8 * (width // 128)
    gains = mine_ref[low:, :].astype(F32) + theirs_ref[low:, :].astype(F32)
    for i, ref in enumerate((ga_ref, gb_ref, gc_ref)):
        ref[...] = jnp.concatenate([gains[8 * j + i : 8 * j + i + 1] for j in range(width // 128)], axis=1)
    for i, ref in ((3, gea_ref), (4, geb_ref)):
        ref[...] = jnp.concatenate([gains[i : i + 1], gains[8 + i : 9 + i]], axis=1)[:, :side]

    def run(first, second):
        every = jnp.concatenate([first[2 * width : low, :], second[2 * width : low, :]], axis=0).astype(F32)
        edge_ref[...] = every[:side]
        out_ref[...] = jnp.concatenate(
            [every[side + i * rows : side + (i + 1) * rows] for i in range(width // 128)], axis=1
        )

    by_core(lambda: run(mine_ref, theirs_ref), lambda: run(theirs_ref, mine_ref))


def whole(shape):
    zeros = (0,) * len(shape)
    return pl.BlockSpec(tuple(shape), lambda i: zeros)


def in_bytes(shape, dtype):
    n = jnp.dtype(dtype).itemsize
    for d in shape:
        n *= d
    return n


AFTER = pl.BlockSpec(memory_space=pl.ANY)


def call(name, body, grid, ins, outs, scratch=(), vmem=24):
    ins = [a if isinstance(a, tuple) else (a, whole(a.shape)) for a in ins]
    outs = [o if len(o) == 3 else o + (whole(o[0]),) for o in outs]
    moved = sum(in_bytes(a.shape, a.dtype) for a, _ in ins) + sum(in_bytes(sh, t) for sh, t, _ in outs)
    return pl.pallas_call(
        body,
        grid=(grid,),
        in_specs=[s for _, s in ins],
        out_specs=[s for _, _, s in outs],
        out_shape=[jax.ShapeDtypeStruct(sh, t) for sh, t, _ in outs],
        scratch_shapes=list(scratch),
        compiler_params=pltpu.CompilerParams(vmem_limit_bytes=vmem << 20, dimension_semantics=("arbitrary",)),
        cost_estimate=pl.CostEstimate(flops=0, bytes_accessed=moved, transcendentals=0),
        name=name,
    )(*[a for a, _ in ins])


def swap(values, axis, bits, size):
    return lax.ppermute(values, axis, [(i, i ^ bits) for i in range(size)])


def partners(values, axis, size):
    return [values] + [swap(values, axis, k, size) for k in range(1, size)]


def deal(pieces, axis, size):
    return [pieces[0]] + [swap(pieces[k], axis, k, size) for k in range(1, size)]


def turn(values, start, axis):
    return lax.dynamic_slice_in_dim(
        jnp.concatenate([values, values], axis=axis), start, values.shape[axis], axis=axis
    )


def after(values, *others):
    return lax.optimization_barrier((values,) + others)[0]


def local(sizes, *args):
    (
        nodes, edges, neighbours, resmask, node_gain_a, edge_gain_a, message_self, message_other, message_edge,
        message_out, node_gain_b, ffn_in, ffn_out, node_gain_c, edge_gain_b, update_self, update_other, update_edge,
        update_out, node_cot, edge_cot,
    ) = args
    cores, graph, mp = sizes
    near = graph <= 4
    at_graph = None if near else lax.axis_index("graph")
    _, rows, width = nodes.shape
    slots, side = edges.shape[2:]
    nbrs = neighbours.shape[2]
    total = resmask.shape[1]
    shard = message_self.shape[1]
    hidden = shard * mp
    ff = ffn_in.shape[1]
    vmem = 16 if total <= 1024 else 60
    tile = 3 if slots % 3 == 0 else 1
    steps = slots // tile
    run = functools.partial(call, vmem=vmem)

    def tiles(*dims):
        return pl.BlockSpec((tile,) + dims, lambda i: (i,) + (0,) * len(dims))

    def gather_rows(values):
        if near:
            return partners(values, "graph", graph)
        return [turn(lax.all_gather(values, "graph", axis=0, tiled=True), at_graph * rows, 0)]

    def return_rows(blocks):
        if near:
            return deal(blocks, "graph", graph)
        placed = turn(blocks[0], total - at_graph * rows, 0)
        return [lax.psum_scatter(placed, "graph", scatter_dimension=0, tiled=True)]

    blocks = [((rows, hidden), BF16)] * graph if near else [((total, hidden), BF16)]
    outs = len(blocks)
    node, cot_n = nodes[0], node_cot[0]
    ga_n, gb_n, gc_n = node_gain_a[None, :], node_gain_b[None, :], node_gain_c[None, :]

    front, back, mine, first, second, half = run(
        "pack_weights", pack_weights, 1,
        [pltpu.with_memory_space_constraint(w, pltpu.HBM) for w in (
            message_self, message_other, message_edge, message_out, update_self, update_other, update_edge, update_out.T
        )],
        [((shard, width + 512), BF16)] + [((shard, 2 * width), BF16)] * 2 + [((shard, width + 128), BF16)] * 3,
    )
    got = partners(mine, "mp", mp)[1:]
    nodes_all = gather_rows(node)
    swapped = [swap(v, "dp", 1, cores) for v in got]

    et = jnp.transpose(edges[0], (1, 2, 0))
    cot = jnp.transpose(edge_cot[0], (1, 2, 0))
    edge_spec, hid_spec = tiles(side, rows), tiles(hidden, rows)
    edge_sh, hid_sh = (slots, side, rows), (slots, hidden, rows)

    f, q, idx, mask_row, gains_e = run(
        "edge_prep", functools.partial(edge_prep, graph, near), steps,
        [(et, edge_spec), jnp.transpose(neighbours, (2, 0, 1)), resmask, edge_gain_a[None, :], edge_gain_b[None, :]],
        [(edge_sh, BF16, edge_spec), (edge_sh, BF16, edge_spec), ((slots, 1, rows), jnp.int32), ((1, total), jnp.int32),
         ((2, side, rows), F32)],
    )
    idx = (idx, tiles(1, rows))
    slope_m, pooled_part, a_all, fronts, backs = run(
        "message_forward", functools.partial(message_forward, 1.0 / nbrs, steps, len(nodes_all)), steps,
        [(f, edge_spec), idx, mask_row, ga_n, front, back] + nodes_all + got + swapped,
        [(hid_sh, BF16, hid_spec), ((rows, hidden), BF16), ((total, width), BF16), ((hidden, width + 512), BF16),
         ((hidden, 2 * width), BF16)],
        [pltpu.VMEM((hidden + 16, total + side), BF16), pltpu.VMEM((total + side, tile * rows), BF16),
         pltpu.VMEM((hidden, rows), F32), pltpu.VMEM((hidden, rows), F32)],
    )

    pooled, h1, b, y, slope_f, h2_part = run(
        "node_forward", node_forward, 1,
        partners(pooled_part, "mp", mp) + [node, backs, gb_n, ffn_in, ffn_out],
        [((rows, hidden), BF16), ((rows, width), F32), ((rows, width), BF16), ((rows, ff), BF16), ((rows, ff), BF16),
         ((rows, width), BF16)],
    )
    h2, c_own, nodes_out = run(
        "node_close", node_close, 1, [h1] + partners(h2_part, "mp", mp) + [gc_n],
        [((rows, width), F32), ((rows, width), BF16), ((rows, width), BF16)],
    )
    c_all = gather_rows(c_own)
    late_got = partners(after(half, c_own), "mp", mp)[1:]
    late_swapped = [swap(v, "dp", 1, cores) for v in late_got]

    w_act, dv, r_upd, firsts, seconds, *s_upd = run(
        "update_nodes", functools.partial(update_nodes, steps, len(c_all), outs), steps,
        [(q, edge_spec), (cot, edge_spec), idx, fronts] + c_all + [first, second] + late_got + late_swapped,
        [(hid_sh, BF16, hid_spec), (hid_sh, BF16, hid_spec), ((rows, hidden), BF16)]
        + [((hidden, width + 128), BF16)] * 2 + blocks,
        [pltpu.VMEM((hidden, total + side), BF16), pltpu.VMEM((total + side, tile * rows), BF16),
         pltpu.VMEM((hidden, rows), F32), pltpu.VMEM((hidden, side), BF16), pltpu.VMEM((hidden, rows), F32),
         pltpu.VMEM((total, hidden), F32)],
    )
    s_upd_parts = return_rows(s_upd)
    eo, dq, *extra = run(
        "update_edges", functools.partial(update_edges, steps), steps,
        [(et, edge_spec), (w_act, hid_spec), (dv, hid_spec), (q, edge_spec), (cot, edge_spec), r_upd, fronts, firsts, seconds],
        [(edge_sh, BF16, edge_spec), (edge_sh, BF16, edge_spec)] + [((rows + 2 * side, shard), BF16)] * mp,
        [pltpu.VMEM((side, hidden), BF16), pltpu.VMEM((side, hidden), BF16), pltpu.VMEM((side, hidden), F32),
         pltpu.VMEM((side, hidden), F32)],
    )
    edges_out = jnp.transpose(eo, (2, 0, 1))[None]
    order = extra[0]
    extra = deal(extra, "mp", mp)

    terms = run(
        "update_terms", functools.partial(update_terms, outs), 1, [r_upd, firsts, seconds] + s_upd_parts + [(order, AFTER)],
        [((rows, width + shard), BF16)] * mp,
    )
    dh2, dr, dp_ffn, gain_c, share, db_part = run(
        "node_backward", node_backward, 1, deal(terms, "mp", mp) + [h2, cot_n, gc_n, slope_f, ffn_in, ffn_out],
        [((rows, width), F32), ((rows, width), BF16), ((rows, ff), BF16), ((1, width), F32), ((rows, shard), BF16),
         ((rows, width), BF16)],
    )
    db_parts = partners(db_part, "mp", mp)

    piece = width // 4 + 48
    keep, send = run(
        "early_grads", early_grads, 1, [b, dp_ffn, y, dr, c_own, share] + extra, [((4 * piece, ff), BF16)] * 2,
    )
    got = swap(send, "dp", 1, cores)
    if near:
        early = run("early_pieces", early_pieces, 1, [keep, got], [((piece, ff), BF16)] * 4)
        order = early[0]
        (early,) = run("early_total", early_total, 1, deal(early, "graph", graph), [((piece, ff), BF16)])
        early = partners(early, "graph", graph)
    else:
        order = got
        early = lax.psum(keep.astype(F32) + got.astype(F32), "graph").astype(BF16)
        early = [early[i * piece : (i + 1) * piece] for i in range(4)]

    dh1, dt, gain_b, du, r_msg, *s_msg = run(
        "message_backward", functools.partial(message_backward, 1.0 / nbrs, steps, outs), steps,
        db_parts + [h1, dh2, gb_n, backs, (slope_m, hid_spec), idx, (order, AFTER)],
        [((rows, width), F32), ((rows, width), BF16), ((1, width), F32), (hid_sh, BF16, hid_spec),
         ((rows, hidden), BF16)] + blocks,
        [pltpu.VMEM((hidden, rows), F32), pltpu.VMEM((hidden, rows), F32), pltpu.VMEM((total, hidden), F32)],
    )
    s_msg_parts = return_rows(s_msg)
    ge, gains_edge, *mixed = run(
        "message_edges", functools.partial(message_edges, steps), steps,
        [(et, edge_spec), (du, hid_spec), (dq, edge_spec), (f, edge_spec), (cot, edge_spec), gains_e, r_msg, fronts],
        [(edge_sh, F32, edge_spec), ((8, 256), F32)] + [((rows + side, shard), BF16)] * mp,
        [pltpu.VMEM((side, hidden), BF16), pltpu.VMEM((side, hidden), F32), pltpu.VMEM((side, rows), F32),
         pltpu.VMEM((side, rows), F32)],
    )
    grad_edges = jnp.transpose(ge, (2, 0, 1))[None]
    mixed = deal(mixed, "mp", mp)

    terms = run(
        "message_terms", functools.partial(message_terms, outs), 1,
        [r_msg, fronts, backs, node, gain_b, gain_c, gains_edge] + s_msg_parts,
        [((rows + 16, width + shard), BF16)] * mp,
    )
    order = terms[0]
    terms = deal(terms, "mp", mp)
    half = (side + width) // 2
    first_rows = pl.BlockSpec((rows, shard), lambda i: (0, 0))
    share_r, keep, send = run(
        "late_grads", late_grads, 1, mixed + [(pooled, first_rows), dt, (order, AFTER)],
        [((rows, shard), BF16)] + [((half, shard), BF16)] * 2,
    )
    late = (keep.astype(F32) + swap(send, "dp", 1, cores).astype(F32)).astype(BF16)
    one = jnp.concatenate([share_r, late], axis=0)
    grad_nodes, two = run(
        "node_finish", node_finish, 1, terms + [node, dh1, ga_n],
        [((rows, width), F32), ((rows + width // 16, shard), BF16)],
    )
    if near:
        one, two = partners(one, "graph", graph), partners(two, "graph", graph)
    else:
        one, two = [one], [two]
    parts = len(one)
    (part,) = run(
        "message_grads", functools.partial(message_grads, parts), 1,
        [(a_all, pl.BlockSpec((parts * rows, width), lambda i: (0, 0)))] + one + two,
        [((2 * width + half + width // 16, shard), BF16)],
    )
    if not near:
        part = lax.psum(part, "graph")
    grad_mo, grad_ms, grad_me, grad_mout, gain_a, gain_b, gain_c, gain_ea, gain_eb = run(
        "finish_late", finish_late, 1, [part, swap(part, "dp", 1, cores)],
        [((width, shard), F32), ((width, shard), F32), ((side, shard), F32), ((shard, width), F32), ((1, width), F32),
         ((1, width), F32), ((1, width), F32), ((1, side), F32), ((1, side), F32)],
    )
    grad_in, grad_out, grad_us, grad_ue, grad_uo, grad_uout = run(
        "finish_early", functools.partial(finish_early, near), 1, early + [swap(v, "dp", 1, cores) for v in early],
        [((width, ff), F32), ((ff, width), F32), ((width, shard), F32), ((side, shard), F32), ((width, shard), F32),
         ((side, shard), F32)],
        [pltpu.VMEM((width + side, shard), F32)] * 2,
    )
    return (
        nodes_out[None],
        edges_out,
        grad_nodes[None],
        grad_edges,
        gain_a[0],
        gain_ea[0],
        grad_ms,
        grad_mo,
        grad_me,
        grad_mout,
        gain_b[0],
        grad_in,
        grad_out,
        gain_c[0],
        gain_eb[0],
        grad_us,
        grad_uo,
        grad_ue,
        grad_uout.T,
    )


def solution(mesh):
    sizes = (mesh.shape["dp"], mesh.shape["graph"], mesh.shape["mp"])
    rows = P("dp", "graph", None)
    slots = P("dp", "graph", "mp", None)
    cols, tops = P(None, "mp"), P("mp", None)
    return jax.shard_map(
        functools.partial(local, sizes),
        mesh=mesh,
        in_specs=(
            rows, slots, rows, P("dp", None), P(), P(), cols, cols, cols, tops, P(), cols, tops, P(), P(), cols, cols,
            cols, tops, rows, slots,
        ),
        out_specs=(
            rows, slots, rows, slots, P(), P(), cols, cols, cols, tops, P(), cols, tops, P(), P(), cols, cols, cols,
            tops,
        ),
        check_vma=False,
    )
```

```python
import functools

import jax
import jax.numpy as jnp
from jax import lax
from jax.experimental import pallas as pl
from jax.experimental.pallas import tpu as pltpu
from jax.sharding import PartitionSpec as P

EPSILON = 1e-05
F32 = jnp.float32
BF16 = jnp.bfloat16
GELU_A = 0.7978845608028654
GELU_B = 0.044715


def dot(left, right):
    return lax.dot_general(left, right, (((1,), (0,)), ((), ())), preferred_element_type=F32)


def dot_nt(left, right):
    return lax.dot_general(left, right, (((1,), (1,)), ((), ())), preferred_element_type=F32)


def dot_tn(left, right):
    return lax.dot_general(left, right, (((0,), (0,)), ((), ())), preferred_element_type=F32)


def normalize(values, axis=-1):
    centre = values - jnp.mean(values, axis=axis, keepdims=True)
    variance = jnp.mean(centre * centre, axis=axis, keepdims=True)
    scale_inv = lax.rsqrt(variance + EPSILON)
    return centre * scale_inv, scale_inv


def norm_back(grad_hat, normed, scale_inv, axis=-1):
    return scale_inv * (
        grad_hat
        - jnp.mean(grad_hat, axis=axis, keepdims=True)
        - normed * jnp.mean(grad_hat * normed, axis=axis, keepdims=True)
    )


def gelu_both(u):
    poly = GELU_A + (GELU_A * GELU_B) * (u * u)
    half = 0.5 + 0.5 * jnp.tanh(u * poly)
    value = u * half
    return value, half + (value * (1.0 - half)) * (6.0 * poly - 4.0 * GELU_A)


def stack(refs, lo, hi):
    return jnp.concatenate([r[:, lo:hi] for r in refs], axis=0)


def rows_of(refs):
    return refs[0][...] if len(refs) == 1 else jnp.concatenate([r[...] for r in refs], axis=0)


def sum_of(refs, lo=None, hi=None):
    parts = [r[...].astype(F32) if lo is None else r[:, lo:hi].astype(F32) for r in refs]
    while len(parts) > 1:
        parts = [sum(parts[i : i + 2]) if i + 1 < len(parts) else parts[i] for i in range(0, len(parts), 2)]
    return parts[0]


def spread(row, count):
    return jnp.concatenate([row[:, i * 128 : i * 128 + 128] for i in range(count)], axis=0)


def by_core(first, second):
    core = lax.axis_index("dp")
    pl.when(core == 0)(first)
    pl.when(core != 0)(second)


def onehot(idx, total):
    here = lax.broadcasted_iota(jnp.int32, (total, idx.shape[1]), 0)
    return (here == idx).astype(F32).astype(BF16)


CHUNK = 32
GROUP = 8


def groups(slots):
    return [range(at, min(at + GROUP, slots)) for at in range(0, slots, GROUP)]


def lanes(refs):
    return jnp.concatenate([refs[s] for s in range(refs.shape[0])], axis=1)


def edge_prep(
    graph, near, et_ref, nbr_ref, res_ref, ga_ref, gb_ref, na_ref, nb_ref, nc_ref, mix_ref, mask_ref, gains_ref, nodes_ref
):
    slots, side, rows = et_ref.shape
    total = mask_ref.shape[1]
    at_graph, at_mp = lax.axis_index("graph"), lax.axis_index("mp")
    for k in range(graph):
        block = (at_graph ^ k) if near else lax.rem(at_graph + k, graph)
        mask_ref[:, k * rows : (k + 1) * rows] = res_ref[:, pl.ds(pl.multiple_of(block * rows, rows), rows)]
    for i, ref in enumerate((na_ref, nb_ref, nc_ref)):
        nodes_ref[i : i + 1, :] = ref[...]
    for i, ref in enumerate((ga_ref, gb_ref)):
        gains_ref[i] = jnp.broadcast_to(ref[...], (rows, ref.shape[1])).T
    for s in range(slots):
        at = slice(s * rows, (s + 1) * rows)
        hat, _ = normalize(et_ref[s].astype(F32), 0)
        mix_ref[:side, at] = (hat * gains_ref[0]).astype(BF16)
        mix_ref[side + total :, at] = (hat * gains_ref[1]).astype(BF16)
        nbr = nbr_ref[at_mp * slots + s]
        if near:
            idx = ((nbr // rows) ^ at_graph) * rows + lax.rem(nbr, rows)
        else:
            moved = nbr + (total - at_graph * rows)
            idx = jnp.where(moved >= total, moved - total, moved)
        mix_ref[side : side + total, at] = onehot(idx, total)


def node_close(h1_ref, p0, p1, p2, p3, gain_ref, h2_ref, c_ref, out_ref):
    h2 = h1_ref[...] + sum_of((p0, p1, p2, p3))
    h2_ref[...] = h2
    hat, _ = normalize(h2)
    c_ref[...] = (hat * gain_ref[2:3, :]).astype(BF16)
    out_ref[...] = h2.astype(BF16)


def node_backward(
    t0, t1, t2, t3, h2_ref, cot_ref, gain_ref, slope_ref, win_ref, wout_ref,
    dh2_ref, dr_ref, dp_ref, gain_out, share_ref, part_ref,
):
    width = h2_ref.shape[1]
    dc = sum_of((t0, t1, t2, t3), 0, width)
    share_ref[...] = sum_of((t0, t1, t2, t3), width, width + 128).astype(BF16)
    hat, inv = normalize(h2_ref[...])
    gain_out[...] = jnp.sum(dc * hat, axis=0, keepdims=True)
    dh2 = cot_ref[...].astype(F32) + norm_back(dc * gain_ref[2:3, :], hat, inv)
    dh2_ref[...] = dh2
    dr = dh2.astype(BF16)
    dr_ref[...] = dr
    dp = (slope_ref[...].astype(F32) * dot_nt(dr, wout_ref[...])).astype(BF16)
    dp_ref[...] = dp
    part_ref[...] = dot_nt(dp, win_ref[...]).astype(BF16)


def pack_weights(ms, mo, me, mout, us, uo, ue, uout_t, full_ref, half_ref, later_ref):
    wide = ms.shape[0]
    size = half_ref.shape[1]

    def turned(ref):
        return ref[...].astype(F32).T.astype(BF16)

    def filled(parts):
        got = sum(p.shape[1] for p in parts)
        return jnp.concatenate(parts + [jnp.zeros((ms.shape[1], size - got), BF16)], axis=1)

    front = filled([turned(mo), turned(me), turned(ue), turned(uout_t)])
    back = filled([turned(ms), mout[...]])
    full_ref[:, :size] = front
    full_ref[:, size:] = back
    later_ref[:, :wide] = turned(us)
    later_ref[:, wide:] = turned(uo)

    def keep_front():
        half_ref[...] = front

    def keep_back():
        half_ref[...] = back

    by_core(keep_front, keep_back)


def row_prep(parts, *refs):
    node_refs, gain_ref, a_ref = refs[:parts], refs[parts], refs[parts + 1]
    total = a_ref.shape[0]
    block = node_refs[0].shape[0] if parts > 1 else 512
    for at in range(0, total, block):
        ref = node_refs[at // block] if parts > 1 else node_refs[0].at[at : at + block]
        hat, _ = normalize(ref[...].astype(F32))
        a_ref[at : at + block, :] = (hat * gain_ref[0:1, :]).astype(BF16)


def message_forward(
    nbr_scale, slots, mix_ref, mask_ref, a_ref, full_ref, cross_ref, diag_ref, cross_two_ref, diag_two_ref,
    slope_ref, pooled_ref, fronts_ref, backs_ref, lhs_ref, u_ref, ps_ref, acc_ref,
):
    total, width = a_ref.shape
    hidden, rows = ps_ref.shape
    side = (mix_ref.shape[0] - total) // 2
    shard, size = diag_ref.shape

    def place(blocks, front, back):
        for k, ref in enumerate(blocks):
            at = slice(k * shard, (k + 1) * shard)
            fronts_ref[at, :] = ref[:, :size]
            backs_ref[at, :] = ref[:, size:]
        fronts_ref[3 * shard :, :] = front[...]
        backs_ref[3 * shard :, :] = back[...]

    by_core(
        lambda: place((full_ref, cross_ref, cross_two_ref), diag_ref, diag_two_ref),
        lambda: place((full_ref, cross_two_ref, cross_ref), diag_two_ref, diag_ref),
    )
    lhs_ref[:hidden, :side] = fronts_ref[:, width : width + side]
    for at in range(0, total, 512):
        lhs_ref[:hidden, side + at : side + at + 512] = dot_nt(
            fronts_ref[:, :width], a_ref[at : at + 512, :]
        ).astype(BF16)
    top = lax.broadcasted_iota(jnp.int32, (16, total), 0) == 0
    lhs_ref[hidden:, side:] = jnp.where(top, mask_ref[...].astype(F32), 0.0).astype(BF16)
    lhs_ref[hidden:, :side] = jnp.zeros((16, side), BF16)
    ps_ref[...] = dot_nt(backs_ref[:, :width], a_ref[:rows, :])

    def product(group):
        lane = slice(group[0] * rows, (group[-1] + 1) * rows)
        u_ref[:, lane] = dot(lhs_ref[...], mix_ref[: side + total, lane])

    parts = groups(slots)
    product(parts[0])
    for i, group in enumerate(parts):
        if i + 1 < len(parts):
            product(parts[i + 1])
        for low in range(0, hidden, CHUNK):
            at = slice(low, low + CHUNK)
            ps = ps_ref[at, :]
            acc = acc_ref[at, :] if i else None
            for s in group:
                lane = slice(s * rows, (s + 1) * rows)
                z, slope = gelu_both(u_ref[at, lane] + ps)
                mask = u_ref[hidden : hidden + 1, lane]
                z = z * mask
                acc = z if acc is None else acc + z
                slope_ref[at, lane] = (slope * mask).astype(BF16)
            acc_ref[at, :] = acc
    pooled_ref[...] = (acc_ref[...] * nbr_scale).T.astype(BF16)


def node_forward(
    s0, s1, s2, s3, nodes_ref, backs_ref, gain_ref, win_ref, wout_ref, s_ref, h1_ref, b_ref, y_ref, slope_ref, part_ref
):
    width = nodes_ref.shape[1]
    sums = []
    for p in range(4):
        sums.append(sum(
            ref[:, (p ^ k) * 128 : (p ^ k) * 128 + 128].astype(F32) for k, ref in enumerate((s0, s1, s2, s3))
        ).astype(BF16))
    pooled = jnp.concatenate(sums, axis=1)
    s_ref[...] = pooled
    h1 = nodes_ref[...].astype(F32) + dot(pooled, backs_ref[:, width : 2 * width])
    h1_ref[...] = h1
    hat, _ = normalize(h1)
    b = (hat * gain_ref[1:2, :]).astype(BF16)
    b_ref[...] = b
    y, slope = gelu_both(dot(b, win_ref[...]))
    y = y.astype(BF16)
    y_ref[...] = y
    slope_ref[...] = slope.astype(BF16)
    part_ref[...] = dot(y, wout_ref[...]).astype(BF16)


def update_nodes(slots, parts, outs, mix_ref, cot_ref, fronts_ref, *rest):
    node_refs, w_refs = rest[:parts], rest[parts : parts + 4]
    w_ref, dv_ref, r_ref = rest[parts + 4 : parts + 7]
    s_refs = rest[parts + 7 : parts + 7 + outs]
    lhs_ref, v_ref, g_ref, ps_ref, racc_ref = rest[parts + 7 + outs :]
    side, rows = cot_ref.shape[1:]
    total = mix_ref.shape[0] - 2 * side
    width = node_refs[0].shape[1]
    hidden = ps_ref.shape[0]
    other = stack(w_refs, width, 2 * width)
    block = node_refs[0].shape[0] if parts > 1 else 512
    for at in range(0, total, block):
        ref = node_refs[at // block] if parts > 1 else node_refs[0].at[at : at + block]
        lhs_ref[:, at : at + block] = dot_nt(other, ref[...]).astype(BF16)
    lhs_ref[:, total:] = fronts_ref[:, width + side : width + 2 * side]
    wo = fronts_ref[:, width + 2 * side : width + 3 * side]
    ps_ref[...] = dot_nt(stack(w_refs, 0, width), node_refs[0][:rows, :])

    v_all = dot(lhs_ref[...], mix_ref[side:, :])
    g_all = dot(wo, lanes(cot_ref))
    for low in range(0, hidden, CHUNK):
        at = slice(low, low + CHUNK)
        ps = ps_ref[at, :]
        acc = None
        for s in range(slots):
            lane = slice(s * rows, (s + 1) * rows)
            w, slope = gelu_both(v_all[at, lane] + ps)
            w_ref[at, lane] = w.astype(BF16)
            dv = slope * g_all[at, lane]
            acc = dv if acc is None else acc + dv
            dv_ref[at, lane] = dv.astype(BF16)
        racc_ref[at, :] = acc
    r_ref[...] = racc_ref[...].T.astype(BF16)
    back = dot_nt(mix_ref[side : side + total, :], dv_ref[...]).astype(BF16) if total <= 512 else None
    for b, ref in enumerate(s_refs):
        n = ref.shape[0]
        for at in range(0, n, 512):
            m = min(512, n)
            low = b * n + at
            if back is not None:
                ref[at : at + m, :] = back[low : low + m]
            else:
                ref[at : at + m, :] = dot_nt(mix_ref[side + low : side + low + m, :], dv_ref[...]).astype(BF16)


def update_edges(et_ref, w_ref, dv_ref, mix_ref, cot_ref, r_ref, fronts_ref, out_ref, dq_ref, x0, x1, x2, x3):
    slots, side, rows = et_ref.shape
    width = r_ref.shape[1]
    low = mix_ref.shape[0] - side
    ue = fronts_ref[:, width + side : width + 2 * side].astype(F32).T.astype(BF16)
    uo = fronts_ref[:, width + 2 * side : width + 3 * side].astype(F32).T.astype(BF16)
    dq_ref[...] = dot(ue, dv_ref[...]).astype(BF16)
    o_all = dot(uo, w_ref[...])
    for s in range(slots):
        out_ref[s] = (et_ref[s].astype(F32) + o_all[:, s * rows : (s + 1) * rows]).astype(BF16)
    gout = dot_nt(lanes(cot_ref), w_ref[...]).astype(BF16)
    gedge = dot_nt(mix_ref[low:, :], dv_ref[...]).astype(BF16)
    for k, ref in enumerate((x0, x1, x2, x3)):
        at = slice(k * 128, k * 128 + 128)
        ref[:rows, :] = r_ref[:, at]
        ref[rows : rows + side, :] = gedge[:, at]
        ref[rows + side :, :] = gout[:, at]


def update_terms(parts, r_ref, w0, w1, w2, w3, *rest):
    s_refs, outs = rest[:parts], rest[-4:]
    width = r_ref.shape[1]
    total = sum_of(s_refs).astype(BF16)
    ws = (w0, w1, w2, w3)
    term = (dot(r_ref[...], stack(ws, 0, width)) + dot(total, stack(ws, width, 2 * width))).astype(BF16)
    for k, ref in enumerate(outs):
        ref[:, :width] = term
        ref[:, width:] = total[:, k * 128 : k * 128 + 128]


def message_shares(x0, x1, x2, x3, _, r_ref, edge_ref, *s_refs):
    rows = r_ref.shape[0]
    every = sum_of((x0, x1, x2, x3)).astype(BF16)
    n = s_refs[0].shape[0]
    for b, ref in enumerate(s_refs):
        ref[...] = every[b * n : (b + 1) * n]
    low = every.shape[0] - edge_ref.shape[0]
    r_ref[...] = every[low - rows : low]
    edge_ref[...] = every[low:]


def message_terms(parts, r_ref, fronts_ref, backs_ref, nodes_ref, gb_ref, gc_ref, ge_ref, *rest):
    s_refs, (term_ref, share_ref) = rest[:parts], rest[parts:]
    rows, shard = r_ref.shape
    width = nodes_ref.shape[1]
    total = sum_of(s_refs).astype(BF16)
    share_ref[:rows, :] = total
    share_ref[rows:, :] = r_ref[...]
    term = dot(r_ref[...], backs_ref[:shard, :width]) + dot(total, fronts_ref[:shard, :width])
    hat, _ = normalize(nodes_ref[...].astype(F32))
    gain = jnp.sum(term * hat, axis=0, keepdims=True)
    edge = jnp.concatenate([ge_ref[0:2, :], jnp.zeros((2, width - 256), F32)], axis=1)
    gains = [gain, gb_ref[...] * 0.25, gc_ref[...] * 0.25, edge, jnp.zeros((11, width), F32)]
    term_ref[...] = jnp.concatenate([term] + gains, axis=0).astype(BF16)


def early_grads(b_ref, dp_ref, y_ref, dr_ref, c_ref, share_ref, x0, x1, x2, x3, _, __, ___, keep_ref, send_ref):
    rows, width = c_ref.shape
    extra = sum_of((x0, x1, x2, x3)).astype(BF16)
    side = (extra.shape[0] - rows) // 2
    part = (width + side) // 4

    def put(ref, large, small):
        ref[:width, :] = large.astype(BF16)
        small = jnp.concatenate(small, axis=0).astype(BF16)
        ref[width : width + part, :] = jnp.concatenate([small[i * part : (i + 1) * part] for i in range(4)], axis=1)
        ref[width + part :, :] = jnp.zeros_like(ref[width + part :, :])

    def run(one, two):
        put(one, dot_tn(b_ref[...], dp_ref[...]),
            [dot_tn(c_ref[...], extra[:rows]), extra[rows : rows + side].astype(F32)])
        put(two, dot_tn(y_ref[...], dr_ref[...]),
            [dot_tn(c_ref[...], share_ref[...]), extra[rows + side :].astype(F32)])

    by_core(lambda: run(keep_ref, send_ref), lambda: run(send_ref, keep_ref))


def split(total, bit, stay_ref, go_ref):
    half = stay_ref.shape[0]
    own = (lax.axis_index("graph") // bit) % 2

    @pl.when(own == 0)
    def _():
        stay_ref[...] = total[:half]
        go_ref[...] = total[half:]

    @pl.when(own != 0)
    def _():
        stay_ref[...] = total[half:]
        go_ref[...] = total[:half]


def sum_split(bit, one_ref, two_ref, *rest):
    stay_ref, go_ref = rest[-2:]
    split((one_ref[...].astype(F32) + two_ref[...].astype(F32)).astype(BF16), bit, stay_ref, go_ref)


def sum_two(one_ref, two_ref, _, out_ref):
    out_ref[...] = (one_ref[...].astype(F32) + two_ref[...].astype(F32)).astype(BF16)


def join(bit, one, two):
    own = (lax.axis_index("graph") // bit) % 2
    return jnp.where(own == 0, one, two), jnp.where(own == 0, two, one)


def join_two(bit, one_ref, two_ref, _, out_ref):
    half = one_ref.shape[0]
    first, second = join(bit, one_ref[...], two_ref[...])
    out_ref[:half, :] = first
    out_ref[half:, :] = second


def finish_early(bit, m0, m1, t0, t1, gin_ref, gout_ref, self_ref, edge_ref, other_ref, out_ref):
    width, side = gin_ref.shape[0], edge_ref.shape[0]
    part = (width + side) // 4

    def run(one, two):
        for pair, large, top, low in ((one, gin_ref, self_ref, edge_ref), (two, gout_ref, other_ref, out_ref)):
            pair = [r[...] for r in pair]
            if bit:
                clear, full = join(bit, *pair)
                quarter = clear.shape[0] // 2
                pair = [clear[:quarter], full[:quarter], clear[quarter:], full[quarter:]]
            every = jnp.concatenate(pair, axis=0).astype(F32)
            large[...] = every[:width]
            small = jnp.concatenate([every[width : width + part, i * 128 : i * 128 + 128] for i in range(4)], axis=0)
            top[...] = small[:width]
            low[...] = small[width:]

    by_core(lambda: run((m0, m1), (t0, t1)), lambda: run((t0, t1), (m0, m1)))


def message_backward(
    nbr_scale, slots, t0, t1, t2, t3, h1_ref, dh2_ref, gain_ref, backs_ref, slope_ref, mix_ref,
    dh1_ref, dt_ref, gain_out, du_ref, x0, x1, x2, x3, g_ref, racc_ref,
):
    hidden, rows = g_ref.shape
    width = h1_ref.shape[1]
    side = mix_ref.shape[0] - x0.shape[0] + rows
    total = x0.shape[0] - rows - side
    db = sum_of((t0, t1, t2, t3))
    hat, inv = normalize(h1_ref[...])
    gain_out[...] = jnp.sum(db * hat, axis=0, keepdims=True)
    dh1 = dh2_ref[...] + norm_back(db * gain_ref[1:2, :], hat, inv)
    dh1_ref[...] = dh1
    dt = dh1.astype(BF16)
    dt_ref[...] = dt
    g_ref[...] = dot_nt(backs_ref[:, width : 2 * width], dt) * nbr_scale
    for low in range(0, hidden, CHUNK):
        at = slice(low, low + CHUNK)
        g = g_ref[at, :]
        acc = None
        for s in range(slots):
            lane = slice(s * rows, (s + 1) * rows)
            du = slope_ref[at, lane].astype(F32) * g
            acc = du if acc is None else acc + du
            du_ref[at, lane] = du.astype(BF16)
        racc_ref[at, :] = acc
    for low in range(0, total, 512):
        back = dot_nt(mix_ref[side + low : side + low + 512, :], du_ref[...]).astype(BF16)
        for k, ref in enumerate((x0, x1, x2, x3)):
            ref[low : low + 512, :] = back[:, k * 128 : k * 128 + 128]
    gedge = dot_nt(mix_ref[:side, :], du_ref[...]).astype(BF16)
    for k, ref in enumerate((x0, x1, x2, x3)):
        ref[total : total + rows, :] = racc_ref[k * 128 : k * 128 + 128, :].T.astype(BF16)
        ref[total + rows :, :] = gedge[:, k * 128 : k * 128 + 128]


def message_edges(
    et_ref, du_ref, dq_ref, cot_ref, gains_ref, fronts_ref, out_ref, ge_ref, ga_ref, gb_ref
):
    slots, side, rows = et_ref.shape
    width = fronts_ref.shape[0]
    we = fronts_ref[:, width : width + side].astype(F32).T.astype(BF16)
    df_all = dot(we, du_ref[...])
    ga_ref[...] = jnp.zeros_like(ga_ref)
    gb_ref[...] = jnp.zeros_like(gb_ref)
    for s in range(slots):
        df = df_all[:, s * rows : (s + 1) * rows]
        dq = dq_ref[:, s * rows : (s + 1) * rows].astype(F32)
        hat, inv = normalize(et_ref[s].astype(F32), 0)
        ga_ref[...] += df * hat
        gb_ref[...] += dq * hat
        out_ref[s] = cot_ref[s].astype(F32) + norm_back(gains_ref[0] * df + gains_ref[1] * dq, hat, inv, 0)
    lane = lax.broadcasted_iota(jnp.int32, (side, 256), 1)
    row = lax.broadcasted_iota(jnp.int32, (side, 256), 0)

    def laid(ref):
        column = jnp.sum(ref[...], axis=1, keepdims=True)
        return jnp.sum(jnp.where(row == lane, column, 0.0), axis=0, keepdims=True)

    ge_ref[...] = jnp.concatenate([laid(ga_ref), laid(gb_ref), jnp.zeros((6, 256), F32)], axis=0)


def late_grads(edge_ref, s_ref, dt_ref, keep_ref, send_ref):
    rows, width = dt_ref.shape
    gout = dot_tn(s_ref[...], dt_ref[...])
    pieces = [edge_ref[...].astype(F32)] + [gout[:, i * 128 : i * 128 + 128] for i in range(width // 128)]
    every = jnp.concatenate(pieces, axis=0).astype(BF16)
    half = keep_ref.shape[0]

    def put(one, two):
        one[...] = every[:half]
        two[...] = every[half:]

    by_core(lambda: put(keep_ref, send_ref), lambda: put(send_ref, keep_ref))


def node_finish(t0, t1, t2, t3, nodes_ref, dh1_ref, gain_ref, keep_ref, got_ref, out_ref, late_ref):
    rows, width = dh1_ref.shape
    half = keep_ref.shape[0]
    every = sum_of((t0, t1, t2, t3))
    hat, inv = normalize(nodes_ref[...].astype(F32))
    out_ref[...] = dh1_ref[...] + norm_back(every[:rows] * gain_ref[0:1, :], hat, inv)
    late_ref[:half, :] = (keep_ref[...].astype(F32) + got_ref[...].astype(F32)).astype(BF16)
    late_ref[half:, :] = jnp.concatenate(
        [every[rows : rows + 8, i * 128 : i * 128 + 128] for i in range(width // 128)], axis=0
    ).astype(BF16)


def message_grads(parts, a_ref, *rest):
    shares, lates, out_ref = rest[:parts], rest[parts : 2 * parts], rest[-1]
    rows = a_ref.shape[0] // parts
    width = a_ref.shape[1]
    both = jnp.concatenate(
        [jnp.concatenate([r[:rows, :], r[rows:, :]], axis=1) for r in shares], axis=0
    )
    grad = dot_tn(a_ref[...], both).astype(BF16)
    out_ref[:width, :] = grad[:, :128]
    out_ref[width : 2 * width, :] = grad[:, 128:]
    out_ref[2 * width :, :] = sum(r[...].astype(F32) for r in lates).astype(BF16)


def finish_late(
    mine_ref, theirs_ref, other_ref, self_ref, edge_ref, out_ref, ga_ref, gb_ref, gc_ref, gea_ref, geb_ref
):
    width, side = other_ref.shape[0], edge_ref.shape[0]
    rows = out_ref.shape[0]
    other_ref[...] = mine_ref[:width, :].astype(F32) + theirs_ref[:width, :].astype(F32)
    self_ref[...] = mine_ref[width : 2 * width, :].astype(F32) + theirs_ref[width : 2 * width, :].astype(F32)
    low = mine_ref.shape[0] - 8 * (width // 128)
    gains = mine_ref[low:, :].astype(F32) + theirs_ref[low:, :].astype(F32)
    for i, ref in enumerate((ga_ref, gb_ref, gc_ref)):
        ref[...] = jnp.concatenate([gains[8 * j + i : 8 * j + i + 1] for j in range(width // 128)], axis=1)
    for i, ref in ((3, gea_ref), (4, geb_ref)):
        ref[...] = jnp.concatenate([gains[i : i + 1], gains[8 + i : 9 + i]], axis=1)[:, :side]

    def run(first, second):
        every = jnp.concatenate([first[2 * width : low, :], second[2 * width : low, :]], axis=0).astype(F32)
        edge_ref[...] = every[:side]
        out_ref[...] = jnp.concatenate(
            [every[side + i * rows : side + (i + 1) * rows] for i in range(width // 128)], axis=1
        )

    by_core(lambda: run(mine_ref, theirs_ref), lambda: run(theirs_ref, mine_ref))


def whole(shape):
    zeros = (0,) * len(shape)
    return pl.BlockSpec(tuple(shape), lambda i: zeros)


def in_bytes(shape, dtype):
    n = jnp.dtype(dtype).itemsize
    for d in shape:
        n *= d
    return n


AFTER = pl.BlockSpec(memory_space=pl.ANY)


def call(name, body, grid, ins, outs, scratch=(), vmem=24, heavy=False):
    ins = [a if isinstance(a, tuple) else (a, whole(a.shape)) for a in ins]
    outs = [o if len(o) == 3 else o + (whole(o[0]),) for o in outs]
    moved = sum(in_bytes(a.shape, a.dtype) for a, _ in ins) + sum(in_bytes(sh, t) for sh, t, _ in outs)
    return pl.pallas_call(
        body,
        grid=(grid,),
        in_specs=[s for _, s in ins],
        out_specs=[s for _, _, s in outs],
        out_shape=[jax.ShapeDtypeStruct(sh, t) for sh, t, _ in outs],
        scratch_shapes=list(scratch),
        compiler_params=pltpu.CompilerParams(vmem_limit_bytes=vmem << 20, dimension_semantics=("arbitrary",)),
        cost_estimate=pl.CostEstimate(flops=2 * 10**10 if heavy else 0, bytes_accessed=moved, transcendentals=0),
        name=name,
    )(*[a for a, _ in ins])


def far_in(values):
    return pltpu.with_memory_space_constraint(values, pltpu.HBM)


def swap(values, axis, bits, size):
    return lax.ppermute(values, axis, [(i, i ^ bits) for i in range(size)])


def partners(values, axis, size):
    return [values] + [swap(values, axis, k, size) for k in range(1, size)]


def deal(pieces, axis, size):
    return [pieces[0]] + [swap(pieces[k], axis, k, size) for k in range(1, size)]


def turn(values, start, axis):
    return lax.dynamic_slice_in_dim(
        jnp.concatenate([values, values], axis=axis), start, values.shape[axis], axis=axis
    )


def after(values, *others):
    return lax.optimization_barrier((values,) + others)[0]


def local(sizes, *args):
    (
        nodes, edges, neighbours, resmask, node_gain_a, edge_gain_a, message_self, message_other, message_edge,
        message_out, node_gain_b, ffn_in, ffn_out, node_gain_c, edge_gain_b, update_self, update_other, update_edge,
        update_out, node_cot, edge_cot,
    ) = args
    cores, graph, mp = sizes
    near = graph <= 4
    at_graph = None if near else lax.axis_index("graph")
    _, rows, width = nodes.shape
    slots, side = edges.shape[2:]
    nbrs = neighbours.shape[2]
    total = resmask.shape[1]
    shard = message_self.shape[1]
    hidden = shard * mp
    ff = ffn_in.shape[1]
    vmem = 20 if total <= 1024 else 60
    run = functools.partial(call, vmem=vmem)

    def gather_rows(values):
        if near:
            return partners(values, "graph", graph)
        return [turn(lax.all_gather(values, "graph", axis=0, tiled=True), at_graph * rows, 0)]

    def return_rows(blocks):
        if near:
            return deal(blocks, "graph", graph)
        placed = turn(blocks[0], total - at_graph * rows, 0)
        return [lax.psum_scatter(placed, "graph", scatter_dimension=0, tiled=True)]

    blocks = [((rows, hidden), BF16)] * graph if near else [((total, hidden), BF16)]
    outs = len(blocks)
    node, cot_n = nodes[0], node_cot[0]

    nodes_all = gather_rows(node)
    et = jnp.transpose(edges[0], (1, 2, 0))
    cot = jnp.transpose(edge_cot[0], (1, 2, 0))
    edge_sh, hid_sh = (slots, side, rows), (hidden, slots * rows)

    mix, mask_row, gains_e, gains_n = run(
        "edge_prep", functools.partial(edge_prep, graph, near), 1,
        [
            far_in(v) for v in (
                et, jnp.transpose(neighbours, (2, 0, 1)), resmask, edge_gain_a[None, :], edge_gain_b[None, :],
                node_gain_a[None, :], node_gain_b[None, :], node_gain_c[None, :],
            )
        ],
        [((2 * side + total, slots * rows), BF16), ((1, total), jnp.int32), ((2, side, rows), F32), ((8, width), F32)],
    )
    full, half, later = run(
        "pack_weights", pack_weights, 1,
        [far_in(w) for w in (
            message_self, message_other, message_edge, message_out, update_self, update_other, update_edge, update_out.T
        )],
        [((shard, 2 * width + 2 * 640), BF16), ((shard, width + 640), BF16), ((shard, 2 * width), BF16)],
    )
    cross = lax.ppermute(full, ("dp", "mp"), [(c * mp + m, c * mp + (m ^ (1 + c))) for c in range(2) for m in range(mp)])
    diag = swap(half, "mp", 3, mp)
    (a_all,) = run(
        "row_prep", functools.partial(row_prep, len(nodes_all)), 1, nodes_all + [gains_n], [((total, width), BF16)],
    )
    cross, diag = after(cross, a_all), after(diag, a_all)
    slope_m, pooled_part, fronts, backs = run(
        "message_forward", functools.partial(message_forward, 1.0 / nbrs, slots), 1,
        [mix, mask_row, a_all, full, cross, diag, swap(cross, "dp", 1, cores), swap(diag, "dp", 1, cores)],
        [(hid_sh, BF16), ((rows, hidden), BF16), ((hidden, width + 640), BF16), ((hidden, width + 640), BF16)],
        [pltpu.VMEM((hidden + 16, total + side), BF16), pltpu.VMEM((hidden + 16, slots * rows), F32),
         pltpu.VMEM((hidden, rows), F32), pltpu.VMEM((hidden, rows), F32)], heavy=True,
    )

    pooled, h1, b, y, slope_f, h2_part = run(
        "node_forward", node_forward, 1,
        partners(pooled_part, "mp", mp) + [node, backs, gains_n, ffn_in, ffn_out],
        [((rows, hidden), BF16), ((rows, width), F32), ((rows, width), BF16), ((rows, ff), BF16), ((rows, ff), BF16),
         ((rows, width), BF16)],
    )
    h2, c_own, nodes_out = run(
        "node_close", node_close, 1, [h1] + partners(h2_part, "mp", mp) + [gains_n],
        [((rows, width), F32), ((rows, width), BF16), ((rows, width), BF16)],
    )
    c_all = gather_rows(c_own)

    wl = partners(after(later, c_own), "mp", mp)
    w_act, dv, r_upd, *s_upd = run(
        "update_nodes", functools.partial(update_nodes, slots, len(c_all), outs), 1,
        [mix, cot, fronts] + c_all + wl,
        [(hid_sh, BF16), (hid_sh, BF16), ((rows, hidden), BF16)] + blocks,
        [pltpu.VMEM((hidden, total + side), BF16), pltpu.VMEM(hid_sh, F32), pltpu.VMEM(hid_sh, F32),
         pltpu.VMEM((hidden, rows), F32), pltpu.VMEM((hidden, rows), F32)], heavy=True,
    )
    s_upd_parts = return_rows(s_upd)
    eo, dq, *extra = run(
        "update_edges", update_edges, 1, [et, w_act, dv, mix, cot, r_upd, fronts],
        [(edge_sh, BF16), ((side, slots * rows), BF16)] + [((rows + 2 * side, shard), BF16)] * mp,
    )
    edges_out = jnp.transpose(eo, (2, 0, 1))[None]
    order = extra[0]
    extra = deal(extra, "mp", mp)

    terms = run(
        "update_terms", functools.partial(update_terms, outs), 1, [r_upd] + wl + s_upd_parts + [(order, AFTER)],
        [((rows, width + shard), BF16)] * mp,
    )
    dh2, dr, dp_ffn, gain_c, share, db_part = run(
        "node_backward", node_backward, 1, deal(terms, "mp", mp) + [h2, cot_n, gains_n, slope_f, ffn_in, ffn_out],
        [((rows, width), F32), ((rows, width), BF16), ((rows, ff), BF16), ((1, width), F32), ((rows, shard), BF16),
         ((rows, width), BF16)],
    )
    db_parts = partners(db_part, "mp", mp)

    size = (width + (width + side) // 4 + 63) // 64 * 64
    keep, send = run(
        "early_grads", early_grads, 1, [b, dp_ffn, y, dr, c_own, share] + extra + [(v, AFTER) for v in db_parts[1:]], [((size, ff), BF16)] * 2,
    )
    got = swap(send, "dp", 1, cores)
    halves, quarters = [((size // 2, ff), BF16)], [((size // 4, ff), BF16)]

    dh1, dt, gain_b, du, *shares = run(
        "message_backward", functools.partial(message_backward, 1.0 / nbrs, slots), 1,
        db_parts + [h1, dh2, gains_n, backs, slope_m, mix],
        [((rows, width), F32), ((rows, width), BF16), ((1, width), F32), (hid_sh, BF16)]
        + [((total + rows + side, shard), BF16)] * mp,
        [pltpu.VMEM((hidden, rows), F32), pltpu.VMEM((hidden, rows), F32)], heavy=True,
    )
    if near:
        stay, go = run("early_one", functools.partial(sum_split, 2), 1, [keep, got, (gain_b, AFTER)], halves * 2)
        go = swap(go, "graph", 2, graph)
    shares = deal(shares, "mp", mp)
    ge, gains_edge = run(
        "message_edges", message_edges, 1, [et, du, dq, cot, gains_e, fronts], [(edge_sh, F32), ((8, 256), F32)],
        [pltpu.VMEM((side, rows), F32), pltpu.VMEM((side, rows), F32)],
    )
    grad_edges = jnp.transpose(ge, (2, 0, 1))[None]

    share_r, grad_edge, *share_s = run(
        "message_shares", message_shares, 1, shares + [(gains_edge, AFTER)],
        [((rows, shard), BF16), ((side, shard), BF16)] + [(sh[:1] + (shard,), t) for sh, t in blocks],
    )
    if near:
        stay, go = run("early_two", functools.partial(sum_split, 1), 1, [stay, go, (share_r, AFTER)], quarters * 2)
        go = swap(go, "graph", 1, graph)
    term, share = run(
        "message_terms", functools.partial(message_terms, outs), 1,
        [share_r, fronts, backs, node, gain_b, gain_c, gains_edge] + return_rows(share_s),
        [((rows + 16, width), BF16), ((2 * rows, shard), BF16)],
    )
    if near:
        (own,) = run("early_three", sum_two, 1, [stay, go, (term, AFTER)], quarters)
        go = swap(own, "graph", 2, graph)
    half = (side + width) // 2
    keep_late, send_late = run(
        "late_grads", late_grads, 1,
        [grad_edge, (pooled, pl.BlockSpec((rows, shard), lambda i: (0, 0))), dt], [((half, shard), BF16)] * 2,
    )
    grad_nodes, late = run(
        "node_finish", node_finish, 1,
        partners(term, "mp", mp) + [node, dh1, gains_n, keep_late, swap(send_late, "dp", 1, cores)],
        [((rows, width), F32), ((half + width // 16, shard), BF16)],
    )
    if near:
        (own,) = run("early_four", functools.partial(join_two, 2), 1, [own, go, (late, AFTER)], halves)
        early_sum = [own, swap(own, "graph", 1, graph)]
        share, late = partners(share, "graph", graph), partners(late, "graph", graph)
    else:
        early = lax.psum(keep.astype(F32) + got.astype(F32), "graph").astype(BF16)
        early_sum = [early[: size // 2], early[size // 2 :]]
        share, late = [share], [late]
    parts = len(share)
    (part,) = run(
        "message_grads", functools.partial(message_grads, parts), 1,
        [(a_all, pl.BlockSpec((parts * rows, width), lambda i: (0, 0)))] + share + late,
        [((2 * width + half + width // 16, shard), BF16)],
    )
    if not near:
        part = lax.psum(part, "graph")
    grad_mo, grad_ms, grad_me, grad_mout, gain_a, gain_b, gain_c, gain_ea, gain_eb = run(
        "finish_late", finish_late, 1, [part, swap(part, "dp", 1, cores)],
        [((width, shard), F32), ((width, shard), F32), ((side, shard), F32), ((shard, width), F32), ((1, width), F32),
         ((1, width), F32), ((1, width), F32), ((1, side), F32), ((1, side), F32)],
    )
    grad_in, grad_out, grad_us, grad_ue, grad_uo, grad_uout = run(
        "finish_early", functools.partial(finish_early, 1 if near else 0), 1, early_sum + [swap(v, "dp", 1, cores) for v in early_sum],
        [((width, ff), F32), ((ff, width), F32), ((width, shard), F32), ((side, shard), F32), ((width, shard), F32),
         ((side, shard), F32)],
    )
    return (
        nodes_out[None],
        edges_out,
        grad_nodes[None],
        grad_edges,
        gain_a[0],
        gain_ea[0],
        grad_ms,
        grad_mo,
        grad_me,
        grad_mout,
        gain_b[0],
        grad_in,
        grad_out,
        gain_c[0],
        gain_eb[0],
        grad_us,
        grad_uo,
        grad_ue,
        grad_uout.T,
    )


def solution(mesh):
    sizes = (mesh.shape["dp"], mesh.shape["graph"], mesh.shape["mp"])
    rows = P("dp", "graph", None)
    slots = P("dp", "graph", "mp", None)
    cols, tops = P(None, "mp"), P("mp", None)
    return jax.shard_map(
        functools.partial(local, sizes),
        mesh=mesh,
        in_specs=(
            rows, slots, rows, P("dp", None), P(), P(), cols, cols, cols, tops, P(), cols, tops, P(), P(), cols, cols,
            cols, tops, rows, slots,
        ),
        out_specs=(
            rows, slots, rows, slots, P(), P(), cols, cols, cols, tops, P(), cols, tops, P(), P(), cols, cols, cols,
            tops,
        ),
        check_vma=False,
    )
```

```python
import functools

import jax
import jax.numpy as jnp
from jax import lax
from jax.experimental import pallas as pl
from jax.experimental.pallas import tpu as pltpu
from jax.sharding import PartitionSpec as P

EPSILON = 1e-05
F32 = jnp.float32
BF16 = jnp.bfloat16
GELU_A = 0.7978845608028654
GELU_B = 0.044715


def dot(left, right):
    return lax.dot_general(left, right, (((1,), (0,)), ((), ())), preferred_element_type=F32)


def dot_nt(left, right):
    return lax.dot_general(left, right, (((1,), (1,)), ((), ())), preferred_element_type=F32)


def dot_tn(left, right):
    return lax.dot_general(left, right, (((0,), (0,)), ((), ())), preferred_element_type=F32)


def normalize(values, axis=-1):
    centre = values - jnp.mean(values, axis=axis, keepdims=True)
    variance = jnp.mean(centre * centre, axis=axis, keepdims=True)
    scale_inv = lax.rsqrt(variance + EPSILON)
    return centre * scale_inv, scale_inv


def norm_back(grad_hat, normed, scale_inv, axis=-1):
    return scale_inv * (
        grad_hat
        - jnp.mean(grad_hat, axis=axis, keepdims=True)
        - normed * jnp.mean(grad_hat * normed, axis=axis, keepdims=True)
    )


def gelu_both(u):
    poly = GELU_A + (GELU_A * GELU_B) * (u * u)
    half = 0.5 + 0.5 * jnp.tanh(u * poly)
    value = u * half
    return value, half + (value * (1.0 - half)) * (6.0 * poly - 4.0 * GELU_A)


def stack(refs, lo, hi):
    return jnp.concatenate([r[:, lo:hi] for r in refs], axis=0)


def rows_of(refs):
    return refs[0][...] if len(refs) == 1 else jnp.concatenate([r[...] for r in refs], axis=0)


def sum_of(refs, lo=None, hi=None):
    parts = [r[...].astype(F32) if lo is None else r[:, lo:hi].astype(F32) for r in refs]
    while len(parts) > 1:
        parts = [sum(parts[i : i + 2]) if i + 1 < len(parts) else parts[i] for i in range(0, len(parts), 2)]
    return parts[0]


def spread(row, count):
    return jnp.concatenate([row[:, i * 128 : i * 128 + 128] for i in range(count)], axis=0)


def by_core(first, second):
    core = lax.axis_index("dp")
    pl.when(core == 0)(first)
    pl.when(core != 0)(second)


def onehot(idx, total):
    here = lax.broadcasted_iota(jnp.int32, (total, idx.shape[1]), 0)
    return (here == idx).astype(F32).astype(BF16)


CHUNK = 32
GROUP = 8


def groups(slots):
    return [range(at, min(at + GROUP, slots)) for at in range(0, slots, GROUP)]


def lanes(refs):
    return jnp.concatenate([refs[s] for s in range(refs.shape[0])], axis=1)


def edge_prep(
    graph, near, et_ref, nbr_ref, res_ref, ga_ref, gb_ref, na_ref, nb_ref, nc_ref, node_ref,
    mix_ref, mask_ref, gains_ref, nodes_ref, own_ref,
):
    slots, side, rows = et_ref.shape
    total = mask_ref.shape[1]
    at_graph, at_mp = lax.axis_index("graph"), lax.axis_index("mp")
    for k in range(graph):
        block = (at_graph ^ k) if near else lax.rem(at_graph + k, graph)
        mask_ref[:, k * rows : (k + 1) * rows] = res_ref[:, pl.ds(pl.multiple_of(block * rows, rows), rows)]
    for i, ref in enumerate((na_ref, nb_ref, nc_ref)):
        nodes_ref[i : i + 1, :] = ref[...]
    hat, _ = normalize(node_ref[...].astype(F32))
    own_ref[...] = (hat * na_ref[...]).astype(BF16)
    for i, ref in enumerate((ga_ref, gb_ref)):
        gains_ref[i] = jnp.broadcast_to(ref[...], (rows, ref.shape[1])).T
    for s in range(slots):
        at = slice(s * rows, (s + 1) * rows)
        hat, _ = normalize(et_ref[s].astype(F32), 0)
        mix_ref[:side, at] = (hat * gains_ref[0]).astype(BF16)
        mix_ref[side + total :, at] = (hat * gains_ref[1]).astype(BF16)
        nbr = nbr_ref[at_mp * slots + s]
        if near:
            idx = ((nbr // rows) ^ at_graph) * rows + lax.rem(nbr, rows)
        else:
            moved = nbr + (total - at_graph * rows)
            idx = jnp.where(moved >= total, moved - total, moved)
        mix_ref[side : side + total, at] = onehot(idx, total)


def node_close(h1_ref, p0, p1, p2, p3, gain_ref, h2_ref, c_ref, out_ref):
    h2 = h1_ref[...] + sum_of((p0, p1, p2, p3))
    h2_ref[...] = h2
    hat, _ = normalize(h2)
    c_ref[...] = (hat * gain_ref[2:3, :]).astype(BF16)
    out_ref[...] = h2.astype(BF16)


def node_backward(
    t0, t1, t2, t3, h2_ref, cot_ref, gain_ref, slope_ref, win_ref, wout_ref,
    dh2_ref, dr_ref, dp_ref, gain_out, share_ref, part_ref,
):
    width = h2_ref.shape[1]
    dc = sum_of((t0, t1, t2, t3), 0, width)
    share_ref[...] = sum_of((t0, t1, t2, t3), width, width + 128).astype(BF16)
    hat, inv = normalize(h2_ref[...])
    gain_out[...] = jnp.sum(dc * hat, axis=0, keepdims=True)
    dh2 = cot_ref[...].astype(F32) + norm_back(dc * gain_ref[2:3, :], hat, inv)
    dh2_ref[...] = dh2
    dr = dh2.astype(BF16)
    dr_ref[...] = dr
    dp = (slope_ref[...].astype(F32) * dot_nt(dr, wout_ref[...])).astype(BF16)
    dp_ref[...] = dp
    part_ref[...] = dot_nt(dp, win_ref[...]).astype(BF16)


def pack_weights(ms, mo, me, mout, us, uo, ue, uout_t, full_ref, half_ref, later_ref, later_half_ref):
    wide = ms.shape[0]
    size = half_ref.shape[1]

    def turned(ref):
        return ref[...].astype(F32).T.astype(BF16)

    def filled(parts):
        got = sum(p.shape[1] for p in parts)
        return jnp.concatenate(parts + [jnp.zeros((ms.shape[1], size - got), BF16)], axis=1)

    front = filled([turned(mo), turned(me), turned(ue), turned(uout_t)])
    back = filled([turned(ms), mout[...]])
    full_ref[:, :size] = front
    full_ref[:, size:] = back
    later_ref[:, :wide] = turned(us)
    later_ref[:, wide:] = turned(uo)

    def keep_front():
        half_ref[...] = front
        later_half_ref[...] = later_ref[:, :wide]

    def keep_back():
        half_ref[...] = back
        later_half_ref[...] = later_ref[:, wide:]

    by_core(keep_front, keep_back)


def row_prep(parts, *refs):
    node_refs, gain_ref, a_ref = refs[:parts], refs[parts], refs[parts + 1]
    total = a_ref.shape[0]
    block = node_refs[0].shape[0] if parts > 1 else 512
    for at in range(0, total, block):
        ref = node_refs[at // block] if parts > 1 else node_refs[0].at[at : at + block]
        if parts > 1 and at == 0:
            a_ref[:block, :] = ref[...]
        else:
            hat, _ = normalize(ref[...].astype(F32))
            a_ref[at : at + block, :] = (hat * gain_ref[0:1, :]).astype(BF16)


def message_forward(
    nbr_scale, slots, mix_ref, mask_ref, a_ref, full_ref, cross_ref, diag_ref, cross_two_ref, diag_two_ref,
    slope_ref, pooled_ref, fronts_ref, backs_ref, lhs_ref, u_ref, ps_ref, acc_ref,
):
    total, width = a_ref.shape
    hidden, rows = ps_ref.shape
    side = (mix_ref.shape[0] - total) // 2
    shard, size = diag_ref.shape

    def place(blocks, front, back):
        for k, ref in enumerate(blocks):
            at = slice(k * shard, (k + 1) * shard)
            fronts_ref[at, :] = ref[:, :size]
            backs_ref[at, :] = ref[:, size:]
        fronts_ref[3 * shard :, :] = front[...]
        backs_ref[3 * shard :, :] = back[...]

    by_core(
        lambda: place((full_ref, cross_ref, cross_two_ref), diag_ref, diag_two_ref),
        lambda: place((full_ref, cross_two_ref, cross_ref), diag_two_ref, diag_ref),
    )
    lhs_ref[:hidden, :side] = fronts_ref[:, width : width + side]
    for at in range(0, total, 512):
        lhs_ref[:hidden, side + at : side + at + 512] = dot_nt(
            fronts_ref[:, :width], a_ref[at : at + 512, :]
        ).astype(BF16)
    top = lax.broadcasted_iota(jnp.int32, (16, total), 0) == 0
    lhs_ref[hidden:, side:] = jnp.where(top, mask_ref[...].astype(F32), 0.0).astype(BF16)
    lhs_ref[hidden:, :side] = jnp.zeros((16, side), BF16)
    ps_ref[...] = dot_nt(backs_ref[:, :width], a_ref[:rows, :])

    def product(group):
        lane = slice(group[0] * rows, (group[-1] + 1) * rows)
        u_ref[:, lane] = dot(lhs_ref[...], mix_ref[: side + total, lane])

    parts = groups(slots)
    product(parts[0])
    for i, group in enumerate(parts):
        if i + 1 < len(parts):
            product(parts[i + 1])
        for low in range(0, hidden, CHUNK):
            at = slice(low, low + CHUNK)
            ps = ps_ref[at, :]
            acc = acc_ref[at, :] if i else None
            for s in group:
                lane = slice(s * rows, (s + 1) * rows)
                z, slope = gelu_both(u_ref[at, lane] + ps)
                mask = u_ref[hidden : hidden + 1, lane]
                z = z * mask
                acc = z if acc is None else acc + z
                slope_ref[at, lane] = (slope * mask).astype(BF16)
            acc_ref[at, :] = acc
    pooled_ref[...] = (acc_ref[...] * nbr_scale).T.astype(BF16)


def node_forward(
    s0, s1, s2, s3, nodes_ref, backs_ref, gain_ref, win_ref, wout_ref, _, __,
    s_ref, h1_ref, b_ref, y_ref, slope_ref, part_ref
):
    width = nodes_ref.shape[1]
    sums = []
    for p in range(4):
        sums.append(sum(
            ref[:, (p ^ k) * 128 : (p ^ k) * 128 + 128].astype(F32) for k, ref in enumerate((s0, s1, s2, s3))
        ).astype(BF16))
    pooled = jnp.concatenate(sums, axis=1)
    s_ref[...] = pooled
    h1 = nodes_ref[...].astype(F32) + dot(pooled, backs_ref[:, width : 2 * width])
    h1_ref[...] = h1
    hat, _ = normalize(h1)
    b = (hat * gain_ref[1:2, :]).astype(BF16)
    b_ref[...] = b
    y, slope = gelu_both(dot(b, win_ref[...]))
    y = y.astype(BF16)
    y_ref[...] = y
    slope_ref[...] = slope.astype(BF16)
    part_ref[...] = dot(y, wout_ref[...]).astype(BF16)


def update_nodes(slots, parts, outs, mix_ref, cot_ref, fronts_ref, *rest):
    node_refs = rest[:parts]
    own_ref, cross_ref, diag_ref, cross_two_ref, diag_two_ref, w_ref, dv_ref, r_ref, laters_ref = rest[parts : parts + 9]
    s_refs = rest[parts + 9 : parts + 9 + outs]
    lhs_ref, v_ref, g_ref, ps_ref, racc_ref = rest[parts + 9 + outs :]
    side, rows = cot_ref.shape[1:]
    total = mix_ref.shape[0] - 2 * side
    width = node_refs[0].shape[1]
    hidden = ps_ref.shape[0]
    shard = own_ref.shape[0]

    def place(blocks, own, other):
        for k, ref in enumerate(blocks):
            laters_ref[k * shard : (k + 1) * shard, :] = ref[...]
        laters_ref[3 * shard :, :width] = own[...]
        laters_ref[3 * shard :, width:] = other[...]

    by_core(
        lambda: place((own_ref, cross_ref, cross_two_ref), diag_ref, diag_two_ref),
        lambda: place((own_ref, cross_two_ref, cross_ref), diag_two_ref, diag_ref),
    )
    other = laters_ref[:, width:]
    if parts > 1:
        lhs_ref[:, :total] = dot_nt(other, rows_of(node_refs)).astype(BF16)
    else:
        for at in range(0, total, 512):
            lhs_ref[:, at : at + 512] = dot_nt(other, node_refs[0][at : at + 512, :]).astype(BF16)
    lhs_ref[:, total:] = fronts_ref[:, width + side : width + 2 * side]
    wo = fronts_ref[:, width + 2 * side : width + 3 * side]
    ps_ref[...] = dot_nt(laters_ref[:, :width], node_refs[0][:rows, :])

    v_all = dot(lhs_ref[...], mix_ref[side:, :])
    g_all = dot(wo, lanes(cot_ref))
    for low in range(0, hidden, CHUNK):
        at = slice(low, low + CHUNK)
        ps = ps_ref[at, :]
        acc = None
        for s in range(slots):
            lane = slice(s * rows, (s + 1) * rows)
            w, slope = gelu_both(v_all[at, lane] + ps)
            w_ref[at, lane] = w.astype(BF16)
            dv = slope * g_all[at, lane]
            acc = dv if acc is None else acc + dv
            dv_ref[at, lane] = dv.astype(BF16)
        racc_ref[at, :] = acc
    r_ref[...] = racc_ref[...].T.astype(BF16)
    back = dot_nt(mix_ref[side : side + total, :], dv_ref[...]).astype(BF16) if total <= 512 else None
    for b, ref in enumerate(s_refs):
        n = ref.shape[0]
        for at in range(0, n, 512):
            m = min(512, n)
            low = b * n + at
            if back is not None:
                ref[at : at + m, :] = back[low : low + m]
            else:
                ref[at : at + m, :] = dot_nt(mix_ref[side + low : side + low + m, :], dv_ref[...]).astype(BF16)


def update_edges(et_ref, w_ref, dv_ref, mix_ref, cot_ref, r_ref, fronts_ref, out_ref, dq_ref, x0, x1, x2, x3):
    slots, side, rows = et_ref.shape
    width = r_ref.shape[1]
    low = mix_ref.shape[0] - side
    ue = fronts_ref[:, width + side : width + 2 * side].astype(F32).T.astype(BF16)
    uo = fronts_ref[:, width + 2 * side : width + 3 * side].astype(F32).T.astype(BF16)
    dq_ref[...] = dot(ue, dv_ref[...]).astype(BF16)
    o_all = dot(uo, w_ref[...])
    for s in range(slots):
        out_ref[s] = (et_ref[s].astype(F32) + o_all[:, s * rows : (s + 1) * rows]).astype(BF16)
    gout = dot_nt(lanes(cot_ref), w_ref[...]).astype(BF16)
    gedge = dot_nt(mix_ref[low:, :], dv_ref[...]).astype(BF16)
    for k, ref in enumerate((x0, x1, x2, x3)):
        at = slice(k * 128, k * 128 + 128)
        ref[:rows, :] = r_ref[:, at]
        ref[rows : rows + side, :] = gedge[:, at]
        ref[rows + side :, :] = gout[:, at]


def update_terms(parts, r_ref, laters_ref, *rest):
    s_refs, outs = rest[:parts], rest[-4:]
    width = r_ref.shape[1]
    total = sum_of(s_refs).astype(BF16)
    term = (dot(r_ref[...], laters_ref[:, :width]) + dot(total, laters_ref[:, width:])).astype(BF16)
    for k, ref in enumerate(outs):
        ref[:, :width] = term
        ref[:, width:] = total[:, k * 128 : k * 128 + 128]


def message_shares(x0, x1, x2, x3, _, r_ref, edge_ref, *s_refs):
    rows = r_ref.shape[0]
    every = sum_of((x0, x1, x2, x3)).astype(BF16)
    n = s_refs[0].shape[0]
    for b, ref in enumerate(s_refs):
        ref[...] = every[b * n : (b + 1) * n]
    low = every.shape[0] - edge_ref.shape[0]
    r_ref[...] = every[low - rows : low]
    edge_ref[...] = every[low:]


def message_terms(parts, r_ref, fronts_ref, backs_ref, nodes_ref, gb_ref, gc_ref, ge_ref, keep_ref, got_ref, *rest):
    s_refs, (term_ref, share_ref, late_ref) = rest[:parts], rest[parts:]
    late_ref[...] = (keep_ref[...].astype(F32) + got_ref[...].astype(F32)).astype(BF16)
    rows, shard = r_ref.shape
    width = nodes_ref.shape[1]
    total = sum_of(s_refs).astype(BF16)
    share_ref[:rows, :] = total
    share_ref[rows:, :] = r_ref[...]
    term = dot(r_ref[...], backs_ref[:shard, :width]) + dot(total, fronts_ref[:shard, :width])
    hat, _ = normalize(nodes_ref[...].astype(F32))
    gain = jnp.sum(term * hat, axis=0, keepdims=True)
    edge = jnp.concatenate([ge_ref[0:2, :], jnp.zeros((2, width - 256), F32)], axis=1)
    gains = [gain, gb_ref[...] * 0.25, gc_ref[...] * 0.25, edge, jnp.zeros((11, width), F32)]
    term_ref[...] = jnp.concatenate([term] + gains, axis=0).astype(BF16)


def early_grads(b_ref, dp_ref, y_ref, dr_ref, c_ref, share_ref, x0, x1, x2, x3, _, keep_ref, send_ref):
    rows, width = c_ref.shape
    extra = sum_of((x0, x1, x2, x3)).astype(BF16)
    side = (extra.shape[0] - rows) // 2
    part = (width + side) // 4

    def put(ref, large, small):
        ref[:width, :] = large.astype(BF16)
        small = jnp.concatenate(small, axis=0).astype(BF16)
        ref[width : width + part, :] = jnp.concatenate([small[i * part : (i + 1) * part] for i in range(4)], axis=1)
        ref[width + part :, :] = jnp.zeros_like(ref[width + part :, :])

    def run(one, two):
        put(one, dot_tn(b_ref[...], dp_ref[...]),
            [dot_tn(c_ref[...], extra[:rows]), extra[rows : rows + side].astype(F32)])
        put(two, dot_tn(y_ref[...], dr_ref[...]),
            [dot_tn(c_ref[...], share_ref[...]), extra[rows + side :].astype(F32)])

    by_core(lambda: run(keep_ref, send_ref), lambda: run(send_ref, keep_ref))


def split(total, bit, stay_ref, go_ref):
    half = stay_ref.shape[0]
    own = (lax.axis_index("graph") // bit) % 2

    @pl.when(own == 0)
    def _():
        stay_ref[...] = total[:half]
        go_ref[...] = total[half:]

    @pl.when(own != 0)
    def _():
        stay_ref[...] = total[half:]
        go_ref[...] = total[:half]


def sum_split(bit, one_ref, two_ref, *rest):
    stay_ref, go_ref = rest[-2:]
    split((one_ref[...].astype(F32) + two_ref[...].astype(F32)).astype(BF16), bit, stay_ref, go_ref)


def sum_two(one_ref, two_ref, _, out_ref):
    out_ref[...] = (one_ref[...].astype(F32) + two_ref[...].astype(F32)).astype(BF16)


def join(bit, one, two):
    own = (lax.axis_index("graph") // bit) % 2
    return jnp.where(own == 0, one, two), jnp.where(own == 0, two, one)


def join_two(bit, one_ref, two_ref, _, out_ref):
    half = one_ref.shape[0]
    first, second = join(bit, one_ref[...], two_ref[...])
    out_ref[:half, :] = first
    out_ref[half:, :] = second


def finish_early(bit, m0, m1, t0, t1, gin_ref, gout_ref, self_ref, edge_ref, other_ref, out_ref):
    width, side = gin_ref.shape[0], edge_ref.shape[0]
    part = (width + side) // 4

    def run(one, two):
        for pair, large, top, low in ((one, gin_ref, self_ref, edge_ref), (two, gout_ref, other_ref, out_ref)):
            pair = [r[...] for r in pair]
            if bit:
                pair = join(bit, *pair)
            every = jnp.concatenate(pair, axis=0).astype(F32)
            large[...] = every[:width]
            small = jnp.concatenate([every[width : width + part, i * 128 : i * 128 + 128] for i in range(4)], axis=0)
            top[...] = small[:width]
            low[...] = small[width:]

    by_core(lambda: run((m0, m1), (t0, t1)), lambda: run((t0, t1), (m0, m1)))


def message_backward(
    nbr_scale, slots, t0, t1, t2, t3, h1_ref, dh2_ref, gain_ref, backs_ref, slope_ref, mix_ref,
    dh1_ref, dt_ref, gain_out, du_ref, x0, x1, x2, x3, g_ref, racc_ref,
):
    hidden, rows = g_ref.shape
    width = h1_ref.shape[1]
    side = mix_ref.shape[0] - x0.shape[0] + rows
    total = x0.shape[0] - rows - side
    db = sum_of((t0, t1, t2, t3))
    hat, inv = normalize(h1_ref[...])
    gain_out[...] = jnp.sum(db * hat, axis=0, keepdims=True)
    dh1 = dh2_ref[...] + norm_back(db * gain_ref[1:2, :], hat, inv)
    dh1_ref[...] = dh1
    dt = dh1.astype(BF16)
    dt_ref[...] = dt
    g_ref[...] = dot_nt(backs_ref[:, width : 2 * width], dt) * nbr_scale
    for low in range(0, hidden, CHUNK):
        at = slice(low, low + CHUNK)
        g = g_ref[at, :]
        acc = None
        for s in range(slots):
            lane = slice(s * rows, (s + 1) * rows)
            du = slope_ref[at, lane].astype(F32) * g
            acc = du if acc is None else acc + du
            du_ref[at, lane] = du.astype(BF16)
        racc_ref[at, :] = acc
    for low in range(0, total, 512):
        back = dot_nt(mix_ref[side + low : side + low + 512, :], du_ref[...]).astype(BF16)
        for k, ref in enumerate((x0, x1, x2, x3)):
            ref[low : low + 512, :] = back[:, k * 128 : k * 128 + 128]
    gedge = dot_nt(mix_ref[:side, :], du_ref[...]).astype(BF16)
    for k, ref in enumerate((x0, x1, x2, x3)):
        ref[total : total + rows, :] = racc_ref[k * 128 : k * 128 + 128, :].T.astype(BF16)
        ref[total + rows :, :] = gedge[:, k * 128 : k * 128 + 128]


def message_edges(
    et_ref, du_ref, dq_ref, cot_ref, gains_ref, fronts_ref, out_ref, ge_ref, ga_ref, gb_ref
):
    slots, side, rows = et_ref.shape
    width = fronts_ref.shape[0]
    we = fronts_ref[:, width : width + side].astype(F32).T.astype(BF16)
    df_all = dot(we, du_ref[...])
    ga_ref[...] = jnp.zeros_like(ga_ref)
    gb_ref[...] = jnp.zeros_like(gb_ref)
    for s in range(slots):
        df = df_all[:, s * rows : (s + 1) * rows]
        dq = dq_ref[:, s * rows : (s + 1) * rows].astype(F32)
        hat, inv = normalize(et_ref[s].astype(F32), 0)
        ga_ref[...] += df * hat
        gb_ref[...] += dq * hat
        out_ref[s] = cot_ref[s].astype(F32) + norm_back(gains_ref[0] * df + gains_ref[1] * dq, hat, inv, 0)
    lane = lax.broadcasted_iota(jnp.int32, (side, 256), 1)
    row = lax.broadcasted_iota(jnp.int32, (side, 256), 0)

    def laid(ref):
        column = jnp.sum(ref[...], axis=1, keepdims=True)
        return jnp.sum(jnp.where(row == lane, column, 0.0), axis=0, keepdims=True)

    ge_ref[...] = jnp.concatenate([laid(ga_ref), laid(gb_ref), jnp.zeros((6, 256), F32)], axis=0)


def late_grads(edge_ref, s_ref, dt_ref, keep_ref, send_ref):
    rows, width = dt_ref.shape
    gout = dot_tn(s_ref[...], dt_ref[...])
    pieces = [edge_ref[...].astype(F32)] + [gout[:, i * 128 : i * 128 + 128] for i in range(width // 128)]
    every = jnp.concatenate(pieces, axis=0).astype(BF16)
    half = keep_ref.shape[0]

    def put(one, two):
        one[...] = every[:half]
        two[...] = every[half:]

    by_core(lambda: put(keep_ref, send_ref), lambda: put(send_ref, keep_ref))


def node_finish(t0, t1, t2, t3, nodes_ref, dh1_ref, gain_ref, share_ref, late_ref, got_ref, out_ref, pack_ref, long_ref):
    rows, width = dh1_ref.shape
    low = share_ref.shape[0]
    every = sum_of((t0, t1, t2, t3))
    hat, inv = normalize(nodes_ref[...].astype(F32))
    out_ref[...] = dh1_ref[...] + norm_back(every[:rows] * gain_ref[0:1, :], hat, inv)
    gains = jnp.concatenate(
        [every[rows : rows + 8, i * 128 : i * 128 + 128] for i in range(width // 128)], axis=0
    ).astype(BF16)
    pack_ref[:low, :] = share_ref[...]
    pack_ref[low:, :] = gains
    long_ref[:low, :] = share_ref[...]
    long_ref[low : pack_ref.shape[0], :] = gains
    long_ref[pack_ref.shape[0] :, :] = (late_ref[...].astype(F32) + got_ref[...].astype(F32)).astype(BF16)


def message_grads(parts, a_ref, *rest):
    packs, (one_ref, two_ref, out_ref) = rest[:parts], rest[parts:]
    rows = a_ref.shape[0] // parts
    width = a_ref.shape[1]
    size = packs[0].shape[0]
    both = jnp.concatenate(
        [jnp.concatenate([r[:rows, :], r[rows : 2 * rows, :]], axis=1) for r in packs], axis=0
    )
    grad = dot_tn(a_ref[...], both).astype(BF16)
    out_ref[:width, :] = grad[:, :128]
    out_ref[width : 2 * width, :] = grad[:, 128:]
    low = 2 * width + one_ref.shape[0] - size
    out_ref[2 * width : low, :] = (one_ref[size:, :].astype(F32) + two_ref[size:, :].astype(F32)).astype(BF16)
    out_ref[low:, :] = sum(r[2 * rows : size, :].astype(F32) for r in packs).astype(BF16)


def finish_late(
    mine_ref, theirs_ref, other_ref, self_ref, edge_ref, out_ref, ga_ref, gb_ref, gc_ref, gea_ref, geb_ref
):
    width, side = other_ref.shape[0], edge_ref.shape[0]
    rows = out_ref.shape[0]
    other_ref[...] = mine_ref[:width, :].astype(F32) + theirs_ref[:width, :].astype(F32)
    self_ref[...] = mine_ref[width : 2 * width, :].astype(F32) + theirs_ref[width : 2 * width, :].astype(F32)
    low = mine_ref.shape[0] - 8 * (width // 128)
    gains = mine_ref[low:, :].astype(F32) + theirs_ref[low:, :].astype(F32)
    for i, ref in enumerate((ga_ref, gb_ref, gc_ref)):
        ref[...] = jnp.concatenate([gains[8 * j + i : 8 * j + i + 1] for j in range(width // 128)], axis=1)
    for i, ref in ((3, gea_ref), (4, geb_ref)):
        ref[...] = jnp.concatenate([gains[i : i + 1], gains[8 + i : 9 + i]], axis=1)[:, :side]

    def run(first, second):
        every = jnp.concatenate([first[2 * width : low, :], second[2 * width : low, :]], axis=0).astype(F32)
        edge_ref[...] = every[:side]
        out_ref[...] = jnp.concatenate(
            [every[side + i * rows : side + (i + 1) * rows] for i in range(width // 128)], axis=1
        )

    by_core(lambda: run(mine_ref, theirs_ref), lambda: run(theirs_ref, mine_ref))


def whole(shape):
    zeros = (0,) * len(shape)
    return pl.BlockSpec(tuple(shape), lambda i: zeros)


def in_bytes(shape, dtype):
    n = jnp.dtype(dtype).itemsize
    for d in shape:
        n *= d
    return n


AFTER = pl.BlockSpec(memory_space=pl.ANY)


def call(name, body, grid, ins, outs, scratch=(), vmem=24, heavy=False):
    ins = [a if isinstance(a, tuple) else (a, whole(a.shape)) for a in ins]
    outs = [o if len(o) == 3 else o + (whole(o[0]),) for o in outs]
    moved = sum(in_bytes(a.shape, a.dtype) for a, _ in ins) + sum(in_bytes(sh, t) for sh, t, _ in outs)
    return pl.pallas_call(
        body,
        grid=(grid,),
        in_specs=[s for _, s in ins],
        out_specs=[s for _, _, s in outs],
        out_shape=[jax.ShapeDtypeStruct(sh, t) for sh, t, _ in outs],
        scratch_shapes=list(scratch),
        compiler_params=pltpu.CompilerParams(vmem_limit_bytes=vmem << 20, dimension_semantics=("arbitrary",)),
        cost_estimate=pl.CostEstimate(flops=2 * 10**10 if heavy else 0, bytes_accessed=moved, transcendentals=0),
        name=name,
    )(*[a for a, _ in ins])


def far_in(values):
    return pltpu.with_memory_space_constraint(values, pltpu.HBM)


def swap(values, axis, bits, size):
    return lax.ppermute(values, axis, [(i, i ^ bits) for i in range(size)])


def partners(values, axis, size):
    return [values] + [swap(values, axis, k, size) for k in range(1, size)]


def deal(pieces, axis, size):
    return [pieces[0]] + [swap(pieces[k], axis, k, size) for k in range(1, size)]


def turn(values, start, axis):
    return lax.dynamic_slice_in_dim(
        jnp.concatenate([values, values], axis=axis), start, values.shape[axis], axis=axis
    )


def after(values, *others):
    return lax.optimization_barrier((values,) + others)[0]


def local(sizes, *args):
    (
        nodes, edges, neighbours, resmask, node_gain_a, edge_gain_a, message_self, message_other, message_edge,
        message_out, node_gain_b, ffn_in, ffn_out, node_gain_c, edge_gain_b, update_self, update_other, update_edge,
        update_out, node_cot, edge_cot,
    ) = args
    cores, graph, mp = sizes
    near = graph <= 4
    at_graph = None if near else lax.axis_index("graph")
    _, rows, width = nodes.shape
    slots, side = edges.shape[2:]
    nbrs = neighbours.shape[2]
    total = resmask.shape[1]
    shard = message_self.shape[1]
    hidden = shard * mp
    ff = ffn_in.shape[1]
    vmem = 20 if total <= 1024 else 60
    run = functools.partial(call, vmem=vmem)

    def gather_rows(values):
        if near:
            return partners(values, "graph", graph)
        return [turn(lax.all_gather(values, "graph", axis=0, tiled=True), at_graph * rows, 0)]

    def return_rows(blocks):
        if near:
            return deal(blocks, "graph", graph)
        placed = turn(blocks[0], total - at_graph * rows, 0)
        return [lax.psum_scatter(placed, "graph", scatter_dimension=0, tiled=True)]

    blocks = [((rows, hidden), BF16)] * graph if near else [((total, hidden), BF16)]
    outs = len(blocks)
    node, cot_n = nodes[0], node_cot[0]

    nodes_all = gather_rows(node)
    et = jnp.transpose(edges[0], (1, 2, 0))
    cot = jnp.transpose(edge_cot[0], (1, 2, 0))
    edge_sh, hid_sh = (slots, side, rows), (hidden, slots * rows)

    mix, mask_row, gains_e, gains_n, a_own = run(
        "edge_prep", functools.partial(edge_prep, graph, near), 1,
        [
            far_in(v) for v in (
                et, jnp.transpose(neighbours, (2, 0, 1)), resmask, edge_gain_a[None, :], edge_gain_b[None, :],
                node_gain_a[None, :], node_gain_b[None, :], node_gain_c[None, :], node,
            )
        ],
        [((2 * side + total, slots * rows), BF16), ((1, total), jnp.int32), ((2, side, rows), F32), ((8, width), F32),
         ((rows, width), BF16)],
    )
    full, half, later, later_half = run(
        "pack_weights", pack_weights, 1,
        [far_in(w) for w in (
            message_self, message_other, message_edge, message_out, update_self, update_other, update_edge, update_out.T
        )],
        [((shard, 2 * width + 2 * 640), BF16), ((shard, width + 640), BF16), ((shard, 2 * width), BF16),
         ((shard, width), BF16)],
    )
    def across(values):
        pairs = [(c * mp + m, c * mp + (m ^ (1 + c))) for c in range(2) for m in range(mp)]
        return lax.ppermute(values, ("dp", "mp"), pairs)

    cross, diag = across(full), swap(half, "mp", 3, mp)
    cross_later, diag_later = across(later), swap(later_half, "mp", 3, mp)
    (a_all,) = run(
        "row_prep", functools.partial(row_prep, len(nodes_all)), 1,
        ([a_own] + nodes_all[1:] if near else nodes_all) + [gains_n], [((total, width), BF16)],
    )
    cross, diag = after(cross, a_all), after(diag, a_all)
    slope_m, pooled_part, fronts, backs = run(
        "message_forward", functools.partial(message_forward, 1.0 / nbrs, slots), 1,
        [mix, mask_row, a_all, full, cross, diag, swap(cross, "dp", 1, cores), swap(diag, "dp", 1, cores),],
        [(hid_sh, BF16), ((rows, hidden), BF16), ((hidden, width + 640), BF16), ((hidden, width + 640), BF16)],
        [pltpu.VMEM((hidden + 16, total + side), BF16), pltpu.VMEM((hidden + 16, slots * rows), F32),
         pltpu.VMEM((hidden, rows), F32), pltpu.VMEM((hidden, rows), F32)], heavy=True,
    )

    pooled, h1, b, y, slope_f, h2_part = run(
        "node_forward", node_forward, 1,
        partners(pooled_part, "mp", mp) + [node, backs, gains_n, ffn_in, ffn_out, (cross_later, AFTER), (diag_later, AFTER)],
        [((rows, hidden), BF16), ((rows, width), F32), ((rows, width), BF16), ((rows, ff), BF16), ((rows, ff), BF16),
         ((rows, width), BF16)],
    )
    h2, c_own, nodes_out = run(
        "node_close", node_close, 1, [h1] + partners(h2_part, "mp", mp) + [gains_n],
        [((rows, width), F32), ((rows, width), BF16), ((rows, width), BF16)],
    )
    c_all = gather_rows(c_own)

    w_act, dv, r_upd, laters, *s_upd = run(
        "update_nodes", functools.partial(update_nodes, slots, len(c_all), outs), 1,
        [mix, cot, fronts] + c_all
        + [later, cross_later, diag_later, swap(cross_later, "dp", 1, cores), swap(diag_later, "dp", 1, cores)],
        [(hid_sh, BF16), (hid_sh, BF16), ((rows, hidden), BF16), ((hidden, 2 * width), BF16)] + blocks,
        [pltpu.VMEM((hidden, total + side), BF16), pltpu.VMEM(hid_sh, F32), pltpu.VMEM(hid_sh, F32),
         pltpu.VMEM((hidden, rows), F32), pltpu.VMEM((hidden, rows), F32)], heavy=True,
    )
    s_upd_parts = return_rows(s_upd)
    eo, dq, *extra = run(
        "update_edges", update_edges, 1, [et, w_act, dv, mix, cot, r_upd, fronts],
        [(edge_sh, BF16), ((side, slots * rows), BF16)] + [((rows + 2 * side, shard), BF16)] * mp,
    )
    edges_out = jnp.transpose(eo, (2, 0, 1))[None]
    order = extra[0]
    extra = deal(extra, "mp", mp)

    terms = run(
        "update_terms", functools.partial(update_terms, outs), 1, [r_upd, laters] + s_upd_parts + [(order, AFTER)],
        [((rows, width + shard), BF16)] * mp,
    )
    dh2, dr, dp_ffn, gain_c, share, db_part = run(
        "node_backward", node_backward, 1, deal(terms, "mp", mp) + [h2, cot_n, gains_n, slope_f, ffn_in, ffn_out],
        [((rows, width), F32), ((rows, width), BF16), ((rows, ff), BF16), ((1, width), F32), ((rows, shard), BF16),
         ((rows, width), BF16)],
    )
    db_parts = partners(db_part, "mp", mp)

    size = (width + (width + side) // 4 + 63) // 64 * 64
    keep, send = run(
        "early_grads", early_grads, 1, [b, dp_ffn, y, dr, c_own, share] + extra + [(db_parts[3], AFTER)], [((size, ff), BF16)] * 2,
    )
    got = swap(send, "dp", 1, cores)
    halves, quarters = [((size // 2, ff), BF16)], [((size // 4, ff), BF16)]

    dh1, dt, gain_b, du, *shares = run(
        "message_backward", functools.partial(message_backward, 1.0 / nbrs, slots), 1,
        db_parts + [h1, dh2, gains_n, backs, slope_m, mix],
        [((rows, width), F32), ((rows, width), BF16), ((1, width), F32), (hid_sh, BF16)]
        + [((total + rows + side, shard), BF16)] * mp,
        [pltpu.VMEM((hidden, rows), F32), pltpu.VMEM((hidden, rows), F32)], heavy=True,
    )
    if near:
        stay, go = run("early_one", functools.partial(sum_split, 1), 1, [keep, got, (gain_b, AFTER)], halves * 2)
        go = swap(go, "graph", 1, graph)
    shares = deal(shares, "mp", mp)
    ge, gains_edge = run(
        "message_edges", message_edges, 1, [et, du, dq, cot, gains_e, fronts], [(edge_sh, F32), ((8, 256), F32)],
        [pltpu.VMEM((side, rows), F32), pltpu.VMEM((side, rows), F32)],
    )
    grad_edges = jnp.transpose(ge, (2, 0, 1))[None]

    share_r, grad_edge, *share_s = run(
        "message_shares", message_shares, 1, shares + [(gains_edge, AFTER)],
        [((rows, shard), BF16), ((side, shard), BF16)] + [(sh[:1] + (shard,), t) for sh, t in blocks],
    )
    if near:
        stay, go = run("early_two", functools.partial(sum_split, 2), 1, [stay, go, (gains_edge, AFTER)], quarters * 2)
        go = swap(go, "graph", 2, graph)
    half = (side + width) // 2
    keep_late, send_late = run(
        "late_grads", late_grads, 1,
        [grad_edge, (pooled, pl.BlockSpec((rows, shard), lambda i: (0, 0))), dt], [((half, shard), BF16)] * 2,
    )
    term, share, late = run(
        "message_terms", functools.partial(message_terms, outs), 1,
        [share_r, fronts, backs, node, gain_b, gain_c, gains_edge, keep_late, swap(send_late, "dp", 1, cores)]
        + return_rows(share_s),
        [((rows + 16, width), BF16), ((2 * rows, shard), BF16), ((half, shard), BF16)],
    )
    if near:
        (own,) = run("early_three", sum_two, 1, [stay, go, (term, AFTER)], quarters)
        go = swap(own, "graph", 2, graph)
    none = jnp.zeros((half, shard), BF16)
    grad_nodes, pack, long = run(
        "node_finish", node_finish, 1,
        partners(term, "mp", mp) + [node, dh1, gains_n, share, late, swap(late, "graph", 1, graph) if near else none],
        [((rows, width), F32), ((2 * rows + width // 16, shard), BF16),
         ((2 * rows + width // 16 + half, shard), BF16)],
    )
    if near:
        (own,) = run("early_four", functools.partial(join_two, 2), 1, [own, go, (pack, AFTER)], halves)
        got = swap(own, "graph", 1, graph)
        long_two = swap(long, "graph", 2, graph)
        packs = [pack, swap(pack, "graph", 1, graph), long_two, swap(pack, "graph", 3, graph)]
        early_sum = [own, after(got, *packs[1:])]
    else:
        early = lax.psum(keep.astype(F32) + got.astype(F32), "graph").astype(BF16)
        early_sum = [early[: size // 2], early[size // 2 :]]
        packs, long_two = [pack], jnp.zeros_like(long)
    grad_in, grad_out, grad_us, grad_ue, grad_uo, grad_uout = run(
        "finish_early", functools.partial(finish_early, 1 if near else 0), 1, early_sum + [swap(v, "dp", 1, cores) for v in early_sum],
        [((width, ff), F32), ((ff, width), F32), ((width, shard), F32), ((side, shard), F32), ((width, shard), F32),
         ((side, shard), F32)],
    )
    parts = len(packs)
    (part,) = run(
        "message_grads", functools.partial(message_grads, parts), 1,
        [(a_all, pl.BlockSpec((parts * rows, width), lambda i: (0, 0)))] + packs + [long, long_two],
        [((2 * width + half + width // 16, shard), BF16)],
    )
    if not near:
        part = lax.psum(part, "graph")
    grad_mo, grad_ms, grad_me, grad_mout, gain_a, gain_b, gain_c, gain_ea, gain_eb = run(
        "finish_late", finish_late, 1, [part, swap(part, "dp", 1, cores)],
        [((width, shard), F32), ((width, shard), F32), ((side, shard), F32), ((shard, width), F32), ((1, width), F32),
         ((1, width), F32), ((1, width), F32), ((1, side), F32), ((1, side), F32)],
    )
    return (
        nodes_out[None],
        edges_out,
        grad_nodes[None],
        grad_edges,
        gain_a[0],
        gain_ea[0],
        grad_ms,
        grad_mo,
        grad_me,
        grad_mout,
        gain_b[0],
        grad_in,
        grad_out,
        gain_c[0],
        gain_eb[0],
        grad_us,
        grad_uo,
        grad_ue,
        grad_uout.T,
    )


def solution(mesh):
    sizes = (mesh.shape["dp"], mesh.shape["graph"], mesh.shape["mp"])
    rows = P("dp", "graph", None)
    slots = P("dp", "graph", "mp", None)
    cols, tops = P(None, "mp"), P("mp", None)
    return jax.shard_map(
        functools.partial(local, sizes),
        mesh=mesh,
        in_specs=(
            rows, slots, rows, P("dp", None), P(), P(), cols, cols, cols, tops, P(), cols, tops, P(), P(), cols, cols,
            cols, tops, rows, slots,
        ),
        out_specs=(
            rows, slots, rows, slots, P(), P(), cols, cols, cols, tops, P(), cols, tops, P(), P(), cols, cols, cols,
            tops,
        ),
        check_vma=False,
    )
```

```python
import functools

import jax
import jax.numpy as jnp
from jax import lax
from jax.experimental import pallas as pl
from jax.experimental.pallas import tpu as pltpu
from jax.sharding import PartitionSpec as P

EPSILON = 1e-05
F32 = jnp.float32
BF16 = jnp.bfloat16
GELU_A = 0.7978845608028654
GELU_B = 0.044715


def dot(left, right):
    return lax.dot_general(left, right, (((1,), (0,)), ((), ())), preferred_element_type=F32)


def dot_nt(left, right):
    return lax.dot_general(left, right, (((1,), (1,)), ((), ())), preferred_element_type=F32)


def dot_tn(left, right):
    return lax.dot_general(left, right, (((0,), (0,)), ((), ())), preferred_element_type=F32)


def normalize(values, axis=-1):
    centre = values - jnp.mean(values, axis=axis, keepdims=True)
    variance = jnp.mean(centre * centre, axis=axis, keepdims=True)
    scale_inv = lax.rsqrt(variance + EPSILON)
    return centre * scale_inv, scale_inv


def norm_back(grad_hat, normed, scale_inv, axis=-1):
    return scale_inv * (
        grad_hat
        - jnp.mean(grad_hat, axis=axis, keepdims=True)
        - normed * jnp.mean(grad_hat * normed, axis=axis, keepdims=True)
    )


def gelu_both(u):
    poly = GELU_A + (GELU_A * GELU_B) * (u * u)
    half = 0.5 + 0.5 * jnp.tanh(u * poly)
    value = u * half
    return value, half + (value * (1.0 - half)) * (6.0 * poly - 4.0 * GELU_A)


def stack(refs, lo, hi):
    return jnp.concatenate([r[:, lo:hi] for r in refs], axis=0)


def rows_of(refs):
    return refs[0][...] if len(refs) == 1 else jnp.concatenate([r[...] for r in refs], axis=0)


def sum_of(refs, lo=None, hi=None):
    parts = [r[...].astype(F32) if lo is None else r[:, lo:hi].astype(F32) for r in refs]
    while len(parts) > 1:
        parts = [sum(parts[i : i + 2]) if i + 1 < len(parts) else parts[i] for i in range(0, len(parts), 2)]
    return parts[0]


def spread(row, count):
    return jnp.concatenate([row[:, i * 128 : i * 128 + 128] for i in range(count)], axis=0)


def by_core(first, second):
    core = lax.axis_index("dp")
    pl.when(core == 0)(first)
    pl.when(core != 0)(second)


def onehot(idx, total):
    here = lax.broadcasted_iota(jnp.int32, (total, idx.shape[1]), 0)
    return (here == idx).astype(F32).astype(BF16)


CHUNK = 32
GROUP = 8


def groups(slots):
    return [range(at, min(at + GROUP, slots)) for at in range(0, slots, GROUP)]


def lanes(refs):
    return jnp.concatenate([refs[s] for s in range(refs.shape[0])], axis=1)


def edge_prep(
    graph, near, et_ref, nbr_ref, res_ref, ga_ref, gb_ref, na_ref, nb_ref, nc_ref, node_ref,
    mix_ref, mask_ref, gains_ref, nodes_ref, own_ref,
):
    slots, side, rows = et_ref.shape
    total = mask_ref.shape[1]
    at_graph, at_mp = lax.axis_index("graph"), lax.axis_index("mp")
    for k in range(graph):
        block = (at_graph ^ k) if near else lax.rem(at_graph + k, graph)
        mask_ref[:, k * rows : (k + 1) * rows] = res_ref[:, pl.ds(pl.multiple_of(block * rows, rows), rows)]
    for i, ref in enumerate((na_ref, nb_ref, nc_ref)):
        nodes_ref[i : i + 1, :] = ref[...]
    hat, _ = normalize(node_ref[...].astype(F32))
    own_ref[...] = (hat * na_ref[...]).astype(BF16)
    for i, ref in enumerate((ga_ref, gb_ref)):
        gains_ref[i] = jnp.broadcast_to(ref[...], (rows, ref.shape[1])).T
    for s in range(slots):
        at = slice(s * rows, (s + 1) * rows)
        hat, _ = normalize(et_ref[s].astype(F32), 0)
        mix_ref[:side, at] = (hat * gains_ref[0]).astype(BF16)
        mix_ref[side + total :, at] = (hat * gains_ref[1]).astype(BF16)
        nbr = nbr_ref[at_mp * slots + s]
        if near:
            idx = ((nbr // rows) ^ at_graph) * rows + lax.rem(nbr, rows)
        else:
            moved = nbr + (total - at_graph * rows)
            idx = jnp.where(moved >= total, moved - total, moved)
        mix_ref[side : side + total, at] = onehot(idx, total)


def node_close(h1_ref, p0, p1, p2, p3, gain_ref, _, __, h2_ref, c_ref, out_ref):
    h2 = h1_ref[...] + sum_of((p0, p1, p2, p3))
    h2_ref[...] = h2
    hat, _ = normalize(h2)
    c_ref[...] = (hat * gain_ref[2:3, :]).astype(BF16)
    out_ref[...] = h2.astype(BF16)


def node_backward(
    t0, t1, t2, t3, h2_ref, cot_ref, gain_ref, slope_ref, win_ref, wout_ref,
    dh2_ref, dr_ref, dp_ref, gain_out, share_ref, part_ref,
):
    width = h2_ref.shape[1]
    dc = sum_of((t0, t1, t2, t3), 0, width)
    share_ref[...] = sum_of((t0, t1, t2, t3), width, width + 128).astype(BF16)
    hat, inv = normalize(h2_ref[...])
    gain_out[...] = jnp.sum(dc * hat, axis=0, keepdims=True)
    dh2 = cot_ref[...].astype(F32) + norm_back(dc * gain_ref[2:3, :], hat, inv)
    dh2_ref[...] = dh2
    dr = dh2.astype(BF16)
    dr_ref[...] = dr
    dp = (slope_ref[...].astype(F32) * dot_nt(dr, wout_ref[...])).astype(BF16)
    dp_ref[...] = dp
    part_ref[...] = dot_nt(dp, win_ref[...]).astype(BF16)


def pack_weights(ms, mo, me, mout, us, uo, ue, uout_t, full_ref, half_ref, later_ref, later_half_ref):
    wide = ms.shape[0]
    size = half_ref.shape[1]

    def turned(ref):
        return ref[...].astype(F32).T.astype(BF16)

    def filled(parts):
        got = sum(p.shape[1] for p in parts)
        return jnp.concatenate(parts + [jnp.zeros((ms.shape[1], size - got), BF16)], axis=1)

    front = filled([turned(mo), turned(me), turned(ue), turned(uout_t)])
    back = filled([turned(ms), mout[...]])
    full_ref[:, :size] = front
    full_ref[:, size:] = back
    later_ref[:, :wide] = turned(us)
    later_ref[:, wide:] = turned(uo)

    def keep_front():
        half_ref[...] = front
        later_half_ref[...] = later_ref[:, :wide]

    def keep_back():
        half_ref[...] = back
        later_half_ref[...] = later_ref[:, wide:]

    by_core(keep_front, keep_back)


def row_prep(parts, *refs):
    node_refs, gain_ref, a_ref = refs[:parts], refs[parts], refs[parts + 1]
    total = a_ref.shape[0]
    block = node_refs[0].shape[0] if parts > 1 else 512
    for at in range(0, total, block):
        ref = node_refs[at // block] if parts > 1 else node_refs[0].at[at : at + block]
        if parts > 1 and at == 0:
            a_ref[:block, :] = ref[...]
        else:
            hat, _ = normalize(ref[...].astype(F32))
            a_ref[at : at + block, :] = (hat * gain_ref[0:1, :]).astype(BF16)


def message_forward(
    nbr_scale, slots, mix_ref, mask_ref, a_ref, full_ref, cross_ref, diag_ref, cross_two_ref, diag_two_ref,
    slope_ref, pooled_ref, fronts_ref, backs_ref, lhs_ref, u_ref, ps_ref, acc_ref,
):
    total, width = a_ref.shape
    hidden, rows = ps_ref.shape
    side = (mix_ref.shape[0] - total) // 2
    shard, size = diag_ref.shape

    def place(blocks, front, back):
        for k, ref in enumerate(blocks):
            at = slice(k * shard, (k + 1) * shard)
            fronts_ref[at, :] = ref[:, :size]
            backs_ref[at, :] = ref[:, size:]
        fronts_ref[3 * shard :, :] = front[...]
        backs_ref[3 * shard :, :] = back[...]

    by_core(
        lambda: place((full_ref, cross_ref, cross_two_ref), diag_ref, diag_two_ref),
        lambda: place((full_ref, cross_two_ref, cross_ref), diag_two_ref, diag_ref),
    )
    lhs_ref[:hidden, :side] = fronts_ref[:, width : width + side]
    for at in range(0, total, 512):
        lhs_ref[:hidden, side + at : side + at + 512] = dot_nt(
            fronts_ref[:, :width], a_ref[at : at + 512, :]
        ).astype(BF16)
    top = lax.broadcasted_iota(jnp.int32, (16, total), 0) == 0
    lhs_ref[hidden:, side:] = jnp.where(top, mask_ref[...].astype(F32), 0.0).astype(BF16)
    lhs_ref[hidden:, :side] = jnp.zeros((16, side), BF16)
    ps_ref[...] = dot_nt(backs_ref[:, :width], a_ref[:rows, :])

    def product(group):
        lane = slice(group[0] * rows, (group[-1] + 1) * rows)
        u_ref[:, lane] = dot(lhs_ref[...], mix_ref[: side + total, lane])

    parts = groups(slots)
    product(parts[0])
    for i, group in enumerate(parts):
        if i + 1 < len(parts):
            product(parts[i + 1])
        for low in range(0, hidden, CHUNK):
            at = slice(low, low + CHUNK)
            ps = ps_ref[at, :]
            acc = acc_ref[at, :] if i else None
            for s in group:
                lane = slice(s * rows, (s + 1) * rows)
                z, slope = gelu_both(u_ref[at, lane] + ps)
                mask = u_ref[hidden : hidden + 1, lane]
                z = z * mask
                acc = z if acc is None else acc + z
                slope_ref[at, lane] = (slope * mask).astype(BF16)
            acc_ref[at, :] = acc
    pooled_ref[...] = (acc_ref[...] * nbr_scale).T.astype(BF16)


def node_forward(
    s0, s1, s2, s3, nodes_ref, backs_ref, gain_ref, win_ref, wout_ref,
    s_ref, h1_ref, b_ref, y_ref, slope_ref, part_ref
):
    width = nodes_ref.shape[1]
    sums = []
    for p in range(4):
        sums.append(sum(
            ref[:, (p ^ k) * 128 : (p ^ k) * 128 + 128].astype(F32) for k, ref in enumerate((s0, s1, s2, s3))
        ).astype(BF16))
    pooled = jnp.concatenate(sums, axis=1)
    s_ref[...] = pooled
    h1 = nodes_ref[...].astype(F32) + dot(pooled, backs_ref[:, width : 2 * width])
    h1_ref[...] = h1
    hat, _ = normalize(h1)
    b = (hat * gain_ref[1:2, :]).astype(BF16)
    b_ref[...] = b
    y, slope = gelu_both(dot(b, win_ref[...]))
    y = y.astype(BF16)
    y_ref[...] = y
    slope_ref[...] = slope.astype(BF16)
    part_ref[...] = dot(y, wout_ref[...]).astype(BF16)


def update_nodes(slots, parts, outs, mix_ref, cot_ref, fronts_ref, *rest):
    node_refs = rest[:parts]
    own_ref, cross_ref, diag_ref, cross_two_ref, diag_two_ref, w_ref, dv_ref, r_ref, laters_ref = rest[parts : parts + 9]
    s_refs = rest[parts + 9 : parts + 9 + outs]
    lhs_ref, v_ref, g_ref, ps_ref, racc_ref = rest[parts + 9 + outs :]
    side, rows = cot_ref.shape[1:]
    total = mix_ref.shape[0] - 2 * side
    width = node_refs[0].shape[1]
    hidden = ps_ref.shape[0]
    shard = own_ref.shape[0]

    def place(blocks, own, other):
        for k, ref in enumerate(blocks):
            laters_ref[k * shard : (k + 1) * shard, :] = ref[...]
        laters_ref[3 * shard :, :width] = own[...]
        laters_ref[3 * shard :, width:] = other[...]

    by_core(
        lambda: place((own_ref, cross_ref, cross_two_ref), diag_ref, diag_two_ref),
        lambda: place((own_ref, cross_two_ref, cross_ref), diag_two_ref, diag_ref),
    )
    other = laters_ref[:, width:]
    if parts > 1:
        lhs_ref[:, :total] = dot_nt(other, rows_of(node_refs)).astype(BF16)
    else:
        for at in range(0, total, 512):
            lhs_ref[:, at : at + 512] = dot_nt(other, node_refs[0][at : at + 512, :]).astype(BF16)
    lhs_ref[:, total:] = fronts_ref[:, width + side : width + 2 * side]
    wo = fronts_ref[:, width + 2 * side : width + 3 * side]
    ps_ref[...] = dot_nt(laters_ref[:, :width], node_refs[0][:rows, :])

    v_all = dot(lhs_ref[...], mix_ref[side:, :])
    g_all = dot(wo, lanes(cot_ref))
    for low in range(0, hidden, CHUNK):
        at = slice(low, low + CHUNK)
        ps = ps_ref[at, :]
        acc = None
        for s in range(slots):
            lane = slice(s * rows, (s + 1) * rows)
            w, slope = gelu_both(v_all[at, lane] + ps)
            w_ref[at, lane] = w.astype(BF16)
            dv = slope * g_all[at, lane]
            acc = dv if acc is None else acc + dv
            dv_ref[at, lane] = dv.astype(BF16)
        racc_ref[at, :] = acc
    r_ref[...] = racc_ref[...].T.astype(BF16)
    back = dot_nt(mix_ref[side : side + total, :], dv_ref[...]).astype(BF16) if total <= 512 else None
    for b, ref in enumerate(s_refs):
        n = ref.shape[0]
        for at in range(0, n, 512):
            m = min(512, n)
            low = b * n + at
            if back is not None:
                ref[at : at + m, :] = back[low : low + m]
            else:
                ref[at : at + m, :] = dot_nt(mix_ref[side + low : side + low + m, :], dv_ref[...]).astype(BF16)


def update_edges(et_ref, w_ref, dv_ref, mix_ref, cot_ref, r_ref, fronts_ref, out_ref, dq_ref, x0, x1, x2, x3):
    slots, side, rows = et_ref.shape
    width = r_ref.shape[1]
    low = mix_ref.shape[0] - side
    ue = fronts_ref[:, width + side : width + 2 * side].astype(F32).T.astype(BF16)
    uo = fronts_ref[:, width + 2 * side : width + 3 * side].astype(F32).T.astype(BF16)
    dq_ref[...] = dot(ue, dv_ref[...]).astype(BF16)
    o_all = dot(uo, w_ref[...])
    for s in range(slots):
        out_ref[s] = (et_ref[s].astype(F32) + o_all[:, s * rows : (s + 1) * rows]).astype(BF16)
    gout = dot_nt(lanes(cot_ref), w_ref[...]).astype(BF16)
    gedge = dot_nt(mix_ref[low:, :], dv_ref[...]).astype(BF16)
    for k, ref in enumerate((x0, x1, x2, x3)):
        at = slice(k * 128, k * 128 + 128)
        ref[:rows, :] = r_ref[:, at]
        ref[rows : rows + side, :] = gedge[:, at]
        ref[rows + side :, :] = gout[:, at]


def update_terms(parts, r_ref, laters_ref, *rest):
    s_refs, outs = rest[:parts], rest[-4:]
    width = r_ref.shape[1]
    total = sum_of(s_refs).astype(BF16)
    term = (dot(r_ref[...], laters_ref[:, :width]) + dot(total, laters_ref[:, width:])).astype(BF16)
    for k, ref in enumerate(outs):
        ref[:, :width] = term
        ref[:, width:] = total[:, k * 128 : k * 128 + 128]


def message_shares(x0, x1, x2, x3, _, r_ref, edge_ref, *s_refs):
    rows = r_ref.shape[0]
    every = sum_of((x0, x1, x2, x3)).astype(BF16)
    n = s_refs[0].shape[0]
    for b, ref in enumerate(s_refs):
        ref[...] = every[b * n : (b + 1) * n]
    low = every.shape[0] - edge_ref.shape[0]
    r_ref[...] = every[low - rows : low]
    edge_ref[...] = every[low:]


def message_terms(parts, r_ref, fronts_ref, backs_ref, nodes_ref, gb_ref, gc_ref, ge_ref, keep_ref, got_ref, *rest):
    s_refs, (term_ref, share_ref, late_ref) = rest[:parts], rest[parts:]
    late_ref[...] = (keep_ref[...].astype(F32) + got_ref[...].astype(F32)).astype(BF16)
    rows, shard = r_ref.shape
    width = nodes_ref.shape[1]
    total = sum_of(s_refs).astype(BF16)
    share_ref[:rows, :] = total
    share_ref[rows:, :] = r_ref[...]
    term = dot(r_ref[...], backs_ref[:shard, :width]) + dot(total, fronts_ref[:shard, :width])
    hat, _ = normalize(nodes_ref[...].astype(F32))
    gain = jnp.sum(term * hat, axis=0, keepdims=True)
    edge = jnp.concatenate([ge_ref[0:2, :], jnp.zeros((2, width - 256), F32)], axis=1)
    gains = [gain, gb_ref[...] * 0.25, gc_ref[...] * 0.25, edge, jnp.zeros((11, width), F32)]
    term_ref[...] = jnp.concatenate([term] + gains, axis=0).astype(BF16)


def early_grads(b_ref, dp_ref, y_ref, dr_ref, c_ref, share_ref, x0, x1, x2, x3, _, keep_ref, send_ref):
    rows, width = c_ref.shape
    extra = sum_of((x0, x1, x2, x3)).astype(BF16)
    side = (extra.shape[0] - rows) // 2
    part = (width + side) // 4

    def put(ref, large, small):
        ref[:width, :] = large.astype(BF16)
        small = jnp.concatenate(small, axis=0).astype(BF16)
        ref[width : width + part, :] = jnp.concatenate([small[i * part : (i + 1) * part] for i in range(4)], axis=1)
        ref[width + part :, :] = jnp.zeros_like(ref[width + part :, :])

    def run(one, two):
        put(one, dot_tn(b_ref[...], dp_ref[...]),
            [dot_tn(c_ref[...], extra[:rows]), extra[rows : rows + side].astype(F32)])
        put(two, dot_tn(y_ref[...], dr_ref[...]),
            [dot_tn(c_ref[...], share_ref[...]), extra[rows + side :].astype(F32)])

    by_core(lambda: run(keep_ref, send_ref), lambda: run(send_ref, keep_ref))


def split(total, bit, stay_ref, go_ref):
    half = stay_ref.shape[0]
    own = (lax.axis_index("graph") // bit) % 2

    @pl.when(own == 0)
    def _():
        stay_ref[...] = total[:half]
        go_ref[...] = total[half:]

    @pl.when(own != 0)
    def _():
        stay_ref[...] = total[half:]
        go_ref[...] = total[:half]


def sum_split(bit, one_ref, two_ref, *rest):
    stay_ref, go_ref = rest[-2:]
    split((one_ref[...].astype(F32) + two_ref[...].astype(F32)).astype(BF16), bit, stay_ref, go_ref)


def sum_two(one_ref, two_ref, _, out_ref):
    out_ref[...] = (one_ref[...].astype(F32) + two_ref[...].astype(F32)).astype(BF16)


def finish_early(near, *refs):
    parts = 4 if near else 1
    mine, theirs = refs[:parts], refs[parts : 2 * parts]
    gin_ref, gout_ref, self_ref, edge_ref, other_ref, out_ref, one_ref, two_ref = refs[2 * parts :]
    width, side = gin_ref.shape[0], edge_ref.shape[0]
    part = (width + side) // 4

    def run(one, two):
        for pieces, every, large, top, low in (
            (one, one_ref, gin_ref, self_ref, edge_ref), (two, two_ref, gout_ref, other_ref, out_ref)
        ):
            size = pieces[0].shape[0]
            for k, ref in enumerate(pieces):
                if near:
                    owner = lax.axis_index("graph") ^ k
                    at = pl.multiple_of(((owner % 2) * 2 + owner // 2) * size, 16)
                    every[pl.ds(at, size), :] = ref[...]
                else:
                    every[...] = ref[...]
            large[...] = every[:width, :].astype(F32)
            small = every[width : width + part, :].astype(F32)
            small = jnp.concatenate([small[:, i * 128 : i * 128 + 128] for i in range(4)], axis=0)
            top[...] = small[:width]
            low[...] = small[width:]

    by_core(lambda: run(mine, theirs), lambda: run(theirs, mine))


def message_backward(
    nbr_scale, slots, t0, t1, t2, t3, h1_ref, dh2_ref, gain_ref, backs_ref, slope_ref, mix_ref,
    dh1_ref, dt_ref, gain_out, du_ref, x0, x1, x2, x3, g_ref, racc_ref,
):
    hidden, rows = g_ref.shape
    width = h1_ref.shape[1]
    side = mix_ref.shape[0] - x0.shape[0] + rows
    total = x0.shape[0] - rows - side
    db = sum_of((t0, t1, t2, t3))
    hat, inv = normalize(h1_ref[...])
    gain_out[...] = jnp.sum(db * hat, axis=0, keepdims=True)
    dh1 = dh2_ref[...] + norm_back(db * gain_ref[1:2, :], hat, inv)
    dh1_ref[...] = dh1
    dt = dh1.astype(BF16)
    dt_ref[...] = dt
    g_ref[...] = dot_nt(backs_ref[:, width : 2 * width], dt) * nbr_scale
    for low in range(0, hidden, CHUNK):
        at = slice(low, low + CHUNK)
        g = g_ref[at, :]
        acc = None
        for s in range(slots):
            lane = slice(s * rows, (s + 1) * rows)
            du = slope_ref[at, lane].astype(F32) * g
            acc = du if acc is None else acc + du
            du_ref[at, lane] = du.astype(BF16)
        racc_ref[at, :] = acc
    for low in range(0, total, 512):
        back = dot_nt(mix_ref[side + low : side + low + 512, :], du_ref[...]).astype(BF16)
        for k, ref in enumerate((x0, x1, x2, x3)):
            ref[low : low + 512, :] = back[:, k * 128 : k * 128 + 128]
    gedge = dot_nt(mix_ref[:side, :], du_ref[...]).astype(BF16)
    for k, ref in enumerate((x0, x1, x2, x3)):
        ref[total : total + rows, :] = racc_ref[k * 128 : k * 128 + 128, :].T.astype(BF16)
        ref[total + rows :, :] = gedge[:, k * 128 : k * 128 + 128]


def message_edges(
    et_ref, du_ref, dq_ref, cot_ref, gains_ref, fronts_ref, out_ref, ge_ref, ga_ref, gb_ref
):
    slots, side, rows = et_ref.shape
    width = fronts_ref.shape[0]
    we = fronts_ref[:, width : width + side].astype(F32).T.astype(BF16)
    df_all = dot(we, du_ref[...])
    ga_ref[...] = jnp.zeros_like(ga_ref)
    gb_ref[...] = jnp.zeros_like(gb_ref)
    for s in range(slots):
        df = df_all[:, s * rows : (s + 1) * rows]
        dq = dq_ref[:, s * rows : (s + 1) * rows].astype(F32)
        hat, inv = normalize(et_ref[s].astype(F32), 0)
        ga_ref[...] += df * hat
        gb_ref[...] += dq * hat
        out_ref[s] = cot_ref[s].astype(F32) + norm_back(gains_ref[0] * df + gains_ref[1] * dq, hat, inv, 0)
    lane = lax.broadcasted_iota(jnp.int32, (side, 256), 1)
    row = lax.broadcasted_iota(jnp.int32, (side, 256), 0)

    def laid(ref):
        column = jnp.sum(ref[...], axis=1, keepdims=True)
        return jnp.sum(jnp.where(row == lane, column, 0.0), axis=0, keepdims=True)

    ge_ref[...] = jnp.concatenate([laid(ga_ref), laid(gb_ref), jnp.zeros((6, 256), F32)], axis=0)


def late_grads(edge_ref, s_ref, dt_ref, keep_ref, send_ref):
    rows, width = dt_ref.shape
    gout = dot_tn(s_ref[...], dt_ref[...])
    pieces = [edge_ref[...].astype(F32)] + [gout[:, i * 128 : i * 128 + 128] for i in range(width // 128)]
    every = jnp.concatenate(pieces, axis=0).astype(BF16)
    half = keep_ref.shape[0]

    def put(one, two):
        one[...] = every[:half]
        two[...] = every[half:]

    by_core(lambda: put(keep_ref, send_ref), lambda: put(send_ref, keep_ref))


def node_finish(t0, t1, t2, t3, nodes_ref, dh1_ref, gain_ref, share_ref, late_ref, got_ref, *rest):
    out_ref, pack_ref, long_ref = rest[-3:]
    rows, width = dh1_ref.shape
    low = share_ref.shape[0]
    every = sum_of((t0, t1, t2, t3))
    hat, inv = normalize(nodes_ref[...].astype(F32))
    out_ref[...] = dh1_ref[...] + norm_back(every[:rows] * gain_ref[0:1, :], hat, inv)
    gains = jnp.concatenate(
        [every[rows : rows + 8, i * 128 : i * 128 + 128] for i in range(width // 128)], axis=0
    ).astype(BF16)
    pack_ref[:low, :] = share_ref[...]
    pack_ref[low:, :] = gains
    long_ref[:low, :] = share_ref[...]
    long_ref[low : pack_ref.shape[0], :] = gains
    long_ref[pack_ref.shape[0] :, :] = (late_ref[...].astype(F32) + got_ref[...].astype(F32)).astype(BF16)


def message_grads(parts, a_ref, *rest):
    packs, (one_ref, two_ref), out_ref = rest[:parts], rest[parts : parts + 2], rest[-1]
    rows = a_ref.shape[0] // parts
    width = a_ref.shape[1]
    size = packs[0].shape[0]
    both = jnp.concatenate(
        [jnp.concatenate([r[:rows, :], r[rows : 2 * rows, :]], axis=1) for r in packs], axis=0
    )
    grad = dot_tn(a_ref[...], both).astype(BF16)
    out_ref[:width, :] = grad[:, :128]
    out_ref[width : 2 * width, :] = grad[:, 128:]
    low = 2 * width + one_ref.shape[0] - size
    out_ref[2 * width : low, :] = (one_ref[size:, :].astype(F32) + two_ref[size:, :].astype(F32)).astype(BF16)
    out_ref[low:, :] = sum(r[2 * rows : size, :].astype(F32) for r in packs).astype(BF16)


def finish_late(
    mine_ref, theirs_ref, other_ref, self_ref, edge_ref, out_ref, ga_ref, gb_ref, gc_ref, gea_ref, geb_ref
):
    width, side = other_ref.shape[0], edge_ref.shape[0]
    rows = out_ref.shape[0]
    other_ref[...] = mine_ref[:width, :].astype(F32) + theirs_ref[:width, :].astype(F32)
    self_ref[...] = mine_ref[width : 2 * width, :].astype(F32) + theirs_ref[width : 2 * width, :].astype(F32)
    low = mine_ref.shape[0] - 8 * (width // 128)
    gains = mine_ref[low:, :].astype(F32) + theirs_ref[low:, :].astype(F32)
    for i, ref in enumerate((ga_ref, gb_ref, gc_ref)):
        ref[...] = jnp.concatenate([gains[8 * j + i : 8 * j + i + 1] for j in range(width // 128)], axis=1)
    for i, ref in ((3, gea_ref), (4, geb_ref)):
        ref[...] = jnp.concatenate([gains[i : i + 1], gains[8 + i : 9 + i]], axis=1)[:, :side]

    def run(first, second):
        every = jnp.concatenate([first[2 * width : low, :], second[2 * width : low, :]], axis=0).astype(F32)
        edge_ref[...] = every[:side]
        out_ref[...] = jnp.concatenate(
            [every[side + i * rows : side + (i + 1) * rows] for i in range(width // 128)], axis=1
        )

    by_core(lambda: run(mine_ref, theirs_ref), lambda: run(theirs_ref, mine_ref))


def whole(shape):
    zeros = (0,) * len(shape)
    return pl.BlockSpec(tuple(shape), lambda i: zeros)


def in_bytes(shape, dtype):
    n = jnp.dtype(dtype).itemsize
    for d in shape:
        n *= d
    return n


AFTER = pl.BlockSpec(memory_space=pl.ANY)


def call(name, body, grid, ins, outs, scratch=(), vmem=24, heavy=False):
    ins = [a if isinstance(a, tuple) else (a, whole(a.shape)) for a in ins]
    outs = [o if len(o) == 3 else o + (whole(o[0]),) for o in outs]
    moved = sum(in_bytes(a.shape, a.dtype) for a, _ in ins) + sum(in_bytes(sh, t) for sh, t, _ in outs)
    return pl.pallas_call(
        body,
        grid=(grid,),
        in_specs=[s for _, s in ins],
        out_specs=[s for _, _, s in outs],
        out_shape=[jax.ShapeDtypeStruct(sh, t) for sh, t, _ in outs],
        scratch_shapes=list(scratch),
        compiler_params=pltpu.CompilerParams(vmem_limit_bytes=vmem << 20, dimension_semantics=("arbitrary",)),
        cost_estimate=pl.CostEstimate(flops=2 * 10**10 if heavy else 0, bytes_accessed=moved, transcendentals=0),
        name=name,
    )(*[a for a, _ in ins])


def far_in(values):
    return pltpu.with_memory_space_constraint(values, pltpu.HBM)


def swap(values, axis, bits, size):
    return lax.ppermute(values, axis, [(i, i ^ bits) for i in range(size)])


def partners(values, axis, size):
    return [values] + [swap(values, axis, k, size) for k in range(1, size)]


def deal(pieces, axis, size):
    return [pieces[0]] + [swap(pieces[k], axis, k, size) for k in range(1, size)]


def turn(values, start, axis):
    return lax.dynamic_slice_in_dim(
        jnp.concatenate([values, values], axis=axis), start, values.shape[axis], axis=axis
    )


def after(values, *others):
    return lax.optimization_barrier((values,) + others)[0]


def local(sizes, *args):
    (
        nodes, edges, neighbours, resmask, node_gain_a, edge_gain_a, message_self, message_other, message_edge,
        message_out, node_gain_b, ffn_in, ffn_out, node_gain_c, edge_gain_b, update_self, update_other, update_edge,
        update_out, node_cot, edge_cot,
    ) = args
    cores, graph, mp = sizes
    near = graph <= 4
    at_graph = None if near else lax.axis_index("graph")
    _, rows, width = nodes.shape
    slots, side = edges.shape[2:]
    nbrs = neighbours.shape[2]
    total = resmask.shape[1]
    shard = message_self.shape[1]
    hidden = shard * mp
    ff = ffn_in.shape[1]
    vmem = 20 if total <= 1024 else 60
    run = functools.partial(call, vmem=vmem)

    def gather_rows(values):
        if near:
            return partners(values, "graph", graph)
        return [turn(lax.all_gather(values, "graph", axis=0, tiled=True), at_graph * rows, 0)]

    def return_rows(blocks):
        if near:
            return deal(blocks, "graph", graph)
        placed = turn(blocks[0], total - at_graph * rows, 0)
        return [lax.psum_scatter(placed, "graph", scatter_dimension=0, tiled=True)]

    blocks = [((rows, hidden), BF16)] * graph if near else [((total, hidden), BF16)]
    outs = len(blocks)
    node, cot_n = nodes[0], node_cot[0]

    nodes_all = gather_rows(node)
    et = jnp.transpose(edges[0], (1, 2, 0))
    cot = jnp.transpose(edge_cot[0], (1, 2, 0))
    edge_sh, hid_sh = (slots, side, rows), (hidden, slots * rows)

    mix, mask_row, gains_e, gains_n, a_own = run(
        "edge_prep", functools.partial(edge_prep, graph, near), 1,
        [
            far_in(v) for v in (
                et, jnp.transpose(neighbours, (2, 0, 1)), resmask, edge_gain_a[None, :], edge_gain_b[None, :],
                node_gain_a[None, :], node_gain_b[None, :], node_gain_c[None, :], node,
            )
        ],
        [((2 * side + total, slots * rows), BF16), ((1, total), jnp.int32), ((2, side, rows), F32), ((8, width), F32),
         ((rows, width), BF16)],
    )
    full, half, later, later_half = run(
        "pack_weights", pack_weights, 1,
        [far_in(w) for w in (
            message_self, message_other, message_edge, message_out, update_self, update_other, update_edge, update_out.T
        )],
        [((shard, 2 * width + 2 * 640), BF16), ((shard, width + 640), BF16), ((shard, 2 * width), BF16),
         ((shard, width), BF16)],
    )
    def across(values):
        pairs = [(c * mp + m, c * mp + (m ^ (1 + c))) for c in range(2) for m in range(mp)]
        return lax.ppermute(values, ("dp", "mp"), pairs)

    cross, diag = across(full), swap(half, "mp", 3, mp)
    cross_later, diag_later = across(later), swap(later_half, "mp", 3, mp)
    (a_all,) = run(
        "row_prep", functools.partial(row_prep, len(nodes_all)), 1,
        ([a_own] + nodes_all[1:] if near else nodes_all) + [gains_n], [((total, width), BF16)],
    )
    cross, diag = after(cross, a_all), after(diag, a_all)
    slope_m, pooled_part, fronts, backs = run(
        "message_forward", functools.partial(message_forward, 1.0 / nbrs, slots), 1,
        [mix, mask_row, a_all, full, cross, diag, swap(cross, "dp", 1, cores), swap(diag, "dp", 1, cores),],
        [(hid_sh, BF16), ((rows, hidden), BF16), ((hidden, width + 640), BF16), ((hidden, width + 640), BF16)],
        [pltpu.VMEM((hidden + 16, total + side), BF16), pltpu.VMEM((hidden + 16, slots * rows), F32),
         pltpu.VMEM((hidden, rows), F32), pltpu.VMEM((hidden, rows), F32)], heavy=True,
    )

    pooled, h1, b, y, slope_f, h2_part = run(
        "node_forward", node_forward, 1,
        partners(pooled_part, "mp", mp) + [node, backs, gains_n, ffn_in, ffn_out],
        [((rows, hidden), BF16), ((rows, width), F32), ((rows, width), BF16), ((rows, ff), BF16), ((rows, ff), BF16),
         ((rows, width), BF16)],
    )
    h2, c_own, nodes_out = run(
        "node_close", node_close, 1, [h1] + partners(h2_part, "mp", mp) + [gains_n, (cross_later, AFTER), (diag_later, AFTER)],
        [((rows, width), F32), ((rows, width), BF16), ((rows, width), BF16)],
    )
    c_all = gather_rows(c_own)

    w_act, dv, r_upd, laters, *s_upd = run(
        "update_nodes", functools.partial(update_nodes, slots, len(c_all), outs), 1,
        [mix, cot, fronts] + c_all
        + [later, cross_later, diag_later, swap(cross_later, "dp", 1, cores), swap(diag_later, "dp", 1, cores)],
        [(hid_sh, BF16), (hid_sh, BF16), ((rows, hidden), BF16), ((hidden, 2 * width), BF16)] + blocks,
        [pltpu.VMEM((hidden, total + side), BF16), pltpu.VMEM(hid_sh, F32), pltpu.VMEM(hid_sh, F32),
         pltpu.VMEM((hidden, rows), F32), pltpu.VMEM((hidden, rows), F32)], heavy=True,
    )
    s_upd_parts = return_rows(s_upd)
    eo, dq, *extra = run(
        "update_edges", update_edges, 1, [et, w_act, dv, mix, cot, r_upd, fronts],
        [(edge_sh, BF16), ((side, slots * rows), BF16)] + [((rows + 2 * side, shard), BF16)] * mp,
    )
    edges_out = jnp.transpose(eo, (2, 0, 1))[None]
    order = extra[0]
    extra = deal(extra, "mp", mp)

    terms = run(
        "update_terms", functools.partial(update_terms, outs), 1, [r_upd, laters] + s_upd_parts + [(order, AFTER)],
        [((rows, width + shard), BF16)] * mp,
    )
    dh2, dr, dp_ffn, gain_c, share, db_part = run(
        "node_backward", node_backward, 1, deal(terms, "mp", mp) + [h2, cot_n, gains_n, slope_f, ffn_in, ffn_out],
        [((rows, width), F32), ((rows, width), BF16), ((rows, ff), BF16), ((1, width), F32), ((rows, shard), BF16),
         ((rows, width), BF16)],
    )
    db_parts = partners(db_part, "mp", mp)

    size = (width + (width + side) // 4 + 63) // 64 * 64
    keep, send = run(
        "early_grads", early_grads, 1, [b, dp_ffn, y, dr, c_own, share] + extra + [(db_parts[3], AFTER)], [((size, ff), BF16)] * 2,
    )
    got = swap(send, "dp", 1, cores)
    halves, quarters = [((size // 2, ff), BF16)], [((size // 4, ff), BF16)]

    dh1, dt, gain_b, du, *shares = run(
        "message_backward", functools.partial(message_backward, 1.0 / nbrs, slots), 1,
        db_parts + [h1, dh2, gains_n, backs, slope_m, mix],
        [((rows, width), F32), ((rows, width), BF16), ((1, width), F32), (hid_sh, BF16)]
        + [((total + rows + side, shard), BF16)] * mp,
        [pltpu.VMEM((hidden, rows), F32), pltpu.VMEM((hidden, rows), F32)], heavy=True,
    )
    if near:
        stay, go = run("early_one", functools.partial(sum_split, 1), 1, [keep, got, (gain_b, AFTER)], halves * 2)
        go = swap(go, "graph", 1, graph)
    shares = deal(shares, "mp", mp)
    ge, gains_edge = run(
        "message_edges", message_edges, 1, [et, du, dq, cot, gains_e, fronts], [(edge_sh, F32), ((8, 256), F32)],
        [pltpu.VMEM((side, rows), F32), pltpu.VMEM((side, rows), F32)],
    )
    grad_edges = jnp.transpose(ge, (2, 0, 1))[None]

    share_r, grad_edge, *share_s = run(
        "message_shares", message_shares, 1, shares + [(gains_edge, AFTER)],
        [((rows, shard), BF16), ((side, shard), BF16)] + [(sh[:1] + (shard,), t) for sh, t in blocks],
    )
    if near:
        stay, go = run("early_two", functools.partial(sum_split, 2), 1, [stay, go, (gains_edge, AFTER)], quarters * 2)
        go = swap(go, "graph", 2, graph)
    half = (side + width) // 2
    keep_late, send_late = run(
        "late_grads", late_grads, 1,
        [grad_edge, (pooled, pl.BlockSpec((rows, shard), lambda i: (0, 0))), dt], [((half, shard), BF16)] * 2,
    )
    term, share, late = run(
        "message_terms", functools.partial(message_terms, outs), 1,
        [share_r, fronts, backs, node, gain_b, gain_c, gains_edge, keep_late, swap(send_late, "dp", 1, cores)]
        + return_rows(share_s),
        [((rows + 16, width), BF16), ((2 * rows, shard), BF16), ((half, shard), BF16)],
    )
    if near:
        (own,) = run("early_three", sum_two, 1, [stay, go, (term, AFTER)], quarters)
        early_sum = [own, swap(own, "graph", 1, graph), swap(own, "graph", 2, graph)]
        early_order = [(v, AFTER) for v in early_sum[1:]]
    else:
        early_order = []
    none = jnp.zeros((half, shard), BF16)
    grad_nodes, pack, long = run(
        "node_finish", node_finish, 1,
        partners(term, "mp", mp) + [node, dh1, gains_n, share, late, swap(late, "graph", 1, graph) if near else none] + early_order,
        [((rows, width), F32), ((2 * rows + width // 16, shard), BF16),
         ((2 * rows + width // 16 + half, shard), BF16)],
    )
    if near:
        early_sum.append(swap(after(early_sum[2], pack), "graph", 1, graph))
        long_two = swap(long, "graph", 2, graph)
        packs = [pack, swap(pack, "graph", 1, graph), long_two, swap(pack, "graph", 3, graph)]
        early_end = [(early_sum[3], AFTER)]
    else:
        early = lax.psum(keep.astype(F32) + got.astype(F32), "graph").astype(BF16)
        early_sum = [early]
        packs, long_two, early_end = [pack], jnp.zeros_like(long), []
    grad_in, grad_out, grad_us, grad_ue, grad_uo, grad_uout = run(
        "finish_early", functools.partial(finish_early, near), 1, early_sum + [swap(v, "dp", 1, cores) for v in early_sum],
        [((width, ff), F32), ((ff, width), F32), ((width, shard), F32), ((side, shard), F32), ((width, shard), F32),
         ((side, shard), F32)],
        [pltpu.VMEM((size, ff), BF16)] * 2,
    )
    parts = len(packs)
    (part,) = run(
        "message_grads", functools.partial(message_grads, parts), 1,
        [(a_all, pl.BlockSpec((parts * rows, width), lambda i: (0, 0)))] + packs + [long, long_two] + early_end,
        [((2 * width + half + width // 16, shard), BF16)],
    )
    if not near:
        part = lax.psum(part, "graph")
    grad_mo, grad_ms, grad_me, grad_mout, gain_a, gain_b, gain_c, gain_ea, gain_eb = run(
        "finish_late", finish_late, 1, [part, swap(part, "dp", 1, cores)],
        [((width, shard), F32), ((width, shard), F32), ((side, shard), F32), ((shard, width), F32), ((1, width), F32),
         ((1, width), F32), ((1, width), F32), ((1, side), F32), ((1, side), F32)],
    )
    return (
        nodes_out[None],
        edges_out,
        grad_nodes[None],
        grad_edges,
        gain_a[0],
        gain_ea[0],
        grad_ms,
        grad_mo,
        grad_me,
        grad_mout,
        gain_b[0],
        grad_in,
        grad_out,
        gain_c[0],
        gain_eb[0],
        grad_us,
        grad_uo,
        grad_ue,
        grad_uout.T,
    )


def solution(mesh):
    sizes = (mesh.shape["dp"], mesh.shape["graph"], mesh.shape["mp"])
    rows = P("dp", "graph", None)
    slots = P("dp", "graph", "mp", None)
    cols, tops = P(None, "mp"), P("mp", None)
    return jax.shard_map(
        functools.partial(local, sizes),
        mesh=mesh,
        in_specs=(
            rows, slots, rows, P("dp", None), P(), P(), cols, cols, cols, tops, P(), cols, tops, P(), P(), cols, cols,
            cols, tops, rows, slots,
        ),
        out_specs=(
            rows, slots, rows, slots, P(), P(), cols, cols, cols, tops, P(), cols, tops, P(), P(), cols, cols, cols,
            tops,
        ),
        check_vma=False,
    )
```
